32 devices in a mesh: dp: 8 (over z, y), fsdp: 4 (over x, core).
Axes of the slice: x: 2, y: 2, z: 4, core: 2. Of those that a mesh axis runs over, the one named last changes fastest.
Arguments:
- tokens: bfloat16 [8192, 768], P(('dp', 'fsdp')), may hold values from -6 to 6
- cotangent: bfloat16 [8192, 768], P(('dp', 'fsdp')), may hold values from -6 to 6
- counts: int32 [8, 4], replicated, may hold values from 128 to 256, as said below
- lengths: int32 [8, 8], replicated, may hold values from 1 to 1017, as said below
- weight_qkv: float32 [768, 2304], P(('dp', 'fsdp')), may hold values from -0.3125 to 0.3125
- weight_out: float32 [768, 768], P(('dp', 'fsdp')), may hold values from -0.21875 to 0.21875
- weight_in: float32 [768, 2304], P(('dp', 'fsdp')), may hold values from -0.21875 to 0.21875
- weight_down: float32 [768, 1152], P(('dp', 'fsdp')), may hold values from -0.1875 to 0.1875
- norm_gains: float32 [2, 768], P(None, ('dp', 'fsdp')), may hold values from 0.5 to 1.5
- first_qkv: float32 [768, 2304], P(('dp', 'fsdp')), may hold values from -448 to 448
- first_out: float32 [768, 768], P(('dp', 'fsdp')), may hold values from -320 to 320
- first_in: float32 [768, 2304], P(('dp', 'fsdp')), may hold values from -256 to 256
- first_down: float32 [768, 1152], P(('dp', 'fsdp')), may hold values from -256 to 256
- first_gains: float32 [2, 768], P(None, ('dp', 'fsdp')), may hold values from -768 to 768
- second_qkv: float32 [768, 2304], P(('dp', 'fsdp')), may hold values from 6144 to 24576
- second_out: float32 [768, 768], P(('dp', 'fsdp')), may hold values from 3072 to 12288
- second_in: float32 [768, 2304], P(('dp', 'fsdp')), may hold values from 2211 to 8847
- second_down: float32 [768, 1152], P(('dp', 'fsdp')), may hold values from 2211 to 8847
- second_gains: float32 [2, 768], P(None, ('dp', 'fsdp')), may hold values from 15728 to 62914
- average_qkv: float32 [768, 2304], P(('dp', 'fsdp')), may hold values from -0.3125 to 0.3125
- average_out: float32 [768, 768], P(('dp', 'fsdp')), may hold values from -0.21875 to 0.21875
- average_in: float32 [768, 2304], P(('dp', 'fsdp')), may hold values from -0.21875 to 0.21875
- average_down: float32 [768, 1152], P(('dp', 'fsdp')), may hold values from -0.1875 to 0.1875
- average_gains: float32 [2, 768], P(None, ('dp', 'fsdp')), may hold values from 0.5 to 1.5
Outputs:
- block_out: bfloat16 [8192, 768], P(('dp', 'fsdp'))
- grad_tokens: float32 [8192, 768], P(('dp', 'fsdp'))
- momentum_qkv: float32 [768, 2304], P(('dp', 'fsdp'))
- momentum_out: float32 [768, 768], P(('dp', 'fsdp'))
- momentum_in: float32 [768, 2304], P(('dp', 'fsdp'))
- momentum_down: float32 [768, 1152], P(('dp', 'fsdp'))
- momentum_gains: float32 [2, 768], P(None, ('dp', 'fsdp'))
- variance_qkv: float32 [768, 2304], P(('dp', 'fsdp'))
- variance_out: float32 [768, 768], P(('dp', 'fsdp'))
- variance_in: float32 [768, 2304], P(('dp', 'fsdp'))
- variance_down: float32 [768, 1152], P(('dp', 'fsdp'))
- variance_gains: float32 [2, 768], P(None, ('dp', 'fsdp'))
- master_qkv: float32 [768, 2304], P(('dp', 'fsdp'))
- master_out: float32 [768, 768], P(('dp', 'fsdp'))
- master_in: float32 [768, 2304], P(('dp', 'fsdp'))
- master_down: float32 [768, 1152], P(('dp', 'fsdp'))
- master_gains: float32 [2, 768], P(None, ('dp', 'fsdp'))
- smooth_qkv: float32 [768, 2304], P(('dp', 'fsdp'))
- smooth_out: float32 [768, 768], P(('dp', 'fsdp'))
- smooth_in: float32 [768, 2304], P(('dp', 'fsdp'))
- smooth_down: float32 [768, 1152], P(('dp', 'fsdp'))
- smooth_gains: float32 [2, 768], P(None, ('dp', 'fsdp'))
- halfcopy_qkv: bfloat16 [768, 2304], P(('dp', 'fsdp'))
- halfcopy_out: bfloat16 [768, 768], P(('dp', 'fsdp'))
- halfcopy_in: bfloat16 [768, 2304], P(('dp', 'fsdp'))
- halfcopy_down: bfloat16 [768, 1152], P(('dp', 'fsdp'))
- halfcopy_gains: bfloat16 [2, 768], P(None, ('dp', 'fsdp'))
The draws below stay inside these ranges and needn't reach their ends.
Inputs may be any that keep to these rules, and one draw needn't show every extreme that they name: counts[g, f] live tokens fill the first rows of device f of pack g; in every pack some device holds exactly 256, and in one pack, drawn from the seed, every device does. lengths[g] are the lengths of the documents laid in order over the live tokens of pack g and add up to the sum of counts[g]; one of them, at an index drawn from the seed, begins on the pack's first device and ends on its last; the others are at most 16 tokens, and in the pack whose devices are all full they are 1.
All inputs are finite; a program needn't handle non-finite values.
Results may differ from the reference program's by a relative error of at most 0.017.
The reference program's roundings to bfloat16 on the way count: a program that leaves them out, or rounds other values in their place, can miss the bound.
Values may be sent and summed in bfloat16 or wider, within the bound.
No kernel may reach another device: no remote copies, remote signals or barrier semaphores. Data moves between devices by JAX's collectives and lax.ppermute only.
A program may use at most 128 MiB of HBM per device.

```python
import math
import jax
import jax.numpy as jnp
from jax import lax

D = 768
HEADS = 12
HD = 64
FF = 1152
CAP = 256
NDOC = 8
STEP = 6
TOKENS = 8192
LIVE = 6144
N_DP = 8
N_FSDP = 4


def pack_layout(key):
    key_counts = jax.random.fold_in(key, 11)
    key_full = jax.random.fold_in(key, 12)
    key_short = jax.random.fold_in(key, 13)
    key_long = jax.random.fold_in(key, 14)
    key_pack = jax.random.fold_in(key, 15)
    drawn_counts = jax.random.randint(key_counts, (N_DP, N_FSDP), CAP // 2, CAP + 1, dtype=jnp.int32)
    full_place = jax.random.randint(key_full, (N_DP, 1), 0, N_FSDP, dtype=jnp.int32)
    device_place = jnp.arange(N_FSDP, dtype=jnp.int32)[None, :]
    full_pack = jax.random.randint(key_pack, (1, 1), 0, N_DP, dtype=jnp.int32)
    is_full_pack = jnp.arange(N_DP, dtype=jnp.int32)[:, None] == full_pack
    counts_out = jnp.where(device_place == full_place, CAP, drawn_counts).astype(jnp.int32)
    counts_out = jnp.where(is_full_pack, CAP, counts_out).astype(jnp.int32)
    short_most = max(1, CAP // 16)
    short_docs = jax.random.randint(key_short, (N_DP, NDOC), 1, short_most + 1, dtype=jnp.int32)
    short_docs = jnp.where(is_full_pack, 1, short_docs).astype(jnp.int32)
    long_place = jax.random.randint(key_long, (N_DP, 1), 0, NDOC, dtype=jnp.int32)
    doc_place = jnp.arange(NDOC, dtype=jnp.int32)[None, :]
    is_long = doc_place == long_place
    short_total = jnp.sum(jnp.where(is_long, 0, short_docs), axis=1, keepdims=True).astype(jnp.int32)
    group_total = jnp.sum(counts_out, axis=1, keepdims=True).astype(jnp.int32)
    lengths_out = jnp.where(is_long, group_total - short_total, short_docs).astype(jnp.int32)
    return (counts_out, lengths_out)


def draw_counts(key, part):
    counts_out, lengths_out = pack_layout(key)
    return counts_out


def draw_lengths(key, part):
    counts_out, lengths_out = pack_layout(key)
    return lengths_out


def block_scale(own_key, extent, cuts, least, high):
    level, own = 1.0, jax.random.fold_in(own_key, 6)
    for axis_at, blocks in cuts:
        draws = jnp.exp(jax.random.uniform(jax.random.fold_in(own, axis_at), (blocks,), jnp.float32, least / len(cuts), high / len(cuts)))
        level = level * jnp.repeat(draws, extent[axis_at] // blocks).reshape([-1 if axis == axis_at else 1 for axis in range(len(extent))])
    return level


def gaussian(stream_key, extent, scale, most, split=(), held_as=jnp.bfloat16):
    loudness = block_scale(stream_key, extent, split, -0.22, 0.18) if split else 1.0
    drawn = jax.random.normal(stream_key, extent, jnp.float32) * scale * loudness
    return jnp.minimum(jnp.maximum(drawn, -most), most).astype(held_as)


def setup_inputs(seed: int = 0) -> dict:
    keys = jax.random.split(jax.random.key(seed), 25)
    tokens = gaussian(keys[0], (TOKENS, D), 1.0, 6.0, ((0, 32),))
    cotangent = gaussian(keys[1], (TOKENS, D), 1.0, 6.0, ((0, 32),))
    counts = draw_counts(jax.random.fold_in(keys[24], 71), 0)
    lengths = draw_lengths(jax.random.fold_in(keys[24], 71), 0)
    weight_qkv = gaussian(keys[4], (D, 3 * D), (D * 2 // 5) ** -0.5, 0.3125, ((0, 32),), jnp.float32)
    weight_out = gaussian(keys[5], (D, D), D ** -0.5, 0.21875, ((0, 32),), jnp.float32)
    weight_in = gaussian(keys[6], (D, 2 * FF), D ** -0.5, 0.21875, ((0, 32),), jnp.float32)
    weight_down = gaussian(keys[7], (D, FF), FF ** -0.5, 0.1875, ((0, 32),), jnp.float32)
    norm_gains = jnp.clip(1.0 + 0.1 * jax.random.normal(keys[8], (2, D), jnp.float32), 0.5, 1.5)
    first_qkv = gaussian(keys[9], (D, 3 * D), (LIVE ** 0.5), 448.0, ((0, 32),), jnp.float32)
    first_out = gaussian(keys[10], (D, D), (0.7 * LIVE ** 0.5), 320.0, ((0, 32),), jnp.float32)
    first_in = gaussian(keys[11], (D, 2 * FF), (0.6 * LIVE ** 0.5), 256.0, ((0, 32),), jnp.float32)
    first_down = gaussian(keys[12], (D, FF), (0.6 * LIVE ** 0.5), 256.0, ((0, 32),), jnp.float32)
    first_gains = gaussian(keys[13], (2, D), (1.6 * LIVE ** 0.5), 768.0, ((1, 32),), jnp.float32)
    second_qkv = jnp.clip(jnp.exp(math.log(24576.0) - 1.3862944 * jax.random.uniform(keys[14], (D, 3 * D), jnp.float32) ** block_scale(keys[14], (D, 3 * D), ((0, 32),), -0.2, 0.2)), 6144.0, 24576.0)
    second_out = jnp.clip(jnp.exp(math.log(12288.0) - 1.3862944 * jax.random.uniform(keys[15], (D, D), jnp.float32) ** block_scale(keys[15], (D, D), ((0, 32),), -0.2, 0.2)), 3072.0, 12288.0)
    second_in = jnp.clip(jnp.exp(math.log(8847.0) - 1.3866335 * jax.random.uniform(keys[16], (D, 2 * FF), jnp.float32) ** block_scale(keys[16], (D, 2 * FF), ((0, 32),), -0.2, 0.2)), 2211.0, 8847.0)
    second_down = jnp.clip(jnp.exp(math.log(8847.0) - 1.3866335 * jax.random.uniform(keys[17], (D, FF), jnp.float32) ** block_scale(keys[17], (D, FF), ((0, 32),), -0.2, 0.2)), 2211.0, 8847.0)
    second_gains = jnp.clip(jnp.exp(math.log(62914.0) - 1.3863262 * jax.random.uniform(keys[18], (2, D), jnp.float32) ** block_scale(keys[18], (2, D), ((1, 32),), -0.2, 0.2)), 15728.0, 62914.0)
    average_qkv = gaussian(keys[19], (D, 3 * D), (D * 2 // 5) ** -0.5, 0.3125, ((0, 32),), jnp.float32)
    average_out = gaussian(keys[20], (D, D), D ** -0.5, 0.21875, ((0, 32),), jnp.float32)
    average_in = gaussian(keys[21], (D, 2 * FF), D ** -0.5, 0.21875, ((0, 32),), jnp.float32)
    average_down = gaussian(keys[22], (D, FF), FF ** -0.5, 0.1875, ((0, 32),), jnp.float32)
    average_gains = jnp.clip(1.0 + 0.1 * jax.random.normal(keys[23], (2, D), jnp.float32), 0.5, 1.5)
    return {"tokens": tokens, "cotangent": cotangent, "counts": counts, "lengths": lengths, "weight_qkv": weight_qkv, "weight_out": weight_out, "weight_in": weight_in, "weight_down": weight_down, "norm_gains": norm_gains, "first_qkv": first_qkv, "first_out": first_out, "first_in": first_in, "first_down": first_down, "first_gains": first_gains, "second_qkv": second_qkv, "second_out": second_out, "second_in": second_in, "second_down": second_down, "second_gains": second_gains, "average_qkv": average_qkv, "average_out": average_out, "average_in": average_in, "average_down": average_down, "average_gains": average_gains}


NORM_EPS = 1e-05
ROTARY_BASE = 160000.0
BETA_FIRST = 0.5
BETA_SECOND = 0.5
ADAM_EPS = 1e-08
WEIGHT_DECAY = 0.01
MATRIX_RATE = 0.04
GAIN_RATE = 0.5
AVERAGE_KEEP = 0.6
MASKED = -1e+30
HIGHEST = lax.Precision.HIGHEST

@jax.custom_vjp
def low(v):
    return lax.optimization_barrier(v.astype(jnp.bfloat16)).astype(jnp.float32)

@jax.custom_vjp
def low_back(v):
    return v

def low_keep(v):
    return (low(v), None)

def low_pass(kept, grad):
    return (grad,)

def back_keep(v):
    return (v, None)

def back_low(kept, grad):
    return (low(grad),)
low.defvjp(low_keep, low_pass)
low_back.defvjp(back_keep, back_low)

def group_layout(count_row, length_row, slots):
    devices_here = count_row.shape[0]
    places = jnp.arange(devices_here * slots, dtype=jnp.int32)
    holder = places // slots
    within = places - holder * slots
    before = (jnp.cumsum(count_row) - count_row).astype(jnp.int32)
    choose = (holder[:, None] == jnp.arange(devices_here, dtype=jnp.int32)[None, :]).astype(jnp.int32)
    offset = (lax.optimization_barrier(jnp.sum(choose * before[None, :], axis=1)) + within).astype(jnp.int32)
    limits = lax.optimization_barrier(jnp.sum(choose * count_row[None, :], axis=1)).astype(jnp.int32)
    living = within < limits
    doc_ends = jnp.cumsum(length_row).astype(jnp.int32)
    passed = offset[:, None] >= doc_ends[None, :]
    document = lax.optimization_barrier(jnp.sum(passed.astype(jnp.int32), axis=1)).astype(jnp.int32)
    begins = lax.optimization_barrier(jnp.max(jnp.where(passed, doc_ends[None, :], 0), axis=1)).astype(jnp.int32)
    number_docs = length_row.shape[0]
    document = jnp.where(living, document, number_docs).astype(jnp.int32)
    position = jnp.where(living, offset - begins, 0).astype(jnp.int32)
    return (document, position, living)

def rotary_tables(position, head_size):
    half_size = head_size // 2
    speeds = ROTARY_BASE ** (-(jnp.arange(half_size, dtype=jnp.float32) * (2.0 / head_size)))
    angles = position.astype(jnp.float32)[:, None] * speeds[None, :]
    return (jnp.cos(angles), jnp.sin(angles))

def rotate(heads_in, cosine_table, sine_table):
    half_size = heads_in.shape[-1] // 2
    leading = heads_in[..., :half_size]
    latter = heads_in[..., half_size:]
    cos_wide = cosine_table[:, None, :]
    sin_wide = sine_table[:, None, :]
    return jnp.concatenate([leading * cos_wide - latter * sin_wide, latter * cos_wide + leading * sin_wide], axis=-1)

def layer_norm(values_in, gain_row):
    center = values_in - lax.optimization_barrier(jnp.mean(values_in, axis=-1, keepdims=True))
    spread = lax.optimization_barrier(jnp.mean(center * center, axis=-1, keepdims=True))
    return center * lax.rsqrt(spread + NORM_EPS) * gain_row

def attend_group(queries, key_rows, value_rows, documents, score_scale):
    total_rows = queries.shape[0]
    block_rows = 512 if total_rows % 512 == 0 else total_rows
    count_blocks = total_rows // block_rows

    def one_block(pieces):
        query_block, doc_block = pieces
        scores = jnp.einsum('qhd,khd->hqk', query_block, key_rows, precision=HIGHEST) * score_scale
        scores = low_back(scores)
        scores = jnp.where(doc_block[None, :, None] == documents[None, None, :], scores, MASKED)
        total_log = jax.nn.logsumexp(scores, axis=-1, keepdims=True)
        weights = low(jnp.exp(scores - total_log))
        return jnp.einsum('hqk,khd->qhd', weights, value_rows, precision=HIGHEST)
    shaped = (queries.reshape(count_blocks, block_rows, queries.shape[1], queries.shape[2]), documents.reshape(count_blocks, block_rows))
    return lax.map(jax.checkpoint(one_block), shaped).reshape(queries.shape)

def forward(tokens_f, weight_qkv, weight_out, weight_in, weight_down, norm_gains, documents, cosine_table, sine_table, living):
    model_width = tokens_f.shape[1]
    rows_all = tokens_f.shape[0]
    gains_low = low(norm_gains)
    normed_one = low(layer_norm(tokens_f, gains_low[0]))
    mixed_qkv = low_back(jnp.dot(normed_one, low(weight_qkv), precision=HIGHEST))
    heads_shape = (rows_all, HEADS, HD)
    queries = low(rotate(mixed_qkv[:, :model_width].reshape(heads_shape), cosine_table, sine_table))
    key_rows = low(rotate(mixed_qkv[:, model_width:2 * model_width].reshape(heads_shape), cosine_table, sine_table))
    value_rows = low(mixed_qkv[:, 2 * model_width:].reshape(heads_shape))
    group_shape = (N_DP, rows_all // N_DP, HEADS, HD)
    score_scale = 1.0 / HD ** 0.5
    attended = lax.map(lambda pieces: attend_group(pieces[0], pieces[1], pieces[2], pieces[3], score_scale), (queries.reshape(group_shape), key_rows.reshape(group_shape), value_rows.reshape(group_shape), documents))
    attended = low(low_back(attended.reshape(rows_all, model_width)))
    branch_one = low_back(jnp.dot(attended, low(weight_out), precision=HIGHEST))
    middle = tokens_f + branch_one
    normed_two = low(layer_norm(middle, gains_low[1]))
    gate_up = low_back(jnp.dot(normed_two, low(weight_in), precision=HIGHEST))
    hidden_units = weight_down.shape[1]
    activated = low(jax.nn.gelu(gate_up[:, :hidden_units], approximate=False) * gate_up[:, hidden_units:])
    branch_two = low_back(jnp.dot(activated, low(weight_down).T, precision=HIGHEST))
    return jnp.where(living[:, None], middle + branch_two, 0.0)

def adam_update(master, first_old, second_old, average_old, gradient, step_rate):
    first_new = BETA_FIRST * first_old + (1.0 - BETA_FIRST) * gradient
    second_new = BETA_SECOND * second_old + (1.0 - BETA_SECOND) * gradient * gradient
    first_fix = first_new / (1.0 - BETA_FIRST ** STEP)
    second_fix = second_new / (1.0 - BETA_SECOND ** STEP)
    master_new = master - step_rate * (first_fix / (jnp.sqrt(second_fix) + ADAM_EPS) + WEIGHT_DECAY * master)
    average_new = AVERAGE_KEEP * average_old + (1.0 - AVERAGE_KEEP) * master_new
    return (first_new, second_new, master_new, average_new, master_new.astype(jnp.bfloat16))

def reference(tokens, cotangent, counts, lengths, weight_qkv, weight_out, weight_in, weight_down, norm_gains, first_qkv, first_out, first_in, first_down, first_gains, second_qkv, second_out, second_in, second_down, second_gains, average_qkv, average_out, average_in, average_down, average_gains):
    documents, positions, living = jax.vmap(lambda count_row, length_row: group_layout(count_row, length_row, CAP))(counts, lengths)
    cosine_table, sine_table = rotary_tables(positions.reshape(-1), HD)
    living_flat = living.reshape(-1)
    tokens_f = tokens.astype(jnp.float32)

    def wrapped(tokens_in, qkv_in, out_in, in_in, down_in, gains_in):
        return forward(tokens_in, qkv_in, out_in, in_in, down_in, gains_in, documents, cosine_table, sine_table, living_flat)
    result, pullback = jax.vjp(wrapped, tokens_f, weight_qkv, weight_out, weight_in, weight_down, norm_gains)
    gradients = pullback(cotangent.astype(jnp.float32))
    masters = (weight_qkv, weight_out, weight_in, weight_down, norm_gains)
    firsts = (first_qkv, first_out, first_in, first_down, first_gains)
    seconds = (second_qkv, second_out, second_in, second_down, second_gains)
    averages = (average_qkv, average_out, average_in, average_down, average_gains)
    rates = (MATRIX_RATE, MATRIX_RATE, MATRIX_RATE, MATRIX_RATE, GAIN_RATE)
    updated = [adam_update(masters[which], firsts[which], seconds[which], averages[which], gradients[which + 1], rates[which]) for which in range(5)]
    return (result.astype(jnp.bfloat16), gradients[0], updated[0][0], updated[1][0], updated[2][0], updated[3][0], updated[4][0], updated[0][1], updated[1][1], updated[2][1], updated[3][1], updated[4][1], updated[0][2], updated[1][2], updated[2][2], updated[3][2], updated[4][2], updated[0][3], updated[1][3], updated[2][3], updated[3][3], updated[4][3], updated[0][4], updated[1][4], updated[2][4], updated[3][4], updated[4][4])
```

```python
import jax
import jax.numpy as jnp
from jax import lax
from jax.experimental import pallas as pl
from jax.experimental.pallas import tpu as pltpu
from jax.sharding import PartitionSpec as P

HEADS = 12
HD = 64
STEP = 6


NORM_EPS = 1e-05
ROTARY_BASE = 160000.0
BETA_FIRST = 0.5
BETA_SECOND = 0.5
ADAM_EPS = 1e-08
WEIGHT_DECAY = 0.01
MATRIX_RATE = 0.04
GAIN_RATE = 0.5
AVERAGE_KEEP = 0.6
MASKED = -1e30


def group_layout(count_row, length_row, slots):
    devices_here = count_row.shape[0]
    places = jnp.arange(devices_here * slots, dtype=jnp.int32)
    holder = places // slots
    within = places - holder * slots
    before = jnp.cumsum(count_row) - count_row
    choose = (holder[:, None] == jnp.arange(devices_here, dtype=jnp.int32)[None, :]).astype(
        jnp.int32
    )
    offset = jnp.sum(choose * before[None, :], axis=1) + within
    limits = jnp.sum(choose * count_row[None, :], axis=1)
    living = within < limits
    doc_ends = jnp.cumsum(length_row)
    passed = offset[:, None] >= doc_ends[None, :]
    document = jnp.sum(passed.astype(jnp.int32), axis=1)
    begins = jnp.max(jnp.where(passed, doc_ends[None, :], 0), axis=1)
    number_docs = length_row.shape[0]
    document = jnp.where(living, document, number_docs)
    position = jnp.where(living, offset - begins, 0)
    return (document, position, living)


def rotary_tables(position, head_size):
    half_size = head_size // 2
    speeds = ROTARY_BASE ** (-(jnp.arange(half_size, dtype=jnp.float32) * (2.0 / head_size)))
    angles = position.astype(jnp.float32)[:, None] * speeds[None, :]
    return (jnp.cos(angles), jnp.sin(angles))


def rotate(heads_in, cosine_table, sine_table):
    half_size = heads_in.shape[-1] // 2
    leading = heads_in[..., :half_size]
    latter = heads_in[..., half_size:]
    cos_wide = cosine_table[:, None, :]
    sin_wide = sine_table[:, None, :]
    return jnp.concatenate(
        [leading * cos_wide - latter * sin_wide, latter * cos_wide + leading * sin_wide], axis=-1
    )


def rotate_back(grads_in, cosine_table, sine_table):
    half_size = grads_in.shape[-1] // 2
    leading = grads_in[..., :half_size]
    latter = grads_in[..., half_size:]
    cos_wide = cosine_table[:, None, :]
    sin_wide = sine_table[:, None, :]
    return jnp.concatenate(
        [leading * cos_wide + latter * sin_wide, latter * cos_wide - leading * sin_wide], axis=-1
    )


def norm_parts(values_in):
    center = values_in - jnp.mean(values_in, axis=-1, keepdims=True)
    inverse = lax.rsqrt(jnp.mean(center * center, axis=-1, keepdims=True) + NORM_EPS)
    return (center * inverse, inverse)


def norm_back(upstream, normed, inverse):
    return inverse * (
        upstream
        - jnp.mean(upstream, axis=-1, keepdims=True)
        - normed * jnp.mean(upstream * normed, axis=-1, keepdims=True)
    )


def block_scores(queries, key_block, doc_query, doc_key, score_scale):
    scores = (
        jnp.einsum("qhd,khd->hqk", queries, key_block, preferred_element_type=jnp.float32)
        * score_scale
    )
    return jnp.where(doc_query[None, :, None] == doc_key[None, None, :], scores, MASKED)


def contract_rows(left_side, right_side):
    return lax.dot_general(
        left_side, right_side, (((0,), (0,)), ((), ())), preferred_element_type=jnp.float32
    )


def contract_cols(left_side, right_side):
    return lax.dot_general(
        left_side, right_side, (((1,), (1,)), ((), ())), preferred_element_type=jnp.float32
    )


def adam_update(master, first_old, second_old, average_old, gradient, step_rate):
    first_new = BETA_FIRST * first_old + (1.0 - BETA_FIRST) * gradient
    second_new = BETA_SECOND * second_old + (1.0 - BETA_SECOND) * gradient * gradient
    first_fix = first_new / (1.0 - BETA_FIRST**STEP)
    second_fix = second_new / (1.0 - BETA_SECOND**STEP)
    master_new = master - step_rate * (
        first_fix / (jnp.sqrt(second_fix) + ADAM_EPS) + WEIGHT_DECAY * master
    )
    average_new = AVERAGE_KEEP * average_old + (1.0 - AVERAGE_KEEP) * master_new
    return (first_new, second_new, master_new, average_new, master_new.astype(jnp.bfloat16))


def general_body(
    tokens,
    cotangent,
    counts,
    lengths,
    weight_qkv,
    weight_out,
    weight_in,
    weight_down,
    norm_gains,
    first_qkv,
    first_out,
    first_in,
    first_down,
    first_gains,
    second_qkv,
    second_out,
    second_in,
    second_down,
    second_gains,
    average_qkv,
    average_out,
    average_in,
    average_down,
    average_gains,
):
    slots = tokens.shape[0]
    model_width = tokens.shape[1]
    hidden_units = weight_down.shape[1]
    head_count = HEADS
    head_size = HD
    score_scale = 1.0 / head_size**0.5
    heads_shape = (slots, head_count, head_size)
    group_row = lax.axis_index("dp")
    own_place = lax.axis_index("fsdp")
    count_row = lax.dynamic_index_in_dim(counts, group_row, 0, keepdims=False)
    length_row = lax.dynamic_index_in_dim(lengths, group_row, 0, keepdims=False)
    doc_all, position_all, living_all = group_layout(count_row, length_row, slots)
    doc_mine = lax.dynamic_slice_in_dim(doc_all, own_place * slots, slots)
    position_mine = lax.dynamic_slice_in_dim(position_all, own_place * slots, slots)
    living_mine = lax.dynamic_slice_in_dim(living_all, own_place * slots, slots)
    cosine_table, sine_table = rotary_tables(position_mine, head_size)
    living_col = living_mine[:, None]
    copies = (
        weight_qkv.astype(jnp.bfloat16),
        weight_out.astype(jnp.bfloat16),
        weight_in.astype(jnp.bfloat16),
        weight_down.astype(jnp.bfloat16),
        norm_gains.astype(jnp.bfloat16),
    )
    qkv_full, out_full, in_full, down_full, gain_full = (
        lax.all_gather(copies[0], ("dp", "fsdp"), axis=0, tiled=True),
        lax.all_gather(copies[1], ("dp", "fsdp"), axis=0, tiled=True),
        lax.all_gather(copies[2], ("dp", "fsdp"), axis=0, tiled=True),
        lax.all_gather(copies[3], ("dp", "fsdp"), axis=0, tiled=True),
        lax.all_gather(copies[4], ("dp", "fsdp"), axis=1, tiled=True),
    )
    tokens_f = tokens.astype(jnp.float32)
    normed_one, inverse_one = norm_parts(tokens_f)
    gain_one = gain_full[0].astype(jnp.float32)
    gain_two = gain_full[1].astype(jnp.float32)
    normed1_low = (normed_one * gain_one).astype(jnp.bfloat16)
    mixed_qkv = jnp.dot(normed1_low, qkv_full, preferred_element_type=jnp.float32)
    queries16 = rotate(
        mixed_qkv[:, :model_width].reshape(heads_shape), cosine_table, sine_table
    ).astype(jnp.bfloat16)
    keys16 = rotate(
        mixed_qkv[:, model_width : 2 * model_width].reshape(heads_shape), cosine_table, sine_table
    ).astype(jnp.bfloat16)
    key_flat = keys16.reshape(slots, model_width)
    value_flat = mixed_qkv[:, 2 * model_width :].astype(jnp.bfloat16)
    key_rows, value_rows = (
        lax.all_gather(key_flat, "fsdp", axis=0, tiled=True),
        lax.all_gather(value_flat, "fsdp", axis=0, tiled=True),
    )
    group_rows = key_rows.shape[0]
    block_rows = 512
    count_blocks = group_rows // block_rows
    blocks_shape = (count_blocks, block_rows, head_count, head_size)
    doc_blocks = doc_all.reshape(count_blocks, block_rows)
    key_blocks = key_rows.reshape(blocks_shape)
    value_blocks = value_rows.reshape(blocks_shape)

    def max_sum(state_now, pieces):
        run_peak, run_total = state_now
        scores = block_scores(queries16, pieces[0], doc_mine, pieces[1], score_scale)
        new_peak = jnp.maximum(run_peak, jnp.max(scores, axis=-1))
        run_total = run_total * jnp.exp(run_peak - new_peak) + jnp.sum(
            jnp.exp(scores - new_peak[:, :, None]), axis=-1
        )
        return ((new_peak, run_total), None)

    start_state = (
        jnp.full((head_count, slots), MASKED, jnp.float32),
        jnp.zeros((head_count, slots), jnp.float32),
    )
    (run_peak, run_total), unused_max = lax.scan(max_sum, start_state, (key_blocks, doc_blocks))
    log_total = run_peak + jnp.log(run_total)

    def weigh_values(accum, pieces):
        scores = block_scores(queries16, pieces[0], doc_mine, pieces[2], score_scale)
        probs16 = jnp.exp(scores - log_total[:, :, None]).astype(jnp.bfloat16)
        return (
            accum
            + jnp.einsum("hqk,khd->qhd", probs16, pieces[1], preferred_element_type=jnp.float32),
            None,
        )

    attended, unused_out = lax.scan(
        weigh_values, jnp.zeros(heads_shape, jnp.float32), (key_blocks, value_blocks, doc_blocks)
    )
    attended16 = attended.reshape(slots, model_width).astype(jnp.bfloat16)
    middle = tokens_f + jnp.dot(attended16, out_full, preferred_element_type=jnp.float32)
    normed_two, inverse_two = norm_parts(middle)
    normed2_low = (normed_two * gain_two).astype(jnp.bfloat16)
    gate_up = jnp.dot(normed2_low, in_full, preferred_element_type=jnp.float32)
    act_half = gate_up[:, :hidden_units]
    gate_half = gate_up[:, hidden_units:]
    activated16 = (jax.nn.gelu(act_half, approximate=False) * gate_half).astype(jnp.bfloat16)
    branch_two = contract_cols(activated16, down_full)
    block_out = jnp.where(living_col, middle + branch_two, 0.0).astype(jnp.bfloat16)
    qkv_back, out_back, in_back, down_back, gain_back = (
        lax.all_gather(copies[0], ("dp", "fsdp"), axis=0, tiled=True),
        lax.all_gather(copies[1], ("dp", "fsdp"), axis=0, tiled=True),
        lax.all_gather(copies[2], ("dp", "fsdp"), axis=0, tiled=True),
        lax.all_gather(copies[3], ("dp", "fsdp"), axis=0, tiled=True),
        lax.all_gather(copies[4], ("dp", "fsdp"), axis=1, tiled=True),
    )
    key_again, value_again = (
        lax.all_gather(key_flat, "fsdp", axis=0, tiled=True),
        lax.all_gather(value_flat, "fsdp", axis=0, tiled=True),
    )
    gain_one_back = gain_back[0].astype(jnp.float32)
    gain_two_back = gain_back[1].astype(jnp.float32)
    dout = jnp.where(living_col, cotangent.astype(jnp.float32), 0.0)
    dym16 = dout.astype(jnp.bfloat16)
    grad_down = contract_rows(dym16, activated16)
    dact = jnp.dot(dym16, down_back, preferred_element_type=jnp.float32)
    unused_gate, gate_pull = jax.vjp(
        lambda front_part, rear_part: jax.nn.gelu(front_part, approximate=False) * rear_part,
        act_half,
        gate_half,
    )
    dfront, drear = gate_pull(dact)
    dgate16 = jnp.concatenate([dfront, drear], axis=1).astype(jnp.bfloat16)
    grad_in = contract_rows(normed2_low, dgate16)
    dnormed_two = contract_cols(dgate16, in_back)
    grad_gain_two = jnp.sum(dnormed_two * normed_two, axis=0)
    dmiddle = dout + norm_back(dnormed_two * gain_two_back, normed_two, inverse_two)
    dbranch16 = dmiddle.astype(jnp.bfloat16)
    grad_out = contract_rows(attended16, dbranch16)
    dattn16 = contract_cols(dbranch16, out_back).astype(jnp.bfloat16).reshape(heads_shape)
    row_delta = jnp.sum(dattn16.astype(jnp.float32) * attended, axis=-1).T
    back_keys = key_again.reshape(blocks_shape)
    back_values = value_again.reshape(blocks_shape)

    def back_block(dquery_sum, pieces):
        key_block, value_block, doc_block = pieces
        scores = block_scores(queries16, key_block, doc_mine, doc_block, score_scale)
        probs = jnp.exp(scores - log_total[:, :, None])
        probs16 = probs.astype(jnp.bfloat16)
        dvalue_block = jnp.einsum(
            "hqk,qhd->khd", probs16, dattn16, preferred_element_type=jnp.float32
        )
        dprobs = jnp.einsum(
            "qhd,khd->hqk", dattn16, value_block, preferred_element_type=jnp.float32
        )
        dscores16 = (probs * (dprobs - row_delta[:, :, None])).astype(jnp.bfloat16)
        dquery_sum = dquery_sum + jnp.einsum(
            "hqk,khd->qhd", dscores16, key_block, preferred_element_type=jnp.float32
        )
        dkey_block = jnp.einsum(
            "hqk,qhd->khd", dscores16, queries16, preferred_element_type=jnp.float32
        )
        return (dquery_sum, (dkey_block, dvalue_block))

    dquery_sum, (dkey_blocks, dvalue_blocks) = lax.scan(
        back_block, jnp.zeros(heads_shape, jnp.float32), (back_keys, back_values, doc_blocks)
    )
    dkey_mine, dvalue_mine = (
        lax.psum_scatter(
            (dkey_blocks.reshape(group_rows, model_width) * score_scale).astype(jnp.bfloat16),
            "fsdp",
            scatter_dimension=0,
            tiled=True,
        ).astype(jnp.float32),
        lax.psum_scatter(
            dvalue_blocks.reshape(group_rows, model_width).astype(jnp.bfloat16),
            "fsdp",
            scatter_dimension=0,
            tiled=True,
        ).astype(jnp.float32),
    )
    dquery_pre = rotate_back(dquery_sum * score_scale, cosine_table, sine_table).reshape(
        slots, model_width
    )
    dkey_pre = rotate_back(dkey_mine.reshape(heads_shape), cosine_table, sine_table).reshape(
        slots, model_width
    )
    dmixed16 = jnp.concatenate([dquery_pre, dkey_pre, dvalue_mine], axis=1).astype(jnp.bfloat16)
    grad_qkv = contract_rows(normed1_low, dmixed16)
    dnormed_one = contract_cols(dmixed16, qkv_back)
    grad_gain_one = jnp.sum(dnormed_one * normed_one, axis=0)
    grad_tokens = dmiddle + norm_back(dnormed_one * gain_one_back, normed_one, inverse_one)
    grad_gains = jnp.stack([grad_gain_one, grad_gain_two], axis=0)
    reduced = (
        lax.psum_scatter(grad_qkv, ("dp", "fsdp"), scatter_dimension=0, tiled=True),
        lax.psum_scatter(grad_out, ("dp", "fsdp"), scatter_dimension=0, tiled=True),
        lax.psum_scatter(grad_in, ("dp", "fsdp"), scatter_dimension=0, tiled=True),
        lax.psum_scatter(grad_down, ("dp", "fsdp"), scatter_dimension=0, tiled=True),
        lax.psum_scatter(grad_gains, ("dp", "fsdp"), scatter_dimension=1, tiled=True),
    )
    masters = (weight_qkv, weight_out, weight_in, weight_down, norm_gains)
    firsts = (first_qkv, first_out, first_in, first_down, first_gains)
    seconds = (second_qkv, second_out, second_in, second_down, second_gains)
    averages = (average_qkv, average_out, average_in, average_down, average_gains)
    rates = (MATRIX_RATE, MATRIX_RATE, MATRIX_RATE, MATRIX_RATE, GAIN_RATE)
    updated = [
        adam_update(
            masters[which],
            firsts[which],
            seconds[which],
            averages[which],
            reduced[which],
            rates[which],
        )
        for which in range(5)
    ]
    return (
        block_out,
        grad_tokens,
        updated[0][0],
        updated[1][0],
        updated[2][0],
        updated[3][0],
        updated[4][0],
        updated[0][1],
        updated[1][1],
        updated[2][1],
        updated[3][1],
        updated[4][1],
        updated[0][2],
        updated[1][2],
        updated[2][2],
        updated[3][2],
        updated[4][2],
        updated[0][3],
        updated[1][3],
        updated[2][3],
        updated[3][3],
        updated[4][3],
        updated[0][4],
        updated[1][4],
        updated[2][4],
        updated[3][4],
        updated[4][4],
    )


BF = jnp.bfloat16
F32 = jnp.float32
AXES = ("dp", "fsdp")
VMEM_LIMIT = 50 * 1024 * 1024


def xperm(value, mask):
    count = lax.axis_size("dp") * lax.axis_size("fsdp")
    return lax.ppermute(value, AXES, [(i, i ^ mask) for i in range(count)])


def dot_nn(a, b):
    return jnp.dot(a, b, preferred_element_type=F32)


def dot_nt(a, b):
    return lax.dot_general(a, b, (((1,), (1,)), ((), ())), preferred_element_type=F32)


def dot_tn(a, b):
    return lax.dot_general(a, b, (((0,), (0,)), ((), ())), preferred_element_type=F32)


def split_columns(first, second):
    src = lax.broadcasted_iota(jnp.int32, (first, second), 0)
    col = lax.broadcasted_iota(jnp.int32, (1, second), 1)
    part = col // 256
    inner = col % 256
    half = inner // 128
    lane = inner % 128
    rotary = jnp.where(lane < 96, 192 * part + 64 * (lane // 32) + 32 * half + lane % 32, -1)
    plain = jnp.where(inner < 192, 384 + inner, -1)
    want = jnp.where(part < 2, rotary, plain)
    return (src == want).astype(F32).astype(BF)


def head_lanes(width, head):
    lane = lax.broadcasted_iota(jnp.int32, (1, width), 1) % 128
    return (lane >= 32 * head) & (lane < 32 * head + 32)


def value_lanes(width, head):
    lane = lax.broadcasted_iota(jnp.int32, (1, width), 1)
    return (lane >= 64 * head) & (lane < 64 * head + 64)


def forward_kernel(
    ids, t0, t1, t2, t3, cos, sin, docq, dock, w0, w1, w2, w3, w4, w5, w6, w7,
    n16, q8, key, val, att, a0, a1, a2, a3, prob, gain, wide, wscr, sems,
):
    step = pl.program_id(0)

    @pl.when(step == 0)
    def _():
        copies = []
        for k, piece in enumerate((w0, w1, w2, w3, w4, w5, w6, w7)):
            at = pl.multiple_of(96 * (ids[1] ^ k), 96)
            copies.append(pltpu.make_async_copy(piece, wscr.at[pl.ds(at, 96)], sems.at[k]))
            copies[-1].start()
        for copy in copies:
            copy.wait()
        weight = wscr[...]
        wide[...] = dot_nn(weight, split_columns(640, 768)).astype(BF)
        row = lax.broadcasted_iota(jnp.int32, (8, 640), 0)
        col = lax.broadcasted_iota(jnp.int32, (8, 640), 1)
        pick = ((col == row + 576) & (row < 2)).astype(F32).astype(BF)
        gain[...] = dot_nt(pick, weight)
        gain_row = gain[0:1, :]
        for i, piece in enumerate((t0, t1, t2, t3)):
            rows = slice(256 * i, 256 * i + 256)
            x = piece[...].astype(F32)
            center = x - jnp.mean(x, axis=-1, keepdims=True)
            inverse = lax.rsqrt(jnp.mean(center * center, axis=-1, keepdims=True) + NORM_EPS)
            normed = (center * inverse * gain_row).astype(BF)
            n16[rows, :] = normed
            mixed = dot_nn(normed, wide[...])
            c, s = cos[rows, :], sin[rows, :]
            qa, qb = mixed[:, :128], mixed[:, 128:256]
            ka, kb = mixed[:, 256:384], mixed[:, 384:512]
            q8[rows, :128] = ((qa * c - qb * s).astype(BF).astype(F32) * 0.125).astype(BF)
            q8[rows, 128:] = ((qb * c + qa * s).astype(BF).astype(F32) * 0.125).astype(BF)
            key[rows, :128] = (ka * c - kb * s).astype(BF)
            key[rows, 128:] = (kb * c + ka * s).astype(BF)
            val[rows, :] = mixed[:, 512:].astype(BF)

    rows = pl.ds(pl.multiple_of(step * 256, 256), 256)
    queries = q8[rows, :]
    keys = key[...]
    values = val[...]
    same = docq[rows, :] == dock[...]
    total = jnp.zeros((256, 256), F32)
    zero = jnp.zeros((), BF)
    for h in range(3):
        scores = dot_nt(jnp.where(head_lanes(256, h), queries, zero), keys)
        scores = jnp.where(same, scores, MASKED)
        peak = jnp.max(scores, axis=-1, keepdims=True)
        weights = jnp.exp(scores - peak)
        scale = 1.0 / jnp.sum(weights, axis=-1, keepdims=True)
        weights16 = (weights * scale).astype(BF)
        prob[h] = weights16
        total += dot_nn(weights16, jnp.where(value_lanes(256, h), values, zero))
    att[...] = total[:, :192]
    low = total[:, :192].astype(BF)
    for i, out in enumerate((a0, a1, a2, a3)):

        @pl.when(step == i)
        def _():
            out[...] = low


def full(shape):
    return pl.BlockSpec(shape, lambda *_: (0,) * len(shape))


SMEM = pl.BlockSpec(memory_space=pltpu.SMEM)
ANY = pl.BlockSpec(memory_space=pl.ANY)


def shaped(shape, dtype):
    return jax.ShapeDtypeStruct(shape, dtype)


def forward_attention(ids, token_pieces, cos, sin, docs, w_pieces):
    return pl.pallas_call(
        forward_kernel,
        grid=(4,),
        in_specs=[SMEM]
        + [full((256, 768))] * 4
        + [full((1024, 128))] * 2
        + [full((1024, 1)), full((1, 1024))]
        + [ANY] * 8,
        out_specs=[
            full((1024, 768)),
            full((1024, 256)),
            full((1024, 256)),
            full((1024, 256)),
            pl.BlockSpec((256, 192), lambda i: (i, 0)),
            full((256, 192)),
            full((256, 192)),
            full((256, 192)),
            full((256, 192)),
            pl.BlockSpec((3, 256, 1024), lambda i: (0, i, 0)),
            full((8, 768)),
            full((768, 768)),
        ],
        out_shape=[
            shaped((1024, 768), BF),
            shaped((1024, 256), BF),
            shaped((1024, 256), BF),
            shaped((1024, 256), BF),
            shaped((1024, 192), F32),
            shaped((256, 192), BF),
            shaped((256, 192), BF),
            shaped((256, 192), BF),
            shaped((256, 192), BF),
            shaped((3, 1024, 1024), BF),
            shaped((8, 768), F32),
            shaped((768, 768), BF),
        ],
        scratch_shapes=[pltpu.VMEM((768, 640), BF), pltpu.SemaphoreType.DMA((8,))],
        compiler_params=pltpu.CompilerParams(vmem_limit_bytes=VMEM_LIMIT),
        cost_estimate=pl.CostEstimate(flops=6 * 10**9, bytes_accessed=16 * 10**6, transcendentals=3 * 10**6),
        name="forward_attention",
    )(ids, *token_pieces, cos, sin, docs[:, None], docs[None, :], *w_pieces)


def erf_pair(x):
    cdf = 0.5 * (1.0 + lax.erf(x * (0.5**0.5)))
    density = jnp.exp(-0.5 * x * x) * (1.0 / (2.0 * 3.141592653589793) ** 0.5)
    return cdf, density


SLOTS = 16


def feed_kernel(*refs):
    ids, tok, cot, live, gain, a0, a1, a2, a3 = refs[:9]
    first = refs[9 : 9 + SLOTS]
    last = refs[9 + SLOTS : 9 + 2 * SLOTS]
    (block, dmid, d0, d1, d2, d3, act16, n2low, dgate, dbr, ggain, w_in, w_out, w_down, sems) = refs[
        9 + 2 * SLOTS :
    ]
    f, core, chip = ids[0], ids[2], ids[3]
    copies = []

    def load(source, target):
        copies.append(pltpu.make_async_copy(source, target, sems.at[len(copies)]))
        copies[-1].start()

    places = []
    for owner in range(2):
        half = core if owner == 0 else 1 - core
        for group in range(8):
            for j in range(2):
                kx, ky, kz = (group >> 1) & 1, (group >> 2) & 1, (group & 1) * 2 + j
                mask = kz * 4 + ky * 2 + kx
                at = pl.multiple_of(48 * (chip ^ mask), 48)
                places.append((owner * 8 + group, j, half, pl.ds(at, 48)))
    for which, j, half, rows in places:
        load(first[which].at[j, :, pl.ds(1152, 384)], w_out.at[half, rows])
    for which, j, half, rows in places:
        load(first[which].at[j, :, pl.ds(0, 1152)], w_in.at[half, rows])
    for which, j, half, rows in places:
        load(last[which].at[j], w_down.at[half, rows])
    for copy in copies[:32]:
        copy.wait()
    tok_f = tok[...].astype(F32)
    pieces = [a[...] for a in (a0, a1, a2, a3)]
    heads = [pl.ds(pl.multiple_of(192 * (f ^ k), 192), 192) for k in range(4)]
    left = jnp.zeros((256, 384), F32)
    right = jnp.zeros((256, 384), F32)
    for k in range(4):
        left += dot_nn(pieces[k], w_out[0, heads[k], :])
        right += dot_nn(pieces[k], w_out[1, heads[k], :])
    middle = tok_f + jnp.concatenate([left, right], axis=1)
    center = middle - jnp.mean(middle, axis=-1, keepdims=True)
    inverse = lax.rsqrt(jnp.mean(center * center, axis=-1, keepdims=True) + NORM_EPS)
    normed = center * inverse
    gain_row = gain[1:2, :]
    low = (normed * gain_row).astype(BF)
    n2low[...] = low
    for copy in copies[32:64]:
        copy.wait()
    act = dot_nn(low, w_in[0])
    gate = dot_nn(low, w_in[1])
    cdf, density = erf_pair(act)
    gelu = act * cdf
    active = (gelu * gate).astype(BF)
    act16[...] = active
    for copy in copies[64:]:
        copy.wait()
    alive = live[...]
    dout = jnp.where(alive > 0.5, cot[...].astype(F32), 0.0)
    dym = dout.astype(BF)
    dact = jnp.concatenate([dot_nn(dym, w_down[0]), dot_nn(dym, w_down[1, :, :512])], axis=1)
    dg_front = (dact * gate * (cdf + act * density)).astype(BF)
    dg_rear = (dact * gelu).astype(BF)
    dgate[:, :1152] = dg_front
    dgate[:, 1152:] = dg_rear
    dnormed = dot_nt(dg_front, w_in[0]) + dot_nt(dg_rear, w_in[1])
    ggain[...] = jnp.broadcast_to(jnp.sum(dnormed * normed, axis=0, keepdims=True), (8, 768))
    up = dnormed * gain_row
    dmiddle = dout + inverse * (
        up
        - jnp.mean(up, axis=-1, keepdims=True)
        - normed * jnp.mean(up * normed, axis=-1, keepdims=True)
    )
    dmid[...] = dmiddle
    dbranch = dmiddle.astype(BF)
    dbr[...] = dbranch
    for k, out in enumerate((d0, d1, d2, d3)):
        out[...] = (
            dot_nt(dbranch[:, :384], w_out[0, heads[k], :]) + dot_nt(dbranch[:, 384:], w_out[1, heads[k], :])
        ).astype(BF)
    branch = dot_nt(active[:, :640], w_down[0]) + dot_nt(active[:, 640:], w_down[1, :, :512])
    block[...] = jnp.where(alive > 0.5, middle + branch, 0.0).astype(BF)


def feed_forward(ids, tokens, cotangent, live, gain, att_pieces, first, last):
    return pl.pallas_call(
        feed_kernel,
        in_specs=[SMEM] + [pl.BlockSpec(memory_space=pltpu.VMEM)] * 8 + [ANY] * (2 * SLOTS),
        out_specs=[pl.BlockSpec(memory_space=pltpu.VMEM)] * 11,
        out_shape=[
            shaped((256, 768), BF),
            shaped((256, 768), F32),
            shaped((256, 192), BF),
            shaped((256, 192), BF),
            shaped((256, 192), BF),
            shaped((256, 192), BF),
            shaped((256, 1152), BF),
            shaped((256, 768), BF),
            shaped((256, 2304), BF),
            shaped((256, 768), BF),
            shaped((8, 768), F32),
        ],
        scratch_shapes=[
            pltpu.VMEM((2, 768, 1152), BF),
            pltpu.VMEM((2, 768, 384), BF),
            pltpu.VMEM((2, 768, 640), BF),
            pltpu.SemaphoreType.DMA((96,)),
        ],
        compiler_params=pltpu.CompilerParams(vmem_limit_bytes=VMEM_LIMIT),
        cost_estimate=pl.CostEstimate(flops=5 * 10**9, bytes_accessed=12 * 10**6, transcendentals=10**6),
        name="feed_forward",
    )(ids, tokens, cotangent, live, gain, *att_pieces, *first, *last)


CHUNK = 2176


def feed_grad_kernel(
    ids, cot, live, act16, n2low, dgate, dbr, a0, a1, a2, a3,
    s0, s1, s2, s3, k0, k1, k2, k3, grads, sems,
):
    f, core, chip = ids[0], ids[2], ids[3]
    dym = jnp.where(live[...] > 0.5, cot[...].astype(F32), 0.0).astype(BF)
    gdown = dot_tn(dym, act16[...])
    grads[0, :, 1536:2176] = gdown[:, :640].astype(BF)
    grads[1, :, 1536:2048] = gdown[:, 640:].astype(BF)
    grads[1, :, 2048:2176] = jnp.zeros((768, 128), BF)
    low = n2low[...]
    grads[0, :, :1152] = dot_tn(low, dgate[:, :1152]).astype(BF)
    grads[1, :, :1152] = dot_tn(low, dgate[:, 1152:]).astype(BF)
    branch = dbr[...]
    for k, piece in enumerate((a0, a1, a2, a3)):
        rows = pl.ds(pl.multiple_of(192 * (f ^ k), 192), 192)
        gout = dot_tn(piece[...], branch).astype(BF)
        grads[0, rows, 1152:1536] = gout[:, :384]
        grads[1, rows, 1152:1536] = gout[:, 384:]
    copies = []
    for group in (3, 1, 2, 0):
        for kz in range(4):
            at = pl.multiple_of(48 * (chip ^ (kz * 4 + group)), 48)
            for half, target in ((1 - core, (s0, s1, s2, s3)[group]), (core, (k0, k1, k2, k3)[group])):
                copies.append(
                    pltpu.make_async_copy(grads.at[half, pl.ds(at, 48)], target.at[kz], sems.at[len(copies)])
                )
                copies[-1].start()
    for copy in copies:
        copy.wait()


def feed_gradients(ids, cotangent, live, act16, n2low, dgate, dbr, att_pieces):
    return pl.pallas_call(
        feed_grad_kernel,
        in_specs=[SMEM] + [pl.BlockSpec(memory_space=pltpu.VMEM)] * 10,
        out_specs=[ANY] * 8,
        out_shape=[shaped((4, 48, CHUNK), BF)] * 8,
        scratch_shapes=[pltpu.VMEM((2, 768, CHUNK), BF), pltpu.SemaphoreType.DMA((32,))],
        compiler_params=pltpu.CompilerParams(vmem_limit_bytes=VMEM_LIMIT),
        cost_estimate=pl.CostEstimate(flops=3 * 10**9, bytes_accessed=12 * 10**6, transcendentals=0),
        name="feed_gradients",
    )(ids, cotangent, live, act16, n2low, dgate, dbr, *att_pieces)


def backward_kernel(
    ids, t0, t1, t2, t3, cos, sin, n16, q8, key, val, att, prob, d0, d1, d2, d3, gain, wide, ggain,
    dn0, dn1, dn2, dn3, far, near, dq, dkt, dvt, grads, sems,
):
    step = pl.program_id(0)

    @pl.when(step == 0)
    def _():
        dkt[...] = jnp.zeros((256, 1024), F32)
        dvt[...] = jnp.zeros((256, 1024), F32)

    rows = pl.ds(pl.multiple_of(step * 256, 256), 256)
    zero = jnp.zeros((), BF)
    keys = key[...]
    values = val[...]
    dattn = d0[...]
    for i, piece in ((1, d1), (2, d2), (3, d3)):
        dattn = jnp.where(step == i, piece[...], dattn)
    dattn = jnp.concatenate([dattn, jnp.zeros((256, 64), BF)], axis=1)
    product = dattn[:, :192].astype(F32) * att[...]
    queries_t = q8[rows, :].T
    dattn_t = dattn.T
    total = jnp.zeros((256, 256), F32)
    for h in range(3):
        weights = prob[h]
        dprob = dot_nt(jnp.where(value_lanes(256, h), dattn, zero), values)
        delta = jnp.sum(jnp.where(value_lanes(192, h), product, 0.0), axis=-1, keepdims=True)
        dscores = (weights.astype(F32) * (dprob - delta)).astype(BF)
        total += dot_nn(dscores, jnp.where(head_lanes(256, h), keys, zero))
        q_head = jnp.concatenate([queries_t[32 * h : 32 * h + 32], queries_t[128 + 32 * h : 160 + 32 * h]], axis=0)
        dk_head = dot_nn(q_head, dscores)
        dkt[32 * h : 32 * h + 32, :] += dk_head[:32]
        dkt[128 + 32 * h : 160 + 32 * h, :] += dk_head[32:]
        dvt[64 * h : 64 * h + 64, :] += dot_nn(dattn_t[64 * h : 64 * h + 64], weights)
    c, s = cos[rows, :], sin[rows, :]
    dqa, dqb = total[:, :128] * 0.125, total[:, 128:] * 0.125
    dq[rows, :128] = (dqa * c + dqb * s).astype(BF)
    dq[rows, 128:256] = (dqb * c - dqa * s).astype(BF)

    @pl.when(step == 3)
    def _():
        dk = dkt[...].T
        ca, sa = cos[...], sin[...]
        dq[:, 256:384] = (dk[:, :128] * ca + dk[:, 128:] * sa).astype(BF)
        dq[:, 384:512] = (dk[:, 128:] * ca - dk[:, :128] * sa).astype(BF)
        dq[:, 512:768] = dvt[...].T.astype(BF)
        ggain1 = jnp.zeros((1, 768), F32)
        for i, (piece, out) in enumerate(((t0, dn0), (t1, dn1), (t2, dn2), (t3, dn3))):
            part = dot_nt(dq[256 * i : 256 * i + 256, :], wide[...])
            x = piece[...].astype(F32)
            center = x - jnp.mean(x, axis=-1, keepdims=True)
            inverse = lax.rsqrt(jnp.mean(center * center, axis=-1, keepdims=True) + NORM_EPS)
            ggain1 += jnp.sum(part * (center * inverse), axis=0, keepdims=True)
            out[...] = part.astype(BF)
        wide_grad = dot_tn(n16[...], dq[...]).astype(BF)
        natural = dot_nt(wide_grad, split_columns(640, 768))
        gains = jnp.concatenate([ggain1, ggain[0:1, :], jnp.zeros((126, 768), F32)], axis=0)
        column = jnp.concatenate([natural[:, :512], natural[:, 512:576], gains.T[:, :64]], axis=1)
        grads[...] = column.astype(BF)
        copies = []
        for ky, target in ((1, far), (0, near)):
            for kz in range(4):
                at = pl.multiple_of(96 * (ids[1] ^ (kz * 2 + ky)), 96)
                copies.append(
                    pltpu.make_async_copy(grads.at[pl.ds(at, 96)], target.at[kz], sems.at[len(copies)])
                )
                copies[-1].start()
        for copy in copies:
            copy.wait()


def backward_attention(ids, token_pieces, cos, sin, n16, q8, key, val, att, prob, d_pieces, gain, wide, ggain):
    return pl.pallas_call(
        backward_kernel,
        grid=(4,),
        in_specs=[SMEM]
        + [full((256, 768))] * 4
        + [full((1024, 128))] * 2
        + [full((1024, 768))]
        + [full((1024, 256))] * 3
        + [pl.BlockSpec((256, 192), lambda i: (i, 0))]
        + [pl.BlockSpec((3, 256, 1024), lambda i: (0, i, 0))]
        + [full((256, 192))] * 4
        + [full((8, 768)), full((768, 768)), full((8, 768))],
        out_specs=[full((256, 768))] * 4 + [ANY, ANY],
        out_shape=[shaped((256, 768), BF)] * 4 + [shaped((4, 96, 640), BF)] * 2,
        scratch_shapes=[
            pltpu.VMEM((1024, 768), BF),
            pltpu.VMEM((256, 1024), F32),
            pltpu.VMEM((256, 1024), F32),
            pltpu.VMEM((768, 640), BF),
            pltpu.SemaphoreType.DMA((8,)),
        ],
        compiler_params=pltpu.CompilerParams(vmem_limit_bytes=VMEM_LIMIT),
        cost_estimate=pl.CostEstimate(flops=8 * 10**9, bytes_accessed=16 * 10**6, transcendentals=0),
        name="backward_attention",
    )(ids, *token_pieces, cos, sin, n16, q8, key, val, att, prob, *d_pieces, gain, wide, ggain)


def pack_layout(count_row, length_row, slots, own_place):
    devices_here = count_row.shape[0]
    places = jnp.arange(devices_here * slots, dtype=jnp.int32)
    holder = (places // slots) ^ own_place
    within = places % slots
    before = jnp.cumsum(count_row) - count_row
    choose = (holder[:, None] == jnp.arange(devices_here, dtype=jnp.int32)[None, :]).astype(jnp.int32)
    offset = jnp.sum(choose * before[None, :], axis=1) + within
    limits = jnp.sum(choose * count_row[None, :], axis=1)
    living = within < limits
    doc_ends = jnp.cumsum(length_row)
    passed = offset[:, None] >= doc_ends[None, :]
    document = jnp.sum(passed.astype(jnp.int32), axis=1)
    begins = jnp.max(jnp.where(passed, doc_ends[None, :], 0), axis=1)
    document = jnp.where(living, document, length_row.shape[0])
    position = jnp.where(living, offset - begins, 0)
    return document, position, living


def by_place(pieces, low_bit, high_bit):
    a, b, c, d = pieces
    t0, t1 = jnp.where(low_bit, b, a), jnp.where(low_bit, a, b)
    t2, t3 = jnp.where(low_bit, d, c), jnp.where(low_bit, c, d)
    return [
        jnp.where(high_bit, t2, t0),
        jnp.where(high_bit, t3, t1),
        jnp.where(high_bit, t0, t2),
        jnp.where(high_bit, t1, t3),
    ]


def gather_halves(halves, core):
    mine = jnp.where(core == 0, halves[0], halves[1])
    other = jnp.where(core == 0, halves[1], halves[0])
    came = xperm(other, 1)
    lower, upper = jnp.where(core == 0, mine, came), jnp.where(core == 0, came, mine)
    own = jnp.concatenate([lower, upper], axis=0)
    z1, z2, z3 = xperm(own, 8), xperm(own, 16), xperm(own, 24)
    p0, p1 = jnp.stack([own, z1]), jnp.stack([z2, z3])
    x0, y0 = xperm(p0, 2), xperm(p0, 4)
    x1, y1 = xperm(p1, 2), xperm(p1, 4)
    xy0 = xperm(y0, 2)
    xy1 = xperm(x1, 4)
    held = [p0, p1, x0, x1, y0, y1, xy0, xy1]
    return held + [xperm(piece, 1) for piece in held]


def fast_body(
    tokens, cotangent, counts, lengths,
    weight_qkv, weight_out, weight_in, weight_down, norm_gains,
    first_qkv, first_out, first_in, first_down, first_gains,
    second_qkv, second_out, second_in, second_down, second_gains,
    average_qkv, average_out, average_in, average_down, average_gains,
):
    slots = tokens.shape[0]
    group_row = lax.axis_index("dp")
    own_place = lax.axis_index("fsdp")
    core, side = own_place & 1, own_place >> 1
    chip = group_row * 2 + side
    ids = jnp.stack([own_place, group_row, core, chip]).astype(jnp.int32)

    qkv16 = weight_qkv.astype(BF)
    blocks = qkv16.reshape(24, 3, 4, 192).transpose(2, 0, 1, 3).reshape(4, 24, 576)
    gain_cols = jnp.concatenate([norm_gains.T.astype(BF), jnp.zeros((24, 62), BF)], axis=1)
    blocks = jnp.concatenate([blocks, jnp.broadcast_to(gain_cols[None], (4, 24, 64))], axis=2)
    sends = [lax.dynamic_index_in_dim(blocks, own_place ^ k, 0, keepdims=False) for k in range(4)]
    came = [sends[0]] + [xperm(sends[k], k) for k in (1, 2, 3)]
    rows_here = jnp.concatenate(by_place(came, core == 1, side == 1), axis=0)
    column = [rows_here, xperm(rows_here, 8), xperm(rows_here, 16), xperm(rows_here, 24)]
    w_pieces = []
    for piece in column:
        w_pieces += [piece, xperm(piece, 4)]

    tok_x, tok_c = xperm(tokens, 2), xperm(tokens, 1)
    token_pieces = [tokens, tok_c, tok_x, xperm(tok_x, 1)]

    in16, out16, down16 = weight_in.astype(BF), weight_out.astype(BF), weight_down.astype(BF)
    down16 = jnp.pad(down16, ((0, 0), (0, 128)))
    first = gather_halves(
        [
            jnp.concatenate([in16[:, 1152 * h : 1152 * h + 1152], out16[:, 384 * h : 384 * h + 384]], axis=1)
            for h in range(2)
        ],
        core,
    )
    last = gather_halves([down16[:, 640 * h : 640 * h + 640] for h in range(2)], core)

    count_row = lax.dynamic_index_in_dim(counts, group_row, 0, keepdims=False)
    length_row = lax.dynamic_index_in_dim(lengths, group_row, 0, keepdims=False)
    docs, position, living = pack_layout(count_row, length_row, slots, own_place)
    speeds = ROTARY_BASE ** (-(jnp.arange(HD // 2, dtype=F32) * (2.0 / HD)))
    angles = position.astype(F32)[:, None] * jnp.tile(speeds, 4)[None, :]
    cos, sin = jnp.cos(angles), jnp.sin(angles)
    live = living[:slots, None].astype(F32)

    n16, q8, key, val, att, a0, a1, a2, a3, prob, gain, wide = forward_attention(
        ids, token_pieces, cos, sin, docs, w_pieces
    )
    att_pieces = [a0, xperm(a1, 1), xperm(a2, 2), xperm(a3, 3)]
    block_out, dmiddle, d0, d1, d2, d3, act16, n2low, dgate, dbr, ggain = feed_forward(
        ids, tokens, cotangent, live, gain, att_pieces, first, last
    )
    d_pieces = [d0, xperm(d1, 1), xperm(d2, 2), xperm(d3, 3)]
    s0, s1, s2, s3, k0, k1, k2, k3 = feed_gradients(
        ids, cotangent, live, act16, n2low, dgate, dbr, att_pieces
    )

    def add(*parts):
        total = parts[0].astype(F32)
        for part in parts[1:]:
            total = total + part.astype(F32)
        return total.astype(BF)

    e3 = add(k3, xperm(s3, 1))
    e1 = add(k1, xperm(s1, 1))
    e2 = add(k2, xperm(s2, 1))
    e0 = add(k0, xperm(s0, 1))
    to_y = xperm(e3[:2], 2)
    to_x = xperm(e3[2:], 4)
    x0 = xperm(e1[:2], 2)
    y1 = xperm(e2[2:], 4)
    y0 = xperm(add(e2[:2], to_y), 4)
    x1 = xperm(add(e1[2:], to_x), 2)
    f0 = add(e0[:2], x0, y0)
    f1 = add(e0[2:], x1, y1)
    chip_rows = add(f0[0], xperm(f0[1], 8), xperm(f1[0], 16), xperm(f1[1], 24))
    lower, upper = chip_rows[:24], chip_rows[24:]
    mine, other = jnp.where(core == 0, lower, upper), jnp.where(core == 0, upper, lower)
    came = xperm(other, 1)
    half0 = jnp.where(core == 0, mine, came).astype(F32)
    half1 = jnp.where(core == 0, came, mine).astype(F32)
    grad_in = jnp.concatenate([half0[:, :1152], half1[:, :1152]], axis=1)
    grad_out = jnp.concatenate([half0[:, 1152:1536], half1[:, 1152:1536]], axis=1)
    grad_down = jnp.concatenate([half0[:, 1536:2176], half1[:, 1536:2048]], axis=1)

    dn0, dn1, dn2, dn3, far, near = backward_attention(
        ids, token_pieces, cos, sin, n16, q8, key, val, att, prob, d_pieces, gain, wide, ggain
    )
    e = add(near, xperm(far, 4))
    dp_rows = add(e[0], xperm(e[1], 8), xperm(e[2], 16), xperm(e[3], 24)).reshape(4, 24, 640)
    sends = [lax.dynamic_index_in_dim(dp_rows, own_place ^ k, 0, keepdims=False) for k in range(4)]
    came = [sends[0]] + [xperm(sends[k], k) for k in (1, 2, 3)]
    placed = jnp.stack(by_place([piece.astype(F32) for piece in came], core == 1, side == 1))
    grad_qkv = placed[:, :, :576].reshape(4, 24, 3, 192).transpose(1, 2, 0, 3).reshape(24, 2304)
    grad_gains = jnp.sum(placed[:, :, 576:578], axis=0).T

    own_sum, x_sum = add(dn0, xperm(dn1, 1)), add(dn2, xperm(dn3, 1))
    dnormed = own_sum.astype(F32) + xperm(x_sum, 2).astype(F32)
    normed, inverse = norm_parts(tokens.astype(F32))
    grad_tokens = dmiddle + norm_back(dnormed * gain[0:1, :], normed, inverse)

    masters = (weight_qkv, weight_out, weight_in, weight_down, norm_gains)
    firsts = (first_qkv, first_out, first_in, first_down, first_gains)
    seconds = (second_qkv, second_out, second_in, second_down, second_gains)
    averages = (average_qkv, average_out, average_in, average_down, average_gains)
    rates = (MATRIX_RATE, MATRIX_RATE, MATRIX_RATE, MATRIX_RATE, GAIN_RATE)
    grads = (grad_qkv, grad_out, grad_in, grad_down, grad_gains)
    updated = [
        adam_update(masters[i], firsts[i], seconds[i], averages[i], grads[i], rates[i]) for i in range(5)
    ]
    return (block_out, grad_tokens) + tuple(updated[i][j] for j in range(5) for i in range(5))


def solution(mesh):
    sizes = dict(mesh.shape)
    body = fast_body if sizes == {"dp": 8, "fsdp": 4} else general_body
    rows, columns = P(("dp", "fsdp"), None), P(None, ("dp", "fsdp"))
    weights = (rows,) * 4 + (columns,)
    return jax.shard_map(
        body,
        mesh=mesh,
        in_specs=(rows, rows, P(), P()) + weights * 4,
        out_specs=(rows, rows) + weights * 5,
        check_vma=False,
    )
```

```python
import functools

import jax
import jax.numpy as jnp
from jax import lax
from jax.experimental import pallas as pl
from jax.experimental.pallas import tpu as pltpu
from jax.sharding import PartitionSpec as P

HEADS = 12
HD = 64
STEP = 6


NORM_EPS = 1e-05
ROTARY_BASE = 160000.0
BETA_FIRST = 0.5
BETA_SECOND = 0.5
ADAM_EPS = 1e-08
WEIGHT_DECAY = 0.01
MATRIX_RATE = 0.04
GAIN_RATE = 0.5
AVERAGE_KEEP = 0.6
MASKED = -1e30


def group_layout(count_row, length_row, slots):
    devices_here = count_row.shape[0]
    places = jnp.arange(devices_here * slots, dtype=jnp.int32)
    holder = places // slots
    within = places - holder * slots
    before = jnp.cumsum(count_row) - count_row
    choose = (holder[:, None] == jnp.arange(devices_here, dtype=jnp.int32)[None, :]).astype(
        jnp.int32
    )
    offset = jnp.sum(choose * before[None, :], axis=1) + within
    limits = jnp.sum(choose * count_row[None, :], axis=1)
    living = within < limits
    doc_ends = jnp.cumsum(length_row)
    passed = offset[:, None] >= doc_ends[None, :]
    document = jnp.sum(passed.astype(jnp.int32), axis=1)
    begins = jnp.max(jnp.where(passed, doc_ends[None, :], 0), axis=1)
    number_docs = length_row.shape[0]
    document = jnp.where(living, document, number_docs)
    position = jnp.where(living, offset - begins, 0)
    return (document, position, living)


def rotary_tables(position, head_size):
    half_size = head_size // 2
    speeds = ROTARY_BASE ** (-(jnp.arange(half_size, dtype=jnp.float32) * (2.0 / head_size)))
    angles = position.astype(jnp.float32)[:, None] * speeds[None, :]
    return (jnp.cos(angles), jnp.sin(angles))


def rotate(heads_in, cosine_table, sine_table):
    half_size = heads_in.shape[-1] // 2
    leading = heads_in[..., :half_size]
    latter = heads_in[..., half_size:]
    cos_wide = cosine_table[:, None, :]
    sin_wide = sine_table[:, None, :]
    return jnp.concatenate(
        [leading * cos_wide - latter * sin_wide, latter * cos_wide + leading * sin_wide], axis=-1
    )


def rotate_back(grads_in, cosine_table, sine_table):
    half_size = grads_in.shape[-1] // 2
    leading = grads_in[..., :half_size]
    latter = grads_in[..., half_size:]
    cos_wide = cosine_table[:, None, :]
    sin_wide = sine_table[:, None, :]
    return jnp.concatenate(
        [leading * cos_wide + latter * sin_wide, latter * cos_wide - leading * sin_wide], axis=-1
    )


def norm_parts(values_in):
    center = values_in - jnp.mean(values_in, axis=-1, keepdims=True)
    inverse = lax.rsqrt(jnp.mean(center * center, axis=-1, keepdims=True) + NORM_EPS)
    return (center * inverse, inverse)


def norm_back(upstream, normed, inverse):
    return inverse * (
        upstream
        - jnp.mean(upstream, axis=-1, keepdims=True)
        - normed * jnp.mean(upstream * normed, axis=-1, keepdims=True)
    )


def block_scores(queries, key_block, doc_query, doc_key, score_scale):
    scores = (
        jnp.einsum("qhd,khd->hqk", queries, key_block, preferred_element_type=jnp.float32)
        * score_scale
    )
    return jnp.where(doc_query[None, :, None] == doc_key[None, None, :], scores, MASKED)


def contract_rows(left_side, right_side):
    return lax.dot_general(
        left_side, right_side, (((0,), (0,)), ((), ())), preferred_element_type=jnp.float32
    )


def contract_cols(left_side, right_side):
    return lax.dot_general(
        left_side, right_side, (((1,), (1,)), ((), ())), preferred_element_type=jnp.float32
    )


def adam_update(master, first_old, second_old, average_old, gradient, step_rate):
    first_new = BETA_FIRST * first_old + (1.0 - BETA_FIRST) * gradient
    second_new = BETA_SECOND * second_old + (1.0 - BETA_SECOND) * gradient * gradient
    first_fix = first_new / (1.0 - BETA_FIRST**STEP)
    second_fix = second_new / (1.0 - BETA_SECOND**STEP)
    master_new = master - step_rate * (
        first_fix / (jnp.sqrt(second_fix) + ADAM_EPS) + WEIGHT_DECAY * master
    )
    average_new = AVERAGE_KEEP * average_old + (1.0 - AVERAGE_KEEP) * master_new
    return (first_new, second_new, master_new, average_new, master_new.astype(jnp.bfloat16))


def general_body(
    tokens,
    cotangent,
    counts,
    lengths,
    weight_qkv,
    weight_out,
    weight_in,
    weight_down,
    norm_gains,
    first_qkv,
    first_out,
    first_in,
    first_down,
    first_gains,
    second_qkv,
    second_out,
    second_in,
    second_down,
    second_gains,
    average_qkv,
    average_out,
    average_in,
    average_down,
    average_gains,
):
    slots = tokens.shape[0]
    model_width = tokens.shape[1]
    hidden_units = weight_down.shape[1]
    head_count = HEADS
    head_size = HD
    score_scale = 1.0 / head_size**0.5
    heads_shape = (slots, head_count, head_size)
    group_row = lax.axis_index("dp")
    own_place = lax.axis_index("fsdp")
    count_row = lax.dynamic_index_in_dim(counts, group_row, 0, keepdims=False)
    length_row = lax.dynamic_index_in_dim(lengths, group_row, 0, keepdims=False)
    doc_all, position_all, living_all = group_layout(count_row, length_row, slots)
    doc_mine = lax.dynamic_slice_in_dim(doc_all, own_place * slots, slots)
    position_mine = lax.dynamic_slice_in_dim(position_all, own_place * slots, slots)
    living_mine = lax.dynamic_slice_in_dim(living_all, own_place * slots, slots)
    cosine_table, sine_table = rotary_tables(position_mine, head_size)
    living_col = living_mine[:, None]
    copies = (
        weight_qkv.astype(jnp.bfloat16),
        weight_out.astype(jnp.bfloat16),
        weight_in.astype(jnp.bfloat16),
        weight_down.astype(jnp.bfloat16),
        norm_gains.astype(jnp.bfloat16),
    )
    qkv_full, out_full, in_full, down_full, gain_full = (
        lax.all_gather(copies[0], ("dp", "fsdp"), axis=0, tiled=True),
        lax.all_gather(copies[1], ("dp", "fsdp"), axis=0, tiled=True),
        lax.all_gather(copies[2], ("dp", "fsdp"), axis=0, tiled=True),
        lax.all_gather(copies[3], ("dp", "fsdp"), axis=0, tiled=True),
        lax.all_gather(copies[4], ("dp", "fsdp"), axis=1, tiled=True),
    )
    tokens_f = tokens.astype(jnp.float32)
    normed_one, inverse_one = norm_parts(tokens_f)
    gain_one = gain_full[0].astype(jnp.float32)
    gain_two = gain_full[1].astype(jnp.float32)
    normed1_low = (normed_one * gain_one).astype(jnp.bfloat16)
    mixed_qkv = jnp.dot(normed1_low, qkv_full, preferred_element_type=jnp.float32)
    queries16 = rotate(
        mixed_qkv[:, :model_width].reshape(heads_shape), cosine_table, sine_table
    ).astype(jnp.bfloat16)
    keys16 = rotate(
        mixed_qkv[:, model_width : 2 * model_width].reshape(heads_shape), cosine_table, sine_table
    ).astype(jnp.bfloat16)
    key_flat = keys16.reshape(slots, model_width)
    value_flat = mixed_qkv[:, 2 * model_width :].astype(jnp.bfloat16)
    key_rows, value_rows = (
        lax.all_gather(key_flat, "fsdp", axis=0, tiled=True),
        lax.all_gather(value_flat, "fsdp", axis=0, tiled=True),
    )
    group_rows = key_rows.shape[0]
    block_rows = 512
    count_blocks = group_rows // block_rows
    blocks_shape = (count_blocks, block_rows, head_count, head_size)
    doc_blocks = doc_all.reshape(count_blocks, block_rows)
    key_blocks = key_rows.reshape(blocks_shape)
    value_blocks = value_rows.reshape(blocks_shape)

    def max_sum(state_now, pieces):
        run_peak, run_total = state_now
        scores = block_scores(queries16, pieces[0], doc_mine, pieces[1], score_scale)
        new_peak = jnp.maximum(run_peak, jnp.max(scores, axis=-1))
        run_total = run_total * jnp.exp(run_peak - new_peak) + jnp.sum(
            jnp.exp(scores - new_peak[:, :, None]), axis=-1
        )
        return ((new_peak, run_total), None)

    start_state = (
        jnp.full((head_count, slots), MASKED, jnp.float32),
        jnp.zeros((head_count, slots), jnp.float32),
    )
    (run_peak, run_total), unused_max = lax.scan(max_sum, start_state, (key_blocks, doc_blocks))
    log_total = run_peak + jnp.log(run_total)

    def weigh_values(accum, pieces):
        scores = block_scores(queries16, pieces[0], doc_mine, pieces[2], score_scale)
        probs16 = jnp.exp(scores - log_total[:, :, None]).astype(jnp.bfloat16)
        return (
            accum
            + jnp.einsum("hqk,khd->qhd", probs16, pieces[1], preferred_element_type=jnp.float32),
            None,
        )

    attended, unused_out = lax.scan(
        weigh_values, jnp.zeros(heads_shape, jnp.float32), (key_blocks, value_blocks, doc_blocks)
    )
    attended16 = attended.reshape(slots, model_width).astype(jnp.bfloat16)
    middle = tokens_f + jnp.dot(attended16, out_full, preferred_element_type=jnp.float32)
    normed_two, inverse_two = norm_parts(middle)
    normed2_low = (normed_two * gain_two).astype(jnp.bfloat16)
    gate_up = jnp.dot(normed2_low, in_full, preferred_element_type=jnp.float32)
    act_half = gate_up[:, :hidden_units]
    gate_half = gate_up[:, hidden_units:]
    activated16 = (jax.nn.gelu(act_half, approximate=False) * gate_half).astype(jnp.bfloat16)
    branch_two = contract_cols(activated16, down_full)
    block_out = jnp.where(living_col, middle + branch_two, 0.0).astype(jnp.bfloat16)
    qkv_back, out_back, in_back, down_back, gain_back = (
        lax.all_gather(copies[0], ("dp", "fsdp"), axis=0, tiled=True),
        lax.all_gather(copies[1], ("dp", "fsdp"), axis=0, tiled=True),
        lax.all_gather(copies[2], ("dp", "fsdp"), axis=0, tiled=True),
        lax.all_gather(copies[3], ("dp", "fsdp"), axis=0, tiled=True),
        lax.all_gather(copies[4], ("dp", "fsdp"), axis=1, tiled=True),
    )
    key_again, value_again = (
        lax.all_gather(key_flat, "fsdp", axis=0, tiled=True),
        lax.all_gather(value_flat, "fsdp", axis=0, tiled=True),
    )
    gain_one_back = gain_back[0].astype(jnp.float32)
    gain_two_back = gain_back[1].astype(jnp.float32)
    dout = jnp.where(living_col, cotangent.astype(jnp.float32), 0.0)
    dym16 = dout.astype(jnp.bfloat16)
    grad_down = contract_rows(dym16, activated16)
    dact = jnp.dot(dym16, down_back, preferred_element_type=jnp.float32)
    unused_gate, gate_pull = jax.vjp(
        lambda front_part, rear_part: jax.nn.gelu(front_part, approximate=False) * rear_part,
        act_half,
        gate_half,
    )
    dfront, drear = gate_pull(dact)
    dgate16 = jnp.concatenate([dfront, drear], axis=1).astype(jnp.bfloat16)
    grad_in = contract_rows(normed2_low, dgate16)
    dnormed_two = contract_cols(dgate16, in_back)
    grad_gain_two = jnp.sum(dnormed_two * normed_two, axis=0)
    dmiddle = dout + norm_back(dnormed_two * gain_two_back, normed_two, inverse_two)
    dbranch16 = dmiddle.astype(jnp.bfloat16)
    grad_out = contract_rows(attended16, dbranch16)
    dattn16 = contract_cols(dbranch16, out_back).astype(jnp.bfloat16).reshape(heads_shape)
    row_delta = jnp.sum(dattn16.astype(jnp.float32) * attended, axis=-1).T
    back_keys = key_again.reshape(blocks_shape)
    back_values = value_again.reshape(blocks_shape)

    def back_block(dquery_sum, pieces):
        key_block, value_block, doc_block = pieces
        scores = block_scores(queries16, key_block, doc_mine, doc_block, score_scale)
        probs = jnp.exp(scores - log_total[:, :, None])
        probs16 = probs.astype(jnp.bfloat16)
        dvalue_block = jnp.einsum(
            "hqk,qhd->khd", probs16, dattn16, preferred_element_type=jnp.float32
        )
        dprobs = jnp.einsum(
            "qhd,khd->hqk", dattn16, value_block, preferred_element_type=jnp.float32
        )
        dscores16 = (probs * (dprobs - row_delta[:, :, None])).astype(jnp.bfloat16)
        dquery_sum = dquery_sum + jnp.einsum(
            "hqk,khd->qhd", dscores16, key_block, preferred_element_type=jnp.float32
        )
        dkey_block = jnp.einsum(
            "hqk,qhd->khd", dscores16, queries16, preferred_element_type=jnp.float32
        )
        return (dquery_sum, (dkey_block, dvalue_block))

    dquery_sum, (dkey_blocks, dvalue_blocks) = lax.scan(
        back_block, jnp.zeros(heads_shape, jnp.float32), (back_keys, back_values, doc_blocks)
    )
    dkey_mine, dvalue_mine = (
        lax.psum_scatter(
            (dkey_blocks.reshape(group_rows, model_width) * score_scale).astype(jnp.bfloat16),
            "fsdp",
            scatter_dimension=0,
            tiled=True,
        ).astype(jnp.float32),
        lax.psum_scatter(
            dvalue_blocks.reshape(group_rows, model_width).astype(jnp.bfloat16),
            "fsdp",
            scatter_dimension=0,
            tiled=True,
        ).astype(jnp.float32),
    )
    dquery_pre = rotate_back(dquery_sum * score_scale, cosine_table, sine_table).reshape(
        slots, model_width
    )
    dkey_pre = rotate_back(dkey_mine.reshape(heads_shape), cosine_table, sine_table).reshape(
        slots, model_width
    )
    dmixed16 = jnp.concatenate([dquery_pre, dkey_pre, dvalue_mine], axis=1).astype(jnp.bfloat16)
    grad_qkv = contract_rows(normed1_low, dmixed16)
    dnormed_one = contract_cols(dmixed16, qkv_back)
    grad_gain_one = jnp.sum(dnormed_one * normed_one, axis=0)
    grad_tokens = dmiddle + norm_back(dnormed_one * gain_one_back, normed_one, inverse_one)
    grad_gains = jnp.stack([grad_gain_one, grad_gain_two], axis=0)
    reduced = (
        lax.psum_scatter(grad_qkv, ("dp", "fsdp"), scatter_dimension=0, tiled=True),
        lax.psum_scatter(grad_out, ("dp", "fsdp"), scatter_dimension=0, tiled=True),
        lax.psum_scatter(grad_in, ("dp", "fsdp"), scatter_dimension=0, tiled=True),
        lax.psum_scatter(grad_down, ("dp", "fsdp"), scatter_dimension=0, tiled=True),
        lax.psum_scatter(grad_gains, ("dp", "fsdp"), scatter_dimension=1, tiled=True),
    )
    masters = (weight_qkv, weight_out, weight_in, weight_down, norm_gains)
    firsts = (first_qkv, first_out, first_in, first_down, first_gains)
    seconds = (second_qkv, second_out, second_in, second_down, second_gains)
    averages = (average_qkv, average_out, average_in, average_down, average_gains)
    rates = (MATRIX_RATE, MATRIX_RATE, MATRIX_RATE, MATRIX_RATE, GAIN_RATE)
    updated = [
        adam_update(
            masters[which],
            firsts[which],
            seconds[which],
            averages[which],
            reduced[which],
            rates[which],
        )
        for which in range(5)
    ]
    return (
        block_out,
        grad_tokens,
        updated[0][0],
        updated[1][0],
        updated[2][0],
        updated[3][0],
        updated[4][0],
        updated[0][1],
        updated[1][1],
        updated[2][1],
        updated[3][1],
        updated[4][1],
        updated[0][2],
        updated[1][2],
        updated[2][2],
        updated[3][2],
        updated[4][2],
        updated[0][3],
        updated[1][3],
        updated[2][3],
        updated[3][3],
        updated[4][3],
        updated[0][4],
        updated[1][4],
        updated[2][4],
        updated[3][4],
        updated[4][4],
    )


BF = jnp.bfloat16
F32 = jnp.float32
AXES = ("dp", "fsdp")
VMEM_LIMIT = 60 * 1024 * 1024


def xperm(value, mask):
    count = lax.axis_size("dp") * lax.axis_size("fsdp")
    return lax.ppermute(value, AXES, [(i, i ^ mask) for i in range(count)])


def dot_nn(a, b):
    return jnp.dot(a, b, preferred_element_type=F32)


def dot_nt(a, b):
    return lax.dot_general(a, b, (((1,), (1,)), ((), ())), preferred_element_type=F32)


def dot_tn(a, b):
    return lax.dot_general(a, b, (((0,), (0,)), ((), ())), preferred_element_type=F32)


def split_columns(first, second):
    src = lax.broadcasted_iota(jnp.int32, (first, second), 0)
    col = lax.broadcasted_iota(jnp.int32, (1, second), 1)
    part = col // 256
    inner = col % 256
    half = inner // 128
    lane = inner % 128
    rotary = jnp.where(lane < 96, 192 * part + 64 * (lane // 32) + 32 * half + lane % 32, -1)
    plain = jnp.where(inner < 192, 384 + inner, -1)
    want = jnp.where(part < 2, rotary, plain)
    return (src == want).astype(F32).astype(BF)


def head_lanes(width, head):
    lane = lax.broadcasted_iota(jnp.int32, (1, width), 1) % 128
    return (lane >= 32 * head) & (lane < 32 * head + 32)


def value_lanes(width, head):
    lane = lax.broadcasted_iota(jnp.int32, (1, width), 1)
    return (lane >= 64 * head) & (lane < 64 * head + 64)


def prologue_kernel(
    ids, wq, w_out, w_in, w_down, gains, own, near, far, mine_in, other_in, mine_rest, other_rest
):
    f, core = ids[0], ids[2]
    row = lax.broadcasted_iota(jnp.int32, (24, 24), 0)
    col = lax.broadcasted_iota(jnp.int32, (24, 24), 1)
    parts = []
    for j in range(2):
        spread = jnp.where(row == col, gains[j : j + 1, :], 0.0)
        parts.append(jnp.sum(spread, axis=-1, keepdims=True))
    lane = lax.broadcasted_iota(jnp.int32, (24, 64), 1)
    columns = jnp.where(lane == 0, parts[0], jnp.where(lane == 1, parts[1], 0.0))
    blocks = []
    for j in range(4):
        pieces = [wq[:, 768 * part + 192 * j : 768 * part + 192 * j + 192] for part in range(3)]
        blocks.append(jnp.concatenate(pieces + [columns], axis=1))
    for k, out in enumerate((own, near, far.at[0], far.at[1])):
        place = f ^ k
        low = jnp.where(place == 0, blocks[0], blocks[1])
        high = jnp.where(place == 2, blocks[2], blocks[3])
        out[...] = jnp.where(place < 2, low, high).astype(BF)
    left, right = w_in[:, :1152], w_in[:, 1152:]
    mine_in[...] = jnp.where(core == 0, left, right).astype(BF)
    other_in[...] = jnp.where(core == 0, right, left).astype(BF)
    left = jnp.concatenate([w_out[:, :384], w_down[:, :640]], axis=1)
    right = jnp.concatenate([w_out[:, 384:], w_down[:, 640:], jnp.zeros((24, 128), F32)], axis=1)
    mine_rest[...] = jnp.where(core == 0, left, right).astype(BF)
    other_rest[...] = jnp.where(core == 0, right, left).astype(BF)


def assemble_kernel(ids, q0, q1, q2, q3, mine_rest, came_rest, mine_in, came_in, rows, rest, into):
    f, core = ids[0], ids[2]
    pieces = [q[...].astype(F32) for q in (q0, q1, q2, q3)]
    ordered = []
    for place in range(4):
        k = f ^ place
        low = jnp.where(k == 0, pieces[0], pieces[1])
        high = jnp.where(k == 2, pieces[2], pieces[3])
        ordered.append(jnp.where(k < 2, low, high))
    rows[...] = jnp.concatenate(ordered, axis=0).astype(BF)
    for mine, came, out in ((mine_rest, came_rest, rest), (mine_in, came_in, into)):
        one, two = mine[...].astype(F32), came[...].astype(F32)
        out[...] = jnp.concatenate(
            [jnp.where(core == 0, one, two), jnp.where(core == 0, two, one)], axis=0
        ).astype(BF)


def project_kernel(
    ids, t0, t1, t2, t3, cos, sin, w0, w1, w2, w3,
    n16, q8, key, val, gain, wide, wscr, sems,
):
    copies = []
    pieces = (w0, w1, w2.at[0], w3.at[0], w2.at[1], w3.at[1], w2.at[2], w3.at[2])
    for k, piece in enumerate(pieces):
        at = pl.multiple_of(96 * (ids[1] ^ k), 96)
        copies.append(pltpu.make_async_copy(piece, wscr.at[pl.ds(at, 96)], sems.at[k]))
        copies[-1].start()
    for copy in copies:
        copy.wait()
    weight = wscr[...]
    wide[...] = dot_nn(weight, split_columns(640, 768)).astype(BF)
    row = lax.broadcasted_iota(jnp.int32, (8, 640), 0)
    col = lax.broadcasted_iota(jnp.int32, (8, 640), 1)
    pick = ((col == row + 576) & (row < 2)).astype(F32).astype(BF)
    gain[...] = dot_nt(pick, weight)
    gain_row = gain[0:1, :]
    for i, piece in enumerate((t0, t1, t2, t3)):
        rows = slice(256 * i, 256 * i + 256)
        x = piece[...].astype(F32)
        center = x - jnp.mean(x, axis=-1, keepdims=True)
        inverse = lax.rsqrt(jnp.mean(center * center, axis=-1, keepdims=True) + NORM_EPS)
        normed = (center * inverse * gain_row).astype(BF)
        n16[rows, :] = normed
        mixed = dot_nn(normed, wide[...])
        c, s = cos[rows, :], sin[rows, :]
        qa, qb = mixed[:, :128], mixed[:, 128:256]
        ka, kb = mixed[:, 256:384], mixed[:, 384:512]
        q8[rows, :128] = ((qa * c - qb * s).astype(BF).astype(F32) * 0.125).astype(BF)
        q8[rows, 128:] = ((qb * c + qa * s).astype(BF).astype(F32) * 0.125).astype(BF)
        key[rows, :128] = (ka * c - kb * s).astype(BF)
        key[rows, 128:] = (kb * c + ka * s).astype(BF)
        val[rows, :] = mixed[:, 512:].astype(BF)


def attend_kernel(q8, key, val, docq, dock, att, low, prob):
    queries = q8[...]
    keys = key[...]
    values = val[...]
    same = docq[...] == dock[...]
    total = jnp.zeros((256, 256), F32)
    zero = jnp.zeros((), BF)
    for h in range(3):
        scores = dot_nt(jnp.where(head_lanes(256, h), queries, zero), keys)
        scores = jnp.where(same, scores, MASKED)
        peak = jnp.max(scores, axis=-1, keepdims=True)
        weights = jnp.exp(scores - peak)
        scale = 1.0 / jnp.sum(weights, axis=-1, keepdims=True)
        weights16 = (weights * scale).astype(BF)
        prob[h] = weights16
        total += dot_nn(weights16, jnp.where(value_lanes(256, h), values, zero))
    att[...] = total[:, :192]
    low[0] = total[:, :192].astype(BF)


def full(shape):
    return pl.BlockSpec(shape, lambda *_: (0,) * len(shape))


VM = pl.BlockSpec(memory_space=pltpu.VMEM)
SMEM = pl.BlockSpec(memory_space=pltpu.SMEM)
ANY = pl.BlockSpec(memory_space=pltpu.HBM)


def shaped(shape, dtype):
    return jax.ShapeDtypeStruct(shape, dtype)


def prologue(ids, weight_qkv, weight_out, weight_in, weight_down, norm_gains):
    return pl.pallas_call(
        prologue_kernel,
        in_specs=[SMEM] + [VM] * 5,
        out_specs=[VM] * 7,
        out_shape=[shaped((24, 640), BF)] * 2 + [shaped((2, 24, 640), BF)] + [shaped((24, 1152), BF)] * 2 + [shaped((24, 1024), BF)] * 2,
        compiler_params=pltpu.CompilerParams(vmem_limit_bytes=VMEM_LIMIT),
        cost_estimate=pl.CostEstimate(flops=10**6, bytes_accessed=10**6, transcendentals=0),
        name="prologue",
    )(ids, weight_qkv, weight_out, weight_in, weight_down, norm_gains)


def assemble(ids, *pieces):
    return pl.pallas_call(
        assemble_kernel,
        in_specs=[SMEM] + [VM] * 8,
        out_specs=[VM] * 3,
        out_shape=[shaped((96, 640), BF), shaped((48, 1024), BF), shaped((48, 1152), BF)],
        compiler_params=pltpu.CompilerParams(vmem_limit_bytes=VMEM_LIMIT),
        cost_estimate=pl.CostEstimate(flops=10**6, bytes_accessed=10**6, transcendentals=0),
        name="assemble",
    )(ids, *pieces)


def project(ids, token_pieces, cos, sin, w_pieces):
    return pl.pallas_call(
        project_kernel,
        in_specs=[SMEM] + [VM] * 6 + [ANY] * 4,
        out_specs=[VM] * 6,
        out_shape=[
            shaped((1024, 768), BF),
            shaped((1024, 256), BF),
            shaped((1024, 256), BF),
            shaped((1024, 256), BF),
            shaped((8, 768), F32),
            shaped((768, 768), BF),
        ],
        scratch_shapes=[pltpu.VMEM((768, 640), BF), pltpu.SemaphoreType.DMA((8,))],
        compiler_params=pltpu.CompilerParams(vmem_limit_bytes=VMEM_LIMIT),
        cost_estimate=pl.CostEstimate(flops=3 * 10**9, bytes_accessed=8 * 10**6, transcendentals=0),
        name="project",
    )(ids, *token_pieces, cos, sin, *w_pieces)


def attend(base, q8, key, val, docs):
    return pl.pallas_call(
        attend_kernel,
        grid=(2,),
        in_specs=[
            pl.BlockSpec((256, 256), lambda i: (base + i, 0)),
            full((1024, 256)),
            full((1024, 256)),
            pl.BlockSpec((256, 1), lambda i: (base + i, 0)),
            full((1, 1024)),
        ],
        out_specs=[
            pl.BlockSpec((256, 192), lambda i: (i, 0)),
            pl.BlockSpec((1, 256, 192), lambda i: (i, 0, 0)),
            pl.BlockSpec((3, 256, 1024), lambda i: (0, i, 0)),
        ],
        out_shape=[
            shaped((512, 192), F32),
            shaped((2, 256, 192), BF),
            shaped((3, 512, 1024), BF),
        ],
        compiler_params=pltpu.CompilerParams(vmem_limit_bytes=VMEM_LIMIT),
        cost_estimate=pl.CostEstimate(flops=3 * 10**9, bytes_accessed=8 * 10**6, transcendentals=2 * 10**6),
        name="attend",
    )(q8, key, val, docs[:, None], docs[None, :])


def erf_pair(x):
    cdf = 0.5 * (1.0 + lax.erf(x * (0.5**0.5)))
    density = jnp.exp(-0.5 * x * x) * (1.0 / (2.0 * 3.141592653589793) ** 0.5)
    return cdf, density


SLOTS = 10
PLACES = [(0, kz, kz * 4) for kz in range(4)]
PLACES += [(1, kz, kz * 4 + 1) for kz in range(4)]
PLACES += [(2, kz, kz * 4 + 2) for kz in range(4)]
PLACES += [(3, kz, kz * 4 + 3) for kz in range(2)]
PLACES += [(4, kz - 2, kz * 4 + 3) for kz in range(2, 4)]


def load_halves(held, target, core, chip, sems):
    copies = []
    for owner in range(2):
        half = core if owner == 0 else 1 - core
        for which, slot, mask in PLACES:
            at = pl.multiple_of(48 * (chip ^ mask), 48)
            copies.append(
                pltpu.make_async_copy(
                    held[owner * 5 + which].at[slot], target.at[half, pl.ds(at, 48)], sems.at[len(copies)]
                )
            )
            copies[-1].start()
    return copies


def feed_kernel(*refs):
    ids, tok, cot, live, gain, a0, a1, a2, a3 = refs[:9]
    held_rest, held_in = refs[9 : 9 + SLOTS], refs[9 + SLOTS : 9 + 2 * SLOTS]
    (block, dmid, d_near, d_far, act16, n2low, dgate, dbr, ggain, w_rest, w_in, sems) = refs[9 + 2 * SLOTS :]
    f, core, chip = ids[0], ids[2], ids[3]
    rest_copies = load_halves(held_rest, w_rest, core, chip, sems.at[0])
    in_copies = load_halves(held_in, w_in, core, chip, sems.at[1])
    tok_f = tok[...].astype(F32)
    pieces = [a[...] for a in (a0, a1, a2, a3)]
    heads = [pl.ds(pl.multiple_of(192 * (f ^ k), 192), 192) for k in range(4)]
    for copy in rest_copies:
        copy.wait()
    left = jnp.zeros((256, 384), F32)
    right = jnp.zeros((256, 384), F32)
    for k in range(4):
        left += dot_nn(pieces[k], w_rest[0, heads[k], :384])
        right += dot_nn(pieces[k], w_rest[1, heads[k], :384])
    middle = tok_f + jnp.concatenate([left, right], axis=1)
    center = middle - jnp.mean(middle, axis=-1, keepdims=True)
    inverse = lax.rsqrt(jnp.mean(center * center, axis=-1, keepdims=True) + NORM_EPS)
    normed = center * inverse
    gain_row = gain[1:2, :]
    low = (normed * gain_row).astype(BF)
    n2low[...] = low
    for copy in in_copies:
        copy.wait()
    act = dot_nn(low, w_in[0])
    gate = dot_nn(low, w_in[1])
    cdf, density = erf_pair(act)
    gelu = act * cdf
    active = (gelu * gate).astype(BF)
    act16[...] = active
    alive = live[...]
    dout = jnp.where(alive > 0.5, cot[...].astype(F32), 0.0)
    dym = dout.astype(BF)
    dact = jnp.concatenate([dot_nn(dym, w_rest[0, :, 384:1024]), dot_nn(dym, w_rest[1, :, 384:896])], axis=1)
    dg_front = (dact * gate * (cdf + act * density)).astype(BF)
    dg_rear = (dact * gelu).astype(BF)
    dgate[:, :1152] = dg_front
    dgate[:, 1152:] = dg_rear
    dnormed = dot_nt(dg_front, w_in[0]) + dot_nt(dg_rear, w_in[1])
    ggain[...] = jnp.broadcast_to(jnp.sum(dnormed * normed, axis=0, keepdims=True), (8, 768))
    up = dnormed * gain_row
    dmiddle = dout + inverse * (
        up
        - jnp.mean(up, axis=-1, keepdims=True)
        - normed * jnp.mean(up * normed, axis=-1, keepdims=True)
    )
    dmid[...] = dmiddle
    dbranch = dmiddle.astype(BF)
    dbr[...] = dbranch
    for k in range(4):
        (d_near, d_far)[k // 2][k % 2] = (
            dot_nt(dbranch[:, :384], w_rest[0, heads[k], :384]) + dot_nt(dbranch[:, 384:], w_rest[1, heads[k], :384])
        ).astype(BF)
    branch = dot_nt(active[:, :640], w_rest[0, :, 384:1024]) + dot_nt(active[:, 640:], w_rest[1, :, 384:896])
    block[...] = jnp.where(alive > 0.5, middle + branch, 0.0).astype(BF)


def feed_forward(ids, tokens, cotangent, live, gain, att_pieces, held_rest, held_in):
    return pl.pallas_call(
        feed_kernel,
        in_specs=[SMEM] + [VM] * 8 + [ANY] * (2 * SLOTS),
        out_specs=[VM] * 9,
        out_shape=[
            shaped((256, 768), BF),
            shaped((256, 768), F32),
            shaped((2, 256, 192), BF),
            shaped((2, 256, 192), BF),
            shaped((256, 1152), BF),
            shaped((256, 768), BF),
            shaped((256, 2304), BF),
            shaped((256, 768), BF),
            shaped((8, 768), F32),
        ],
        scratch_shapes=[
            pltpu.VMEM((2, 768, 1024), BF),
            pltpu.VMEM((2, 768, 1152), BF),
            pltpu.SemaphoreType.DMA((2, 32)),
        ],
        compiler_params=pltpu.CompilerParams(vmem_limit_bytes=VMEM_LIMIT),
        cost_estimate=pl.CostEstimate(flops=5 * 10**9, bytes_accessed=12 * 10**6, transcendentals=10**6),
        name="feed_forward",
    )(ids, tokens, cotangent, live, gain, *att_pieces, *held_rest, *held_in)


def store_chunks(grads, far_sent, sent, far_kept, kept, core, chip, sems):
    copies = []
    for group in (3, 0, 1, 2):
        for kz in range(4):
            at = pl.multiple_of(48 * (chip ^ (kz * 4 + group)), 48)
            for half, far, near in ((1 - core, far_sent, sent), (core, far_kept, kept)):
                target = far.at[kz] if group == 3 else near.at[group * 4 + kz]
                copies.append(pltpu.make_async_copy(grads.at[half, pl.ds(at, 48)], target, sems.at[len(copies)]))
                copies[-1].start()
    for copy in copies:
        copy.wait()


def grad_in_kernel(ids, n2low, dgate, far_sent, sent, far_kept, kept, grads, sems):
    low = n2low[...]
    grads[0] = dot_tn(low, dgate[:, :1152]).astype(BF)
    grads[1] = dot_tn(low, dgate[:, 1152:]).astype(BF)
    store_chunks(grads, far_sent, sent, far_kept, kept, ids[2], ids[3], sems)


def grad_rest_kernel(
    ids, cot, live, act16, dbr, a0, a1, a2, a3, far_sent, sent, far_kept, kept, grads, sems
):
    f = ids[0]
    dym = jnp.where(live[...] > 0.5, cot[...].astype(F32), 0.0).astype(BF)
    gdown = dot_tn(dym, act16[...])
    grads[0, :, 384:1024] = gdown[:, :640].astype(BF)
    grads[1, :, 384:896] = gdown[:, 640:].astype(BF)
    grads[1, :, 896:1024] = jnp.zeros((768, 128), BF)
    branch = dbr[...]
    for k, piece in enumerate((a0, a1, a2, a3)):
        rows = pl.ds(pl.multiple_of(192 * (f ^ k), 192), 192)
        gout = dot_tn(piece[...], branch).astype(BF)
        grads[0, rows, :384] = gout[:, :384]
        grads[1, rows, :384] = gout[:, 384:]
    store_chunks(grads, far_sent, sent, far_kept, kept, ids[2], ids[3], sems)


def chunk_call(kernel, name, width, ids, *operands):
    return pl.pallas_call(
        kernel,
        in_specs=[SMEM] + [VM] * len(operands),
        out_specs=[ANY] * 4,
        out_shape=[shaped((4, 48, width), BF), shaped((12, 48, width), BF)] * 2,
        scratch_shapes=[pltpu.VMEM((2, 768, width), BF), pltpu.SemaphoreType.DMA((32,))],
        compiler_params=pltpu.CompilerParams(vmem_limit_bytes=VMEM_LIMIT),
        cost_estimate=pl.CostEstimate(flops=15 * 10**8, bytes_accessed=8 * 10**6, transcendentals=0),
        name=name,
    )(ids, *operands)


def backward_kernel(*refs, resumed):
    cos, sin, q8, key, val, att, prob, first, second = refs[:9]
    refs = refs[9:]
    if resumed:
        dkt_in, dvt_in, refs = refs[0], refs[1], refs[2:]
    dq, dkt, dvt = refs
    step = pl.program_id(0)

    @pl.when(step == 0)
    def _():
        dkt[...] = dkt_in[...] if resumed else jnp.zeros((256, 1024), F32)
        dvt[...] = dvt_in[...] if resumed else jnp.zeros((256, 1024), F32)

    zero = jnp.zeros((), BF)
    keys = key[...]
    values = val[...]
    dattn = jnp.where(step == 0, first[...], second[...])
    dattn = jnp.concatenate([dattn, jnp.zeros((256, 64), BF)], axis=1)
    product = dattn[:, :192].astype(F32) * att[...]
    queries_t = q8[...].T
    dattn_t = dattn.T
    total = jnp.zeros((256, 256), F32)
    for h in range(3):
        weights = prob[h]
        dprob = dot_nt(jnp.where(value_lanes(256, h), dattn, zero), values)
        delta = jnp.sum(jnp.where(value_lanes(192, h), product, 0.0), axis=-1, keepdims=True)
        dscores = (weights.astype(F32) * (dprob - delta)).astype(BF)
        total += dot_nn(dscores, jnp.where(head_lanes(256, h), keys, zero))
        q_head = jnp.concatenate([queries_t[32 * h : 32 * h + 32], queries_t[128 + 32 * h : 160 + 32 * h]], axis=0)
        dk_head = dot_nn(q_head, dscores)
        dkt[32 * h : 32 * h + 32, :] += dk_head[:32]
        dkt[128 + 32 * h : 160 + 32 * h, :] += dk_head[32:]
        dvt[64 * h : 64 * h + 64, :] += dot_nn(dattn_t[64 * h : 64 * h + 64], weights)
    c, s = cos[...], sin[...]
    dqa, dqb = total[:, :128] * 0.125, total[:, 128:] * 0.125
    dq[:, :128] = (dqa * c + dqb * s).astype(BF)
    dq[:, 128:] = (dqb * c - dqa * s).astype(BF)


def backward(base, cos, sin, q8, key, val, att, prob, d_pieces, sums=()):
    return pl.pallas_call(
        functools.partial(backward_kernel, resumed=bool(sums)),
        grid=(2,),
        in_specs=[
            pl.BlockSpec((256, 128), lambda i: (base + i, 0)),
            pl.BlockSpec((256, 128), lambda i: (base + i, 0)),
            pl.BlockSpec((256, 256), lambda i: (base + i, 0)),
            full((1024, 256)),
            full((1024, 256)),
            pl.BlockSpec((256, 192), lambda i: (i, 0)),
            pl.BlockSpec((3, 256, 1024), lambda i: (0, i, 0)),
            full((256, 192)),
            full((256, 192)),
        ]
        + [full((256, 1024))] * len(sums),
        out_specs=[pl.BlockSpec((256, 256), lambda i: (i, 0)), full((256, 1024)), full((256, 1024))],
        out_shape=[shaped((512, 256), BF), shaped((256, 1024), F32), shaped((256, 1024), F32)],
        compiler_params=pltpu.CompilerParams(vmem_limit_bytes=VMEM_LIMIT),
        cost_estimate=pl.CostEstimate(flops=3 * 10**9, bytes_accessed=8 * 10**6, transcendentals=0),
        name="backward",
    )(cos, sin, q8, key, val, att, prob, *d_pieces, *sums)


def finish_kernel(
    ids, t0, t1, t2, t3, cos, sin, n16, dq_low, dq_high, dkt, dvt, wide, ggain,
    dn0, dn1, dn2, dn3, far, near, dmixed, grads, sems,
):
    dk = dkt[...].T
    c, s = cos[...], sin[...]
    dmixed[:512, :256] = dq_low[...]
    dmixed[512:, :256] = dq_high[...]
    dmixed[:, 256:384] = (dk[:, :128] * c + dk[:, 128:] * s).astype(BF)
    dmixed[:, 384:512] = (dk[:, 128:] * c - dk[:, :128] * s).astype(BF)
    dmixed[:, 512:768] = dvt[...].T.astype(BF)
    ggain1 = jnp.zeros((1, 768), F32)
    for i, (piece, out) in enumerate(((t0, dn0), (t1, dn1), (t2, dn2), (t3, dn3))):
        part = dot_nt(dmixed[256 * i : 256 * i + 256, :], wide[...])
        x = piece[...].astype(F32)
        center = x - jnp.mean(x, axis=-1, keepdims=True)
        inverse = lax.rsqrt(jnp.mean(center * center, axis=-1, keepdims=True) + NORM_EPS)
        ggain1 += jnp.sum(part * (center * inverse), axis=0, keepdims=True)
        out[...] = part.astype(BF)
    wide_grad = dot_tn(n16[...], dmixed[...]).astype(BF)
    natural = dot_nt(wide_grad, split_columns(640, 768))
    gains = jnp.concatenate([ggain1, ggain[0:1, :], jnp.zeros((126, 768), F32)], axis=0)
    column = jnp.concatenate([natural[:, :512], natural[:, 512:576], gains.T[:, :64]], axis=1)
    grads[...] = column.astype(BF)
    copies = []
    for ky, target in ((1, far), (0, near)):
        for kz in range(4):
            at = pl.multiple_of(96 * (ids[1] ^ (kz * 2 + ky)), 96)
            copies.append(pltpu.make_async_copy(grads.at[pl.ds(at, 96)], target.at[kz], sems.at[len(copies)]))
            copies[-1].start()
    for copy in copies:
        copy.wait()


def finish(ids, token_pieces, cos, sin, n16, dq_low, dq_high, dkt, dvt, wide, ggain):
    return pl.pallas_call(
        finish_kernel,
        in_specs=[SMEM] + [VM] * 13,
        out_specs=[VM] * 4 + [ANY, ANY],
        out_shape=[shaped((256, 768), BF)] * 4 + [shaped((4, 96, 640), BF)] * 2,
        scratch_shapes=[
            pltpu.VMEM((1024, 768), BF),
            pltpu.VMEM((768, 640), BF),
            pltpu.SemaphoreType.DMA((8,)),
        ],
        compiler_params=pltpu.CompilerParams(vmem_limit_bytes=VMEM_LIMIT),
        cost_estimate=pl.CostEstimate(flops=4 * 10**9, bytes_accessed=8 * 10**6, transcendentals=0),
        name="finish",
    )(ids, *token_pieces, cos, sin, n16, dq_low, dq_high, dkt, dvt, wide, ggain)


def pack_layout(count_row, length_row, slots, own_place):
    devices_here = count_row.shape[0]
    places = jnp.arange(devices_here * slots, dtype=jnp.int32)
    holder = (places // slots) ^ own_place
    within = places % slots
    before = jnp.cumsum(count_row) - count_row
    choose = (holder[:, None] == jnp.arange(devices_here, dtype=jnp.int32)[None, :]).astype(jnp.int32)
    offset = jnp.sum(choose * before[None, :], axis=1) + within
    limits = jnp.sum(choose * count_row[None, :], axis=1)
    living = within < limits
    doc_ends = jnp.cumsum(length_row)
    passed = offset[:, None] >= doc_ends[None, :]
    document = jnp.sum(passed.astype(jnp.int32), axis=1)
    begins = jnp.max(jnp.where(passed, doc_ends[None, :], 0), axis=1)
    document = jnp.where(living, document, length_row.shape[0])
    position = jnp.where(living, offset - begins, 0)
    return document, position, living


def by_place(pieces, low_bit, high_bit):
    a, b, c, d = pieces
    t0, t1 = jnp.where(low_bit, b, a), jnp.where(low_bit, a, b)
    t2, t3 = jnp.where(low_bit, d, c), jnp.where(low_bit, c, d)
    return [
        jnp.where(high_bit, t2, t0),
        jnp.where(high_bit, t3, t1),
        jnp.where(high_bit, t0, t2),
        jnp.where(high_bit, t1, t3),
    ]


def after(values, *signals):
    held = lax.optimization_barrier((tuple(values), signals))
    return list(held[0])


def fast_body(
    tokens, cotangent, counts, lengths,
    weight_qkv, weight_out, weight_in, weight_down, norm_gains,
    first_qkv, first_out, first_in, first_down, first_gains,
    second_qkv, second_out, second_in, second_down, second_gains,
    average_qkv, average_out, average_in, average_down, average_gains,
):
    slots = tokens.shape[0]
    group_row = lax.axis_index("dp")
    own_place = lax.axis_index("fsdp")
    core, side = own_place & 1, own_place >> 1
    chip = group_row * 2 + side
    ids = jnp.stack([own_place, group_row, core, chip]).astype(jnp.int32)

    def exchange(near, far):
        came = xperm(far, 2)
        return [xperm(near, 1), came[0], xperm(came[1], 1)]

    own, near, far, mine_in, other_in, mine_rest, other_rest = prologue(
        ids, weight_qkv, weight_out, weight_in, weight_down, norm_gains
    )
    tok_c = xperm(tokens, 1)

    def column_of(own):
        return jnp.stack([own, xperm(own, 8), xperm(own, 16), xperm(own, 24)])

    came_rest, came_in = xperm(other_rest, 1), xperm(other_in, 1)
    rows_here, own_rest, own_in = assemble(
        ids, own, *exchange(near, far), mine_rest, came_rest, mine_in, came_in
    )
    rows_z = jnp.stack([xperm(rows_here, 8), xperm(rows_here, 16), xperm(rows_here, 24)])
    w_pieces = [rows_here, xperm(rows_here, 4), rows_z, xperm(rows_z, 4)]
    (tokens_later,) = after([tokens], rows_here, tok_c)
    tok_x = xperm(tokens_later, 2)
    token_pieces = [tokens, tok_c, tok_x, xperm(tok_x, 1)]

    (own_rest,) = after([own_rest], rows_z, w_pieces[1])
    rest = column_of(own_rest)
    rest_x, rest_y = xperm(rest, 2), xperm(rest, 4)
    (own_in,) = after([own_in], rest, w_pieces[3])
    into = column_of(own_in)
    into_x, into_y = xperm(into, 2), xperm(into, 4)

    count_row = lax.dynamic_index_in_dim(counts, group_row, 0, keepdims=False)
    length_row = lax.dynamic_index_in_dim(lengths, group_row, 0, keepdims=False)
    count_row, length_row = after([count_row, length_row], rows_here)
    docs, position, living = pack_layout(count_row, length_row, slots, own_place)
    speeds = ROTARY_BASE ** (-(jnp.arange(HD // 2, dtype=F32) * (2.0 / HD)))
    angles = position.astype(F32)[:, None] * jnp.tile(speeds, 4)[None, :]
    cos, sin = jnp.cos(angles), jnp.sin(angles)
    live = living[:slots, None].astype(F32)

    (cos_ready,) = after([cos], rest)
    n16, q8, key, val, gain, wide = project(ids, token_pieces, cos_ready, sin, w_pieces)
    (q8_high,) = after([q8], into, rest_x, rest_y)
    att_high, far, prob_high = attend(2, q8_high, key, val, docs)
    (q8_low,) = after([q8], far, into_x, into_y)
    att_low, near, prob_low = attend(0, q8_low, key, val, docs)

    def relay(held, held_x, held_y, signal):
        held = [held, held_x, held_y]
        _, ready_x, ready_y = after(held, signal)
        return held + [xperm(ready_y[:2], 2), xperm(ready_x[2:], 4)]

    held_rest = relay(rest, rest_x, rest_y, far)
    far_came = xperm(far, 2)
    (near_last,) = after([near[1]], held_rest[3], held_rest[4], far_came)
    held_in = relay(into, into_x, into_y, near)
    att_pieces = [near[0], xperm(near_last, 1), far_came[0], xperm(far_came[1], 1)]
    held_rest += [xperm(piece, 1) for piece in held_rest]
    held_in += [xperm(piece, 1) for piece in held_in]
    block_out, dmiddle, d_near, d_far, act16, n2low, dgate, dbr, ggain = feed_forward(
        ids, tokens, cotangent, live, gain, att_pieces, held_rest, held_in
    )
    d_came = xperm(d_far, 2)
    d_pieces = [d_near[0], xperm(d_near[1], 1), d_came[0], xperm(d_came[1], 1)]

    def add(*parts):
        total = parts[0].astype(F32)
        for part in parts[1:]:
            total = total + part.astype(F32)
        return total.astype(BF)

    def reduce_begin(far_sent, sent, far_kept, kept, *signals):
        came, rest = xperm(far_sent, 1), xperm(sent, 1)
        far_kept, came = after([far_kept, came], *signals)
        for_y, for_x = add(far_kept[:2], came[:2]), add(far_kept[2:], came[2:])
        return xperm(for_y, 2), xperm(for_x, 4), kept, rest, for_y, for_x

    def reduce_middle(to_y, to_x, kept, rest, *signals):
        kept, to_x, to_y = after([kept, to_x, to_y], *signals)
        one = jnp.concatenate([add(kept[4:6], rest[4:6]), add(kept[6:8], rest[6:8], to_x)], axis=0)
        two = jnp.concatenate([add(kept[8:10], rest[8:10], to_y), add(kept[10:], rest[10:])], axis=0)
        return xperm(one, 2), xperm(two, 4)

    def reduce_column(one, two, kept, rest, *signals):
        kept, one = after([kept, one], *signals)
        pieces = [add(kept[kz], rest[kz], one[kz], two[kz]) for kz in range(4)]
        return [pieces[0]] + [xperm(pieces[kz], 8 * kz) for kz in (1, 2, 3)]

    def reduce_end(pieces):
        rows = add(*pieces)
        lower, upper = rows[:24], rows[24:]
        mine, other = jnp.where(core == 0, lower, upper), jnp.where(core == 0, upper, lower)
        came = xperm(other, 1)
        return (
            jnp.where(core == 0, mine, came).astype(F32),
            jnp.where(core == 0, came, mine).astype(F32),
        )

    chunks_in = chunk_call(grad_in_kernel, "grad_in", 1152, ids, n2low, dgate)
    *state_in, for_y, for_x = reduce_begin(*chunks_in)
    (cot_later,) = after([cotangent], for_y, for_x, d_came)
    chunks_rest = chunk_call(
        grad_rest_kernel, "grad_rest", 1024, ids, cot_later, live, act16, dbr, *att_pieces
    )
    one_in, two_in = reduce_middle(*state_in, chunks_rest[0])
    (key_low,) = after([key], d_pieces[2], d_pieces[3], state_in[0], state_in[1])
    dq_low, dkt, dvt = backward(0, cos, sin, q8, key_low, val, att_low, prob_low, d_pieces[:2])
    *state_rest, _, _ = reduce_begin(*chunks_rest, dq_low)
    (key_high,) = after([key], state_rest[3], one_in, two_in)
    dq_high, dkt, dvt = backward(2, cos, sin, q8, key_high, val, att_high, prob_high, d_pieces[2:], (dkt, dvt))
    one_rest, two_rest = reduce_middle(*state_rest, dq_high)
    column_in = reduce_column(one_in, two_in, *state_in[2:], dq_low)
    (dkt_ready,) = after([dkt], state_rest[0], state_rest[1], *column_in)
    dn0, dn1, dn2, dn3, far, near = finish(
        ids, token_pieces, cos, sin, n16, dq_low, dq_high, dkt_ready, dvt, wide, ggain
    )
    (far,) = after([far], one_rest, two_rest)
    (far_y,) = after([xperm(far, 4)], *column_in)
    column_rest = reduce_column(one_rest, two_rest, *state_rest[2:], near)
    half0, half1 = reduce_end(column_in)
    grad_in = jnp.concatenate([half0, half1], axis=1)
    half0, half1 = reduce_end(column_rest)
    grad_out = jnp.concatenate([half0[:, :384], half1[:, :384]], axis=1)
    grad_down = jnp.concatenate([half0[:, 384:], half1[:, 384:896]], axis=1)

    e = add(near, far_y)
    dp_rows = add(e[0], xperm(e[1], 8), xperm(e[2], 16), xperm(e[3], 24)).reshape(4, 24, 640)
    sends = [lax.dynamic_index_in_dim(dp_rows, own_place ^ k, 0, keepdims=False) for k in range(4)]
    came = [sends[0]] + exchange(sends[1], jnp.stack(sends[2:]))
    placed = jnp.stack(by_place([piece.astype(F32) for piece in came], core == 1, side == 1))
    grad_qkv = placed[:, :, :576].reshape(4, 24, 3, 192).transpose(1, 2, 0, 3).reshape(24, 2304)
    grad_gains = jnp.sum(placed[:, :, 576:578], axis=0).T

    own_sum, x_sum = add(dn0, xperm(dn1, 1)), add(dn2, xperm(dn3, 1))
    dnormed = own_sum.astype(F32) + xperm(x_sum, 2).astype(F32)
    normed, inverse = norm_parts(tokens.astype(F32))
    grad_tokens = dmiddle + norm_back(dnormed * gain[0:1, :], normed, inverse)

    masters = (weight_qkv, weight_out, weight_in, weight_down, norm_gains)
    firsts = (first_qkv, first_out, first_in, first_down, first_gains)
    seconds = (second_qkv, second_out, second_in, second_down, second_gains)
    averages = (average_qkv, average_out, average_in, average_down, average_gains)
    rates = (MATRIX_RATE, MATRIX_RATE, MATRIX_RATE, MATRIX_RATE, GAIN_RATE)
    grads = (grad_qkv, grad_out, grad_in, grad_down, grad_gains)
    updated = [
        adam_update(masters[i], firsts[i], seconds[i], averages[i], grads[i], rates[i]) for i in range(5)
    ]
    return (block_out, grad_tokens) + tuple(updated[i][j] for j in range(5) for i in range(5))


def solution(mesh):
    sizes = dict(mesh.shape)
    body = fast_body if sizes == {"dp": 8, "fsdp": 4} else general_body
    rows, columns = P(("dp", "fsdp"), None), P(None, ("dp", "fsdp"))
    weights = (rows,) * 4 + (columns,)
    return jax.shard_map(
        body,
        mesh=mesh,
        in_specs=(rows, rows, P(), P()) + weights * 4,
        out_specs=(rows, rows) + weights * 5,
        check_vma=False,
    )
```

```python
import functools

import jax
import jax.numpy as jnp
from jax import lax
from jax.experimental import pallas as pl
from jax.experimental.pallas import tpu as pltpu
from jax.sharding import PartitionSpec as P

HEADS = 12
HD = 64
STEP = 6


NORM_EPS = 1e-05
ROTARY_BASE = 160000.0
BETA_FIRST = 0.5
BETA_SECOND = 0.5
ADAM_EPS = 1e-08
WEIGHT_DECAY = 0.01
MATRIX_RATE = 0.04
GAIN_RATE = 0.5
AVERAGE_KEEP = 0.6
MASKED = -1e30


def group_layout(count_row, length_row, slots):
    devices_here = count_row.shape[0]
    places = jnp.arange(devices_here * slots, dtype=jnp.int32)
    holder = places // slots
    within = places - holder * slots
    before = jnp.cumsum(count_row) - count_row
    choose = (holder[:, None] == jnp.arange(devices_here, dtype=jnp.int32)[None, :]).astype(
        jnp.int32
    )
    offset = jnp.sum(choose * before[None, :], axis=1) + within
    limits = jnp.sum(choose * count_row[None, :], axis=1)
    living = within < limits
    doc_ends = jnp.cumsum(length_row)
    passed = offset[:, None] >= doc_ends[None, :]
    document = jnp.sum(passed.astype(jnp.int32), axis=1)
    begins = jnp.max(jnp.where(passed, doc_ends[None, :], 0), axis=1)
    number_docs = length_row.shape[0]
    document = jnp.where(living, document, number_docs)
    position = jnp.where(living, offset - begins, 0)
    return (document, position, living)


def rotary_tables(position, head_size):
    half_size = head_size // 2
    speeds = ROTARY_BASE ** (-(jnp.arange(half_size, dtype=jnp.float32) * (2.0 / head_size)))
    angles = position.astype(jnp.float32)[:, None] * speeds[None, :]
    return (jnp.cos(angles), jnp.sin(angles))


def rotate(heads_in, cosine_table, sine_table):
    half_size = heads_in.shape[-1] // 2
    leading = heads_in[..., :half_size]
    latter = heads_in[..., half_size:]
    cos_wide = cosine_table[:, None, :]
    sin_wide = sine_table[:, None, :]
    return jnp.concatenate(
        [leading * cos_wide - latter * sin_wide, latter * cos_wide + leading * sin_wide], axis=-1
    )


def rotate_back(grads_in, cosine_table, sine_table):
    half_size = grads_in.shape[-1] // 2
    leading = grads_in[..., :half_size]
    latter = grads_in[..., half_size:]
    cos_wide = cosine_table[:, None, :]
    sin_wide = sine_table[:, None, :]
    return jnp.concatenate(
        [leading * cos_wide + latter * sin_wide, latter * cos_wide - leading * sin_wide], axis=-1
    )


def norm_parts(values_in):
    center = values_in - jnp.mean(values_in, axis=-1, keepdims=True)
    inverse = lax.rsqrt(jnp.mean(center * center, axis=-1, keepdims=True) + NORM_EPS)
    return (center * inverse, inverse)


def norm_back(upstream, normed, inverse):
    return inverse * (
        upstream
        - jnp.mean(upstream, axis=-1, keepdims=True)
        - normed * jnp.mean(upstream * normed, axis=-1, keepdims=True)
    )


def block_scores(queries, key_block, doc_query, doc_key, score_scale):
    scores = (
        jnp.einsum("qhd,khd->hqk", queries, key_block, preferred_element_type=jnp.float32)
        * score_scale
    )
    return jnp.where(doc_query[None, :, None] == doc_key[None, None, :], scores, MASKED)


def contract_rows(left_side, right_side):
    return lax.dot_general(
        left_side, right_side, (((0,), (0,)), ((), ())), preferred_element_type=jnp.float32
    )


def contract_cols(left_side, right_side):
    return lax.dot_general(
        left_side, right_side, (((1,), (1,)), ((), ())), preferred_element_type=jnp.float32
    )


def adam_update(master, first_old, second_old, average_old, gradient, step_rate):
    first_new = BETA_FIRST * first_old + (1.0 - BETA_FIRST) * gradient
    second_new = BETA_SECOND * second_old + (1.0 - BETA_SECOND) * gradient * gradient
    first_fix = first_new / (1.0 - BETA_FIRST**STEP)
    second_fix = second_new / (1.0 - BETA_SECOND**STEP)
    master_new = master - step_rate * (
        first_fix / (jnp.sqrt(second_fix) + ADAM_EPS) + WEIGHT_DECAY * master
    )
    average_new = AVERAGE_KEEP * average_old + (1.0 - AVERAGE_KEEP) * master_new
    return (first_new, second_new, master_new, average_new, master_new.astype(jnp.bfloat16))


def general_body(
    tokens,
    cotangent,
    counts,
    lengths,
    weight_qkv,
    weight_out,
    weight_in,
    weight_down,
    norm_gains,
    first_qkv,
    first_out,
    first_in,
    first_down,
    first_gains,
    second_qkv,
    second_out,
    second_in,
    second_down,
    second_gains,
    average_qkv,
    average_out,
    average_in,
    average_down,
    average_gains,
):
    slots = tokens.shape[0]
    model_width = tokens.shape[1]
    hidden_units = weight_down.shape[1]
    head_count = HEADS
    head_size = HD
    score_scale = 1.0 / head_size**0.5
    heads_shape = (slots, head_count, head_size)
    group_row = lax.axis_index("dp")
    own_place = lax.axis_index("fsdp")
    count_row = lax.dynamic_index_in_dim(counts, group_row, 0, keepdims=False)
    length_row = lax.dynamic_index_in_dim(lengths, group_row, 0, keepdims=False)
    doc_all, position_all, living_all = group_layout(count_row, length_row, slots)
    doc_mine = lax.dynamic_slice_in_dim(doc_all, own_place * slots, slots)
    position_mine = lax.dynamic_slice_in_dim(position_all, own_place * slots, slots)
    living_mine = lax.dynamic_slice_in_dim(living_all, own_place * slots, slots)
    cosine_table, sine_table = rotary_tables(position_mine, head_size)
    living_col = living_mine[:, None]
    copies = (
        weight_qkv.astype(jnp.bfloat16),
        weight_out.astype(jnp.bfloat16),
        weight_in.astype(jnp.bfloat16),
        weight_down.astype(jnp.bfloat16),
        norm_gains.astype(jnp.bfloat16),
    )
    qkv_full, out_full, in_full, down_full, gain_full = (
        lax.all_gather(copies[0], ("dp", "fsdp"), axis=0, tiled=True),
        lax.all_gather(copies[1], ("dp", "fsdp"), axis=0, tiled=True),
        lax.all_gather(copies[2], ("dp", "fsdp"), axis=0, tiled=True),
        lax.all_gather(copies[3], ("dp", "fsdp"), axis=0, tiled=True),
        lax.all_gather(copies[4], ("dp", "fsdp"), axis=1, tiled=True),
    )
    tokens_f = tokens.astype(jnp.float32)
    normed_one, inverse_one = norm_parts(tokens_f)
    gain_one = gain_full[0].astype(jnp.float32)
    gain_two = gain_full[1].astype(jnp.float32)
    normed1_low = (normed_one * gain_one).astype(jnp.bfloat16)
    mixed_qkv = jnp.dot(normed1_low, qkv_full, preferred_element_type=jnp.float32)
    queries16 = rotate(
        mixed_qkv[:, :model_width].reshape(heads_shape), cosine_table, sine_table
    ).astype(jnp.bfloat16)
    keys16 = rotate(
        mixed_qkv[:, model_width : 2 * model_width].reshape(heads_shape), cosine_table, sine_table
    ).astype(jnp.bfloat16)
    key_flat = keys16.reshape(slots, model_width)
    value_flat = mixed_qkv[:, 2 * model_width :].astype(jnp.bfloat16)
    key_rows, value_rows = (
        lax.all_gather(key_flat, "fsdp", axis=0, tiled=True),
        lax.all_gather(value_flat, "fsdp", axis=0, tiled=True),
    )
    group_rows = key_rows.shape[0]
    block_rows = 512
    count_blocks = group_rows // block_rows
    blocks_shape = (count_blocks, block_rows, head_count, head_size)
    doc_blocks = doc_all.reshape(count_blocks, block_rows)
    key_blocks = key_rows.reshape(blocks_shape)
    value_blocks = value_rows.reshape(blocks_shape)

    def max_sum(state_now, pieces):
        run_peak, run_total = state_now
        scores = block_scores(queries16, pieces[0], doc_mine, pieces[1], score_scale)
        new_peak = jnp.maximum(run_peak, jnp.max(scores, axis=-1))
        run_total = run_total * jnp.exp(run_peak - new_peak) + jnp.sum(
            jnp.exp(scores - new_peak[:, :, None]), axis=-1
        )
        return ((new_peak, run_total), None)

    start_state = (
        jnp.full((head_count, slots), MASKED, jnp.float32),
        jnp.zeros((head_count, slots), jnp.float32),
    )
    (run_peak, run_total), unused_max = lax.scan(max_sum, start_state, (key_blocks, doc_blocks))
    log_total = run_peak + jnp.log(run_total)

    def weigh_values(accum, pieces):
        scores = block_scores(queries16, pieces[0], doc_mine, pieces[2], score_scale)
        probs16 = jnp.exp(scores - log_total[:, :, None]).astype(jnp.bfloat16)
        return (
            accum
            + jnp.einsum("hqk,khd->qhd", probs16, pieces[1], preferred_element_type=jnp.float32),
            None,
        )

    attended, unused_out = lax.scan(
        weigh_values, jnp.zeros(heads_shape, jnp.float32), (key_blocks, value_blocks, doc_blocks)
    )
    attended16 = attended.reshape(slots, model_width).astype(jnp.bfloat16)
    middle = tokens_f + jnp.dot(attended16, out_full, preferred_element_type=jnp.float32)
    normed_two, inverse_two = norm_parts(middle)
    normed2_low = (normed_two * gain_two).astype(jnp.bfloat16)
    gate_up = jnp.dot(normed2_low, in_full, preferred_element_type=jnp.float32)
    act_half = gate_up[:, :hidden_units]
    gate_half = gate_up[:, hidden_units:]
    activated16 = (jax.nn.gelu(act_half, approximate=False) * gate_half).astype(jnp.bfloat16)
    branch_two = contract_cols(activated16, down_full)
    block_out = jnp.where(living_col, middle + branch_two, 0.0).astype(jnp.bfloat16)
    qkv_back, out_back, in_back, down_back, gain_back = (
        lax.all_gather(copies[0], ("dp", "fsdp"), axis=0, tiled=True),
        lax.all_gather(copies[1], ("dp", "fsdp"), axis=0, tiled=True),
        lax.all_gather(copies[2], ("dp", "fsdp"), axis=0, tiled=True),
        lax.all_gather(copies[3], ("dp", "fsdp"), axis=0, tiled=True),
        lax.all_gather(copies[4], ("dp", "fsdp"), axis=1, tiled=True),
    )
    key_again, value_again = (
        lax.all_gather(key_flat, "fsdp", axis=0, tiled=True),
        lax.all_gather(value_flat, "fsdp", axis=0, tiled=True),
    )
    gain_one_back = gain_back[0].astype(jnp.float32)
    gain_two_back = gain_back[1].astype(jnp.float32)
    dout = jnp.where(living_col, cotangent.astype(jnp.float32), 0.0)
    dym16 = dout.astype(jnp.bfloat16)
    grad_down = contract_rows(dym16, activated16)
    dact = jnp.dot(dym16, down_back, preferred_element_type=jnp.float32)
    unused_gate, gate_pull = jax.vjp(
        lambda front_part, rear_part: jax.nn.gelu(front_part, approximate=False) * rear_part,
        act_half,
        gate_half,
    )
    dfront, drear = gate_pull(dact)
    dgate16 = jnp.concatenate([dfront, drear], axis=1).astype(jnp.bfloat16)
    grad_in = contract_rows(normed2_low, dgate16)
    dnormed_two = contract_cols(dgate16, in_back)
    grad_gain_two = jnp.sum(dnormed_two * normed_two, axis=0)
    dmiddle = dout + norm_back(dnormed_two * gain_two_back, normed_two, inverse_two)
    dbranch16 = dmiddle.astype(jnp.bfloat16)
    grad_out = contract_rows(attended16, dbranch16)
    dattn16 = contract_cols(dbranch16, out_back).astype(jnp.bfloat16).reshape(heads_shape)
    row_delta = jnp.sum(dattn16.astype(jnp.float32) * attended, axis=-1).T
    back_keys = key_again.reshape(blocks_shape)
    back_values = value_again.reshape(blocks_shape)

    def back_block(dquery_sum, pieces):
        key_block, value_block, doc_block = pieces
        scores = block_scores(queries16, key_block, doc_mine, doc_block, score_scale)
        probs = jnp.exp(scores - log_total[:, :, None])
        probs16 = probs.astype(jnp.bfloat16)
        dvalue_block = jnp.einsum(
            "hqk,qhd->khd", probs16, dattn16, preferred_element_type=jnp.float32
        )
        dprobs = jnp.einsum(
            "qhd,khd->hqk", dattn16, value_block, preferred_element_type=jnp.float32
        )
        dscores16 = (probs * (dprobs - row_delta[:, :, None])).astype(jnp.bfloat16)
        dquery_sum = dquery_sum + jnp.einsum(
            "hqk,khd->qhd", dscores16, key_block, preferred_element_type=jnp.float32
        )
        dkey_block = jnp.einsum(
            "hqk,qhd->khd", dscores16, queries16, preferred_element_type=jnp.float32
        )
        return (dquery_sum, (dkey_block, dvalue_block))

    dquery_sum, (dkey_blocks, dvalue_blocks) = lax.scan(
        back_block, jnp.zeros(heads_shape, jnp.float32), (back_keys, back_values, doc_blocks)
    )
    dkey_mine, dvalue_mine = (
        lax.psum_scatter(
            (dkey_blocks.reshape(group_rows, model_width) * score_scale).astype(jnp.bfloat16),
            "fsdp",
            scatter_dimension=0,
            tiled=True,
        ).astype(jnp.float32),
        lax.psum_scatter(
            dvalue_blocks.reshape(group_rows, model_width).astype(jnp.bfloat16),
            "fsdp",
            scatter_dimension=0,
            tiled=True,
        ).astype(jnp.float32),
    )
    dquery_pre = rotate_back(dquery_sum * score_scale, cosine_table, sine_table).reshape(
        slots, model_width
    )
    dkey_pre = rotate_back(dkey_mine.reshape(heads_shape), cosine_table, sine_table).reshape(
        slots, model_width
    )
    dmixed16 = jnp.concatenate([dquery_pre, dkey_pre, dvalue_mine], axis=1).astype(jnp.bfloat16)
    grad_qkv = contract_rows(normed1_low, dmixed16)
    dnormed_one = contract_cols(dmixed16, qkv_back)
    grad_gain_one = jnp.sum(dnormed_one * normed_one, axis=0)
    grad_tokens = dmiddle + norm_back(dnormed_one * gain_one_back, normed_one, inverse_one)
    grad_gains = jnp.stack([grad_gain_one, grad_gain_two], axis=0)
    reduced = (
        lax.psum_scatter(grad_qkv, ("dp", "fsdp"), scatter_dimension=0, tiled=True),
        lax.psum_scatter(grad_out, ("dp", "fsdp"), scatter_dimension=0, tiled=True),
        lax.psum_scatter(grad_in, ("dp", "fsdp"), scatter_dimension=0, tiled=True),
        lax.psum_scatter(grad_down, ("dp", "fsdp"), scatter_dimension=0, tiled=True),
        lax.psum_scatter(grad_gains, ("dp", "fsdp"), scatter_dimension=1, tiled=True),
    )
    masters = (weight_qkv, weight_out, weight_in, weight_down, norm_gains)
    firsts = (first_qkv, first_out, first_in, first_down, first_gains)
    seconds = (second_qkv, second_out, second_in, second_down, second_gains)
    averages = (average_qkv, average_out, average_in, average_down, average_gains)
    rates = (MATRIX_RATE, MATRIX_RATE, MATRIX_RATE, MATRIX_RATE, GAIN_RATE)
    updated = [
        adam_update(
            masters[which],
            firsts[which],
            seconds[which],
            averages[which],
            reduced[which],
            rates[which],
        )
        for which in range(5)
    ]
    return (
        block_out,
        grad_tokens,
        updated[0][0],
        updated[1][0],
        updated[2][0],
        updated[3][0],
        updated[4][0],
        updated[0][1],
        updated[1][1],
        updated[2][1],
        updated[3][1],
        updated[4][1],
        updated[0][2],
        updated[1][2],
        updated[2][2],
        updated[3][2],
        updated[4][2],
        updated[0][3],
        updated[1][3],
        updated[2][3],
        updated[3][3],
        updated[4][3],
        updated[0][4],
        updated[1][4],
        updated[2][4],
        updated[3][4],
        updated[4][4],
    )


FL = {'C2': 1, 'GO': 2, 'H1': 3, 'H2': 2, 'H3': 1, 'H5': 1, 'H7': 2, 'H8': 1, 'T3': 4, 'T4': 3, 'T5': 3, 'T6': 1, 'TA': 3, 'TC': 1}
BF = jnp.bfloat16
F32 = jnp.float32
AXES = ("dp", "fsdp")
VMEM_LIMIT = 60 * 1024 * 1024


def xperm(value, mask):
    count = lax.axis_size("dp") * lax.axis_size("fsdp")
    return lax.ppermute(value, AXES, [(i, i ^ mask) for i in range(count)])


def dot_nn(a, b):
    return jnp.dot(a, b, preferred_element_type=F32)


def dot_nt(a, b):
    return lax.dot_general(a, b, (((1,), (1,)), ((), ())), preferred_element_type=F32)


def dot_tn(a, b):
    return lax.dot_general(a, b, (((0,), (0,)), ((), ())), preferred_element_type=F32)


def spread_columns(weight):
    rows = weight.shape[0]
    gap, end = jnp.zeros((rows, 32), weight.dtype), jnp.zeros((rows, 64), weight.dtype)
    parts = []
    for i in range(4):
        parts += [weight[:, 96 * i : 96 * i + 96], gap]
    return jnp.concatenate(parts + [weight[:, 384:576], end], axis=1)


def pack_columns(spread, last):
    return jnp.concatenate([spread[:, 128 * i : 128 * i + 96] for i in range(4)] + [spread[:, 512:704], last], axis=1)


def pack_heads(block):
    return jnp.concatenate([block[64 * i : 64 * i + 64] for i in range(4)], axis=1)


def unpack_heads(packed):
    return jnp.concatenate([packed[:, 192 * i : 192 * i + 192] for i in range(4)], axis=0)


def head_lanes(width, head):
    lane = lax.broadcasted_iota(jnp.int32, (1, width), 1) % 128
    return (lane >= 32 * head) & (lane < 32 * head + 32)


def value_lanes(width, head):
    lane = lax.broadcasted_iota(jnp.int32, (1, width), 1)
    return (lane >= 64 * head) & (lane < 64 * head + 64)


def prologue_kernel(ids, wq, w_out, w_in, w_down, gains, near, far, mine, other):
    f, core = ids[0], ids[2]
    row = lax.broadcasted_iota(jnp.int32, (24, 24), 0)
    col = lax.broadcasted_iota(jnp.int32, (24, 24), 1)
    parts = []
    for j in range(2):
        spread = jnp.where(row == col, gains[j : j + 1, :], 0.0)
        parts.append(jnp.sum(spread, axis=-1, keepdims=True))
    lane = lax.broadcasted_iota(jnp.int32, (24, 64), 1)
    columns = jnp.where(lane == 0, parts[0], jnp.where(lane == 1, parts[1], 0.0))
    blocks = []
    for j in range(4):
        pieces = []
        for part in range(2):
            heads = wq[:, 768 * part + 192 * j : 768 * part + 192 * j + 192]
            pieces += [heads[:, 64 * h + 32 * half : 64 * h + 32 * half + 32] for half in range(2) for h in range(3)]
        blocks.append(jnp.concatenate(pieces + [wq[:, 1536 + 192 * j : 1728 + 192 * j], columns], axis=1))
    for k, out in enumerate((near.at[0], near.at[1], far.at[0], far.at[1])):
        place = f ^ k
        low = jnp.where(place == 0, blocks[0], blocks[1])
        high = jnp.where(place == 2, blocks[2], blocks[3])
        out[...] = jnp.where(place < 2, low, high).astype(BF)
    left = jnp.concatenate([w_in[:, :1152], w_out[:, :384], w_down[:, :640]], axis=1)
    right = jnp.concatenate([w_in[:, 1152:], w_out[:, 384:], w_down[:, 640:], jnp.zeros((24, 128), F32)], axis=1)
    mine[...] = jnp.where(core == 0, left, right).astype(BF)
    other[...] = jnp.where(core == 0, right, left).astype(BF)


def assemble_kernel(ids, q0, q1, q2, q3, mine, came, rows, other):
    f, core = ids[0], ids[2]
    pieces = [q[i].astype(F32) for q, i in ((q0, 0), (q1, 1), (q2, 0), (q3, 1))]
    ordered = []
    for place in range(4):
        k = f ^ place
        low = jnp.where(k == 0, pieces[0], pieces[1])
        high = jnp.where(k == 2, pieces[2], pieces[3])
        ordered.append(jnp.where(k < 2, low, high))
    rows[...] = jnp.concatenate(ordered, axis=0).astype(BF)
    one, two = mine[...].astype(F32), came[...].astype(F32)
    other[...] = jnp.concatenate([jnp.where(core == 0, one, two), jnp.where(core == 0, two, one)], axis=0).astype(BF)


def forward_kernel(
    ids, t0, t1, t2, t3, cos, sin, docq, dock, w0, w1, w2, w3,
    q8, key, val, att, near, far, prob, gain, wide, wscr, sems,
):
    step = pl.program_id(0)

    @pl.when(step == 0)
    def _():
        copies = []
        pieces = (w0, w1, w2.at[0], w3.at[0], w2.at[1], w3.at[1], w2.at[2], w3.at[2])
        for k, piece in enumerate(pieces):
            at = pl.multiple_of(96 * (ids[1] ^ k), 96)
            copies.append(pltpu.make_async_copy(piece, wscr.at[pl.ds(at, 96)], sems.at[k]))
            copies[-1].start()
        for copy in copies:
            copy.wait()
        weight = wscr[...]
        wide[...] = spread_columns(weight)
        row = lax.broadcasted_iota(jnp.int32, (8, 640), 0)
        col = lax.broadcasted_iota(jnp.int32, (8, 640), 1)
        pick = ((col == row + 576) & (row < 2)).astype(F32).astype(BF)
        gain[...] = dot_nt(pick, weight)
        gain_row = gain[0:1, :]
        for i, piece in enumerate((t0, t1, t2, t3)):
            rows = slice(256 * i, 256 * i + 256)
            x = piece[...].astype(F32)
            center = x - jnp.mean(x, axis=-1, keepdims=True)
            inverse = lax.rsqrt(jnp.mean(center * center, axis=-1, keepdims=True) + NORM_EPS)
            mixed = dot_nn((center * inverse * gain_row).astype(BF), wide[...])
            c, s = cos[rows, :], sin[rows, :]
            qa, qb = mixed[:, :128], mixed[:, 128:256]
            ka, kb = mixed[:, 256:384], mixed[:, 384:512]
            q8[rows, :128] = ((qa * c - qb * s).astype(BF).astype(F32) * 0.125).astype(BF)
            q8[rows, 128:] = ((qb * c + qa * s).astype(BF).astype(F32) * 0.125).astype(BF)
            key[rows, :128] = (ka * c - kb * s).astype(BF)
            key[rows, 128:] = (kb * c + ka * s).astype(BF)
            val[rows, :] = mixed[:, 512:].astype(BF)

    rows = pl.ds(pl.multiple_of(step * 256, 256), 256)
    queries = q8[rows, :]
    keys = key[...]
    values = val[...]
    same = docq[rows, :] == dock[...]
    total = jnp.zeros((256, 256), F32)
    zero = jnp.zeros((), BF)
    for h in range(3):
        scores = dot_nt(jnp.where(head_lanes(256, h), queries, zero), keys)
        scores = jnp.where(same, scores, MASKED)
        peak = jnp.max(scores, axis=-1, keepdims=True)
        weights = jnp.exp(scores - peak)
        scale = 1.0 / jnp.sum(weights, axis=-1, keepdims=True)
        weights16 = (weights * scale).astype(BF)
        prob[h] = weights16
        total += dot_nn(weights16, jnp.where(value_lanes(256, h), values, zero))
    att[...] = total[:, :192]
    low = total[:, :192].astype(BF)

    @pl.when(step < 2)
    def _():
        near[0] = pack_heads(low)

    @pl.when(step >= 2)
    def _():
        far[0] = pack_heads(low)


def project_kernel(ids, t0, t1, t2, t3, cos, sin, w0, w1, w2, w3, q8, key, val, gain, wide, wscr, sems):
    copies = []
    pieces = (w0, w1, w2.at[0], w3.at[0], w2.at[1], w3.at[1], w2.at[2], w3.at[2])
    for k, piece in enumerate(pieces):
        at = pl.multiple_of(96 * (ids[1] ^ k), 96)
        copies.append(pltpu.make_async_copy(piece, wscr.at[pl.ds(at, 96)], sems.at[k]))
        copies[-1].start()
    for copy in copies:
        copy.wait()
    weight = wscr[...]
    wide[...] = spread_columns(weight)
    row = lax.broadcasted_iota(jnp.int32, (8, 640), 0)
    col = lax.broadcasted_iota(jnp.int32, (8, 640), 1)
    pick = ((col == row + 576) & (row < 2)).astype(F32).astype(BF)
    gain[...] = dot_nt(pick, weight)
    gain_row = gain[0:1, :]
    for i, piece in enumerate((t0, t1, t2, t3)):
        rows = slice(256 * i, 256 * i + 256)
        x = piece[...].astype(F32)
        center = x - jnp.mean(x, axis=-1, keepdims=True)
        inverse = lax.rsqrt(jnp.mean(center * center, axis=-1, keepdims=True) + NORM_EPS)
        mixed = dot_nn((center * inverse * gain_row).astype(BF), wide[...])
        c, s = cos[rows, :], sin[rows, :]
        qa, qb = mixed[:, :128], mixed[:, 128:256]
        ka, kb = mixed[:, 256:384], mixed[:, 384:512]
        q8[rows, :128] = ((qa * c - qb * s).astype(BF).astype(F32) * 0.125).astype(BF)
        q8[rows, 128:] = ((qb * c + qa * s).astype(BF).astype(F32) * 0.125).astype(BF)
        key[rows, :128] = (ka * c - kb * s).astype(BF)
        key[rows, 128:] = (kb * c + ka * s).astype(BF)
        val[rows, :] = mixed[:, 512:].astype(BF)


def attend_kernel(q8, key, val, docq, dock, att, near, far, prob):
    step = pl.program_id(0)
    rows = pl.ds(pl.multiple_of(step * 256, 256), 256)
    queries = q8[rows, :]
    keys = key[...]
    values = val[...]
    same = docq[rows, :] == dock[...]
    total = jnp.zeros((256, 256), F32)
    zero = jnp.zeros((), BF)
    for h in range(3):
        scores = dot_nt(jnp.where(head_lanes(256, h), queries, zero), keys)
        scores = jnp.where(same, scores, MASKED)
        peak = jnp.max(scores, axis=-1, keepdims=True)
        weights = jnp.exp(scores - peak)
        scale = 1.0 / jnp.sum(weights, axis=-1, keepdims=True)
        weights16 = (weights * scale).astype(BF)
        prob[h] = weights16
        total += dot_nn(weights16, jnp.where(value_lanes(256, h), values, zero))
    att[...] = total[:, :192]
    low = total[:, :192].astype(BF)

    @pl.when(step < 2)
    def _():
        near[0] = pack_heads(low)

    @pl.when(step >= 2)
    def _():
        far[0] = pack_heads(low)


def full(shape):
    return pl.BlockSpec(shape, lambda *_: (0,) * len(shape))


VM = pl.BlockSpec(memory_space=pltpu.VMEM)
SMEM = pl.BlockSpec(memory_space=pltpu.SMEM)
ANY = pl.BlockSpec(memory_space=pltpu.HBM)


def shaped(shape, dtype):
    return jax.ShapeDtypeStruct(shape, dtype)


def prologue(ids, weight_qkv, weight_out, weight_in, weight_down, norm_gains):
    return pl.pallas_call(
        prologue_kernel,
        in_specs=[SMEM] + [VM] * 5,
        out_specs=[VM] * 4,
        out_shape=[shaped((2, 24, 640), BF)] * 2 + [shaped((24, 2176), BF)] * 2,
        compiler_params=pltpu.CompilerParams(vmem_limit_bytes=VMEM_LIMIT),
        cost_estimate=pl.CostEstimate(flops=10**6, bytes_accessed=10**6, transcendentals=0),
        name="prologue",
    )(ids, weight_qkv, weight_out, weight_in, weight_down, norm_gains)


def assemble(ids, *pieces):
    return pl.pallas_call(
        assemble_kernel,
        in_specs=[SMEM] + [VM] * 6,
        out_specs=[VM] * 2,
        out_shape=[shaped((96, 640), BF), shaped((48, 2176), BF)],
        compiler_params=pltpu.CompilerParams(vmem_limit_bytes=VMEM_LIMIT),
        cost_estimate=pl.CostEstimate(flops=10**6, bytes_accessed=10**6, transcendentals=0),
        name="assemble",
    )(ids, *pieces)


def forward_attention(ids, token_pieces, cos, sin, docs, w_pieces):
    return pl.pallas_call(
        forward_kernel,
        grid=(4,),
        in_specs=[SMEM]
        + [full((256, 768))] * 4
        + [full((1024, 128))] * 2
        + [full((1024, 1)), full((1, 1024))]
        + [ANY] * 4,
        out_specs=[
            full((1024, 256)),
            full((1024, 256)),
            full((1024, 256)),
            pl.BlockSpec((256, 192), lambda i: (i, 0)),
            pl.BlockSpec((1, 64, 768), lambda i: (jnp.minimum(i, 1), 0, 0)),
            pl.BlockSpec((1, 64, 768), lambda i: (jnp.maximum(i - 2, 0), 0, 0)),
            pl.BlockSpec((3, 256, 1024), lambda i: (0, i, 0)),
            full((8, 768)),
            full((768, 768)),
        ],
        out_shape=[
            shaped((1024, 256), BF),
            shaped((1024, 256), BF),
            shaped((1024, 256), BF),
            shaped((1024, 192), F32),
            shaped((2, 64, 768), BF),
            shaped((2, 64, 768), BF),
            shaped((3, 1024, 1024), BF),
            shaped((8, 768), F32),
            shaped((768, 768), BF),
        ],
        scratch_shapes=[pltpu.VMEM((768, 640), BF), pltpu.SemaphoreType.DMA((8,))],
        compiler_params=pltpu.CompilerParams(vmem_limit_bytes=VMEM_LIMIT),
        cost_estimate=pl.CostEstimate(flops=6 * 10**9, bytes_accessed=16 * 10**6, transcendentals=3 * 10**6),
        name="forward_attention",
    )(ids, *token_pieces, cos, sin, docs[:, None], docs[None, :], *w_pieces)


def project(ids, token_pieces, cos, sin, w_pieces):
    return pl.pallas_call(
        project_kernel,
        in_specs=[SMEM] + [VM] * 6 + [ANY] * 4,
        out_specs=[VM] * 5,
        out_shape=[
            shaped((1024, 256), BF),
            shaped((1024, 256), BF),
            shaped((1024, 256), BF),
            shaped((8, 768), F32),
            shaped((768, 768), BF),
        ],
        scratch_shapes=[pltpu.VMEM((768, 640), BF), pltpu.SemaphoreType.DMA((8,))],
        compiler_params=pltpu.CompilerParams(vmem_limit_bytes=VMEM_LIMIT),
        cost_estimate=pl.CostEstimate(flops=3 * 10**9, bytes_accessed=8 * 10**6, transcendentals=0),
        name="project",
    )(ids, *token_pieces, cos, sin, *w_pieces)


def attend(q8, key, val, docs):
    return pl.pallas_call(
        attend_kernel,
        grid=(4,),
        in_specs=[full((1024, 256))] * 3 + [full((1024, 1)), full((1, 1024))],
        out_specs=[
            pl.BlockSpec((256, 192), lambda i: (i, 0)),
            pl.BlockSpec((1, 64, 768), lambda i: (jnp.minimum(i, 1), 0, 0)),
            pl.BlockSpec((1, 64, 768), lambda i: (jnp.maximum(i - 2, 0), 0, 0)),
            pl.BlockSpec((3, 256, 1024), lambda i: (0, i, 0)),
        ],
        out_shape=[
            shaped((1024, 192), F32),
            shaped((2, 64, 768), BF),
            shaped((2, 64, 768), BF),
            shaped((3, 1024, 1024), BF),
        ],
        compiler_params=pltpu.CompilerParams(vmem_limit_bytes=VMEM_LIMIT),
        cost_estimate=pl.CostEstimate(flops=3 * 10**9, bytes_accessed=8 * 10**6, transcendentals=3 * 10**6),
        name="attend",
    )(q8, key, val, docs[:, None], docs[None, :])


def erf_pair(x):
    cdf = 0.5 * (1.0 + lax.erf(x * (0.5**0.5)))
    density = jnp.exp(-0.5 * x * x) * (1.0 / (2.0 * 3.141592653589793) ** 0.5)
    return cdf, density


def load_halves(held, w_in, w_rest, core, chip, sems):
    groups = [[], []]
    for owner in range(2):
        half = core if owner == 0 else 1 - core
        arrays = held[owner * 5 : owner * 5 + 5]
        for group in range(4):
            for kz in range(4):
                rows = pl.ds(pl.multiple_of(48 * (chip ^ (kz * 4 + group)), 48), 48)
                if group < 3:
                    in_parts = [(arrays[group].at[kz, :, pl.ds(0, 1152)], w_in.at[half, rows])]
                    rest_part = arrays[group].at[kz, :, pl.ds(1152, 1024)]
                else:
                    in_parts = [
                        (arrays[3].at[pl.ds(48 * kz, 48)], w_in.at[half, rows, pl.ds(0, 768)]),
                        (arrays[4].at[kz, :, pl.ds(0, 384)], w_in.at[half, rows, pl.ds(768, 384)]),
                    ]
                    rest_part = arrays[4].at[kz, :, pl.ds(384, 1024)]
                for which, parts in ((0, in_parts), (1, [(rest_part, w_rest.at[half, rows])])):
                    for source, target in parts:
                        sem = sems.at[which, len(groups[which])]
                        groups[which].append(pltpu.make_async_copy(source, target, sem))
    for copy in groups[1] + groups[0]:
        copy.start()
    return groups


def feed_kernel(*refs):
    ids, tok, cot, live, gain, a0, a1, a2, a3 = refs[:9]
    held = refs[9:-12]
    (block, dmid, d_near, d_far, act16, n2low, dgate, dbr, ggain, w_rest, w_in, sems) = refs[-12:]
    f, core, chip = ids[0], ids[2], ids[3]
    in_copies, rest_copies = load_halves(held, w_in, w_rest, core, chip, sems)
    tok_f = tok[...].astype(F32)
    pieces = [unpack_heads(a) for a in (a0[0], a1[1], a2[192:256, :], a3[256:320, :])]
    heads = [pl.ds(pl.multiple_of(192 * (f ^ k), 192), 192) for k in range(4)]
    for copy in rest_copies:
        copy.wait()
    left = jnp.zeros((256, 384), F32)
    right = jnp.zeros((256, 384), F32)
    for k in range(4):
        left += dot_nn(pieces[k], w_rest[0, heads[k], :384])
        right += dot_nn(pieces[k], w_rest[1, heads[k], :384])
    middle = tok_f + jnp.concatenate([left, right], axis=1)
    center = middle - jnp.mean(middle, axis=-1, keepdims=True)
    inverse = lax.rsqrt(jnp.mean(center * center, axis=-1, keepdims=True) + NORM_EPS)
    normed = center * inverse
    gain_row = gain[1:2, :]
    low = (normed * gain_row).astype(BF)
    n2low[...] = low
    for copy in in_copies:
        copy.wait()
    act = dot_nn(low, w_in[0])
    gate = dot_nn(low, w_in[1])
    cdf, density = erf_pair(act)
    gelu = act * cdf
    active = (gelu * gate).astype(BF)
    act16[...] = active
    alive = live[...]
    dout = jnp.where(alive > 0.5, cot[...].astype(F32), 0.0)
    dym = dout.astype(BF)
    dact = jnp.concatenate([dot_nn(dym, w_rest[0, :, 384:1024]), dot_nn(dym, w_rest[1, :, 384:896])], axis=1)
    dg_front = (dact * gate * (cdf + act * density)).astype(BF)
    dg_rear = (dact * gelu).astype(BF)
    dgate[:, :1152] = dg_front
    dgate[:, 1152:] = dg_rear
    dnormed = dot_nt(dg_front, w_in[0]) + dot_nt(dg_rear, w_in[1])
    ggain[...] = jnp.broadcast_to(jnp.sum(dnormed * normed, axis=0, keepdims=True), (8, 768))
    up = dnormed * gain_row
    dmiddle = dout + inverse * (
        up
        - jnp.mean(up, axis=-1, keepdims=True)
        - normed * jnp.mean(up * normed, axis=-1, keepdims=True)
    )
    dmid[...] = dmiddle
    dbranch = dmiddle.astype(BF)
    dbr[...] = dbranch
    for k in range(4):
        (d_near, d_far)[k // 2][k % 2] = pack_heads(
            (
                dot_nt(dbranch[:, :384], w_rest[0, heads[k], :384])
                + dot_nt(dbranch[:, 384:], w_rest[1, heads[k], :384])
            ).astype(BF)
        )
    branch = dot_nt(active[:, :640], w_rest[0, :, 384:1024]) + dot_nt(active[:, 640:], w_rest[1, :, 384:896])
    block[...] = jnp.where(alive > 0.5, middle + branch, 0.0).astype(BF)


def feed_forward(ids, tokens, cotangent, live, gain, att_pieces, held):
    return pl.pallas_call(
        feed_kernel,
        in_specs=[SMEM] + [VM] * 8 + [ANY] * len(held),
        out_specs=[VM] * 9,
        out_shape=[
            shaped((256, 768), BF),
            shaped((256, 768), F32),
            shaped((2, 64, 768), BF),
            shaped((2, 64, 768), BF),
            shaped((256, 1152), BF),
            shaped((256, 768), BF),
            shaped((256, 2304), BF),
            shaped((256, 768), BF),
            shaped((8, 768), F32),
        ],
        scratch_shapes=[
            pltpu.VMEM((2, 768, 1024), BF),
            pltpu.VMEM((2, 768, 1152), BF),
            pltpu.SemaphoreType.DMA((2, 40)),
        ],
        compiler_params=pltpu.CompilerParams(vmem_limit_bytes=VMEM_LIMIT),
        cost_estimate=pl.CostEstimate(flops=5 * 10**9, bytes_accessed=12 * 10**6, transcendentals=10**6),
        name="feed_forward",
    )(ids, tokens, cotangent, live, gain, *att_pieces, *held)


def store_chunks(grads, sent, kept, order, core, chip, sems, what="both"):
    copies = []
    for slot, group in enumerate(order):
        for kz in range(4):
            at = pl.multiple_of(48 * (chip ^ (kz * 4 + group)), 48)
            for half, target in ((1 - core, sent), (core, kept)):
                copies.append(
                    pltpu.make_async_copy(
                        grads.at[half, pl.ds(at, 48)], target.at[slot * 4 + kz], sems.at[len(copies)]
                    )
                )
                if what != "wait":
                    copies[-1].start()
    if what != "start":
        for copy in copies:
            copy.wait()


def grad_in_kernel(ids, n2low, dgate, sent, kept, grads, sems, wait=True):
    low = n2low[...]
    grads[0] = dot_tn(low, dgate[:, :1152]).astype(BF)
    grads[1] = dot_tn(low, dgate[:, 1152:]).astype(BF)
    store_chunks(grads, sent, kept, (3, 1, 2, 0), ids[2], ids[3], sems, "both" if wait else "start")


def grad_rest_kernel(ids, cot, live, act16, dbr, a0, a1, a2, a3, sent, kept, grads, sems, wait=True):
    f = ids[0]
    dym = jnp.where(live[...] > 0.5, cot[...].astype(F32), 0.0).astype(BF)
    gdown = dot_tn(dym, act16[...])
    grads[0, :, 384:1024] = gdown[:, :640].astype(BF)
    grads[1, :, 384:896] = gdown[:, 640:].astype(BF)
    grads[1, :, 896:1024] = jnp.zeros((768, 128), BF)
    branch = dbr[...]
    for k, piece in enumerate((a0[0], a1[1], a2[192:256, :], a3[256:320, :])):
        piece = unpack_heads(piece)
        rows = pl.ds(pl.multiple_of(192 * (f ^ k), 192), 192)
        gout = dot_tn(piece, branch).astype(BF)
        grads[0, rows, :384] = gout[:, :384]
        grads[1, rows, :384] = gout[:, 384:]
    store_chunks(grads, sent, kept, (3, 2, 1, 0), ids[2], ids[3], sems, "both" if wait else "start")


def grads_kernel(
    ids, cot, live, act16, dbr, a0, a1, a2, a3, n2low, dgate, sent_in, kept_in, sent_rest, kept_rest, g_in, g_rest, sems
):
    grad_in_kernel(ids, n2low, dgate, sent_in, kept_in, g_in, sems.at[0], False)
    grad_rest_kernel(ids, cot, live, act16, dbr, a0, a1, a2, a3, sent_rest, kept_rest, g_rest, sems.at[1], False)
    store_chunks(g_in, sent_in, kept_in, (3, 1, 2, 0), ids[2], ids[3], sems.at[0], "wait")
    store_chunks(g_rest, sent_rest, kept_rest, (3, 2, 1, 0), ids[2], ids[3], sems.at[1], "wait")


def feed_gradients(ids, *operands):
    return pl.pallas_call(
        grads_kernel,
        in_specs=[SMEM] + [VM] * len(operands),
        out_specs=[ANY] * 4,
        out_shape=[shaped((16, 48, width), BF) for width in (1152, 1152, 1024, 1024)],
        scratch_shapes=[
            pltpu.VMEM((2, 768, 1152), BF),
            pltpu.VMEM((2, 768, 1024), BF),
            pltpu.SemaphoreType.DMA((2, 32)),
        ],
        compiler_params=pltpu.CompilerParams(vmem_limit_bytes=VMEM_LIMIT),
        cost_estimate=pl.CostEstimate(flops=3 * 10**9, bytes_accessed=16 * 10**6, transcendentals=0),
        name="grads",
    )(ids, *operands)


def chunk_call(kernel, name, width, ids, *operands):
    return pl.pallas_call(
        kernel,
        in_specs=[SMEM] + [VM] * len(operands),
        out_specs=[ANY] * 2,
        out_shape=[shaped((16, 48, width), BF)] * 2,
        scratch_shapes=[pltpu.VMEM((2, 768, width), BF), pltpu.SemaphoreType.DMA((32,))],
        compiler_params=pltpu.CompilerParams(vmem_limit_bytes=VMEM_LIMIT),
        cost_estimate=pl.CostEstimate(flops=15 * 10**8, bytes_accessed=8 * 10**6, transcendentals=0),
        name=name,
    )(ids, *operands)


def backward_kernel(*refs, base, blocks):
    resumed, last = base > 0, base + blocks == 4
    ids, t0, t1, t2, t3, cos, sin, q8, key, val, att, prob, d0, d1, gain, wide, ggain = refs[:17]
    refs = refs[17:]
    if blocks == 4:
        d2, d3, refs = refs[0], refs[1], refs[2:]
    if resumed:
        dq_in, dkt_in, dvt_in, refs = refs[0], refs[1], refs[2], refs[3:]
    if last:
        dn0, dn1, dn2, dn3, far, near, dq, dkt, dvt, n16, grads, sems = refs
    else:
        dq, dkt, dvt = refs
    step = pl.program_id(0)

    @pl.when(step == 0)
    def _():
        if resumed:
            dkt[...] = dkt_in[...]
            dvt[...] = dvt_in[...]
            dq[:512, :256] = dq_in[...]
        else:
            dkt[...] = jnp.zeros((256, 1024), F32)
            dvt[...] = jnp.zeros((256, 1024), F32)

    rows = pl.ds(pl.multiple_of((base + step) * 256, 256), 256)
    zero = jnp.zeros((), BF)
    keys = key[...]
    values = val[...]
    dattn = unpack_heads(d0[0])
    others = ((1, d1[1]),) if blocks == 2 else ((1, d1[1]), (2, d2[0]), (3, d3[1]))
    for i, piece in others:
        dattn = jnp.where(step == i, unpack_heads(piece), dattn)
    dattn = jnp.concatenate([dattn, jnp.zeros((256, 64), BF)], axis=1)
    product = dattn[:, :192].astype(F32) * att[...]
    queries_t = q8[rows, :].T
    dattn_t = dattn.T
    total = jnp.zeros((256, 256), F32)
    for h in range(3):
        weights = prob[h]
        dprob = dot_nt(jnp.where(value_lanes(256, h), dattn, zero), values)
        delta = jnp.sum(jnp.where(value_lanes(192, h), product, 0.0), axis=-1, keepdims=True)
        dscores = (weights.astype(F32) * (dprob - delta)).astype(BF)
        total += dot_nn(dscores, jnp.where(head_lanes(256, h), keys, zero))
        q_head = jnp.concatenate([queries_t[32 * h : 32 * h + 32], queries_t[128 + 32 * h : 160 + 32 * h]], axis=0)
        dk_head = dot_nn(q_head, dscores)
        dkt[32 * h : 32 * h + 32, :] += dk_head[:32]
        dkt[128 + 32 * h : 160 + 32 * h, :] += dk_head[32:]
        dvt[64 * h : 64 * h + 64, :] += dot_nn(dattn_t[64 * h : 64 * h + 64], weights)
    c, s = cos[rows, :], sin[rows, :]
    dqa, dqb = total[:, :128] * 0.125, total[:, 128:] * 0.125
    dq[rows, :128] = (dqa * c + dqb * s).astype(BF)
    dq[rows, 128:256] = (dqb * c - dqa * s).astype(BF)

    if not last:
        return

    @pl.when(step == blocks - 1)
    def _():
        dk = dkt[...].T
        ca, sa = cos[...], sin[...]
        dq[:, 256:384] = (dk[:, :128] * ca + dk[:, 128:] * sa).astype(BF)
        dq[:, 384:512] = (dk[:, 128:] * ca - dk[:, :128] * sa).astype(BF)
        dq[:, 512:768] = dvt[...].T.astype(BF)
        ggain1 = jnp.zeros((1, 768), F32)
        gain_row = gain[0:1, :]
        for i, (piece, out) in enumerate(((t0, dn0), (t1, dn1), (t2, dn2), (t3, dn3))):
            part = dot_nt(dq[256 * i : 256 * i + 256, :], wide[...])
            x = piece[...].astype(F32)
            center = x - jnp.mean(x, axis=-1, keepdims=True)
            inverse = lax.rsqrt(jnp.mean(center * center, axis=-1, keepdims=True) + NORM_EPS)
            normed = center * inverse
            n16[256 * i : 256 * i + 256, :] = (normed * gain_row).astype(BF)
            ggain1 += jnp.sum(part * normed, axis=0, keepdims=True)
            out[...] = part.astype(BF)
        gains = jnp.concatenate([ggain1, ggain[0:1, :], jnp.zeros((126, 768), F32)], axis=0)
        grads[...] = pack_columns(dot_tn(n16[...], dq[...]), gains.T[:, :64]).astype(BF)
        copies = []
        for ky, target in ((1, far), (0, near)):
            for kz in range(4):
                at = pl.multiple_of(96 * (ids[1] ^ (kz * 2 + ky)), 96)
                copies.append(
                    pltpu.make_async_copy(grads.at[pl.ds(at, 96)], target.at[kz], sems.at[len(copies)])
                )
                copies[-1].start()
        for copy in copies:
            copy.wait()


def backward_attention(
    ids, token_pieces, cos, sin, q8, key, val, att, prob, d_pieces, gain, wide, ggain, base=0, blocks=4, sums=()
):
    last = base + blocks == 4
    if last:
        out_specs = [full((256, 768))] * 4 + [ANY, ANY]
        out_shape = [shaped((256, 768), BF)] * 4 + [shaped((4, 96, 640), BF)] * 2
        scratch = [
            pltpu.VMEM((1024, 768), BF),
            pltpu.VMEM((256, 1024), F32),
            pltpu.VMEM((256, 1024), F32),
            pltpu.VMEM((1024, 768), BF),
            pltpu.VMEM((768, 640), BF),
            pltpu.SemaphoreType.DMA((8,)),
        ]
    else:
        out_specs = [full((512, 256)), full((256, 1024)), full((256, 1024))]
        out_shape = [shaped((512, 256), BF), shaped((256, 1024), F32), shaped((256, 1024), F32)]
        scratch = []
    sum_specs = [full((512, 256)), full((256, 1024)), full((256, 1024))] if sums else []
    return pl.pallas_call(
        functools.partial(backward_kernel, base=base, blocks=blocks),
        grid=(blocks,),
        in_specs=[SMEM]
        + [full((256, 768))] * 4
        + [full((1024, 128))] * 2
        + [full((1024, 256))] * 3
        + [pl.BlockSpec((256, 192), lambda i: (base + i, 0))]
        + [pl.BlockSpec((3, 256, 1024), lambda i: (0, base + i, 0))]
        + [full((2, 64, 768))] * 2
        + [full((8, 768)), full((768, 768)), full((8, 768))]
        + [full((2, 64, 768))] * (len(d_pieces) - 2)
        + sum_specs,
        out_specs=out_specs,
        out_shape=out_shape,
        scratch_shapes=scratch,
        compiler_params=pltpu.CompilerParams(vmem_limit_bytes=VMEM_LIMIT),
        cost_estimate=pl.CostEstimate(flops=2 * blocks * 10**9, bytes_accessed=16 * 10**6, transcendentals=0),
        name="backward_attention",
    )(ids, *token_pieces, cos, sin, q8, key, val, att, prob, *d_pieces[:2], gain, wide, ggain, *d_pieces[2:], *sums)


def sum_heads_kernel(ids, e0, e1, e2, e3, near, far):
    f = ids[0]
    total = e0[...].astype(F32) + e1[...].astype(F32) + e2[...].astype(F32) + e3[...].astype(F32)
    pieces = [total[24 * j : 24 * j + 24, :] for j in range(4)]
    for k, out in enumerate((near.at[0], near.at[1], far.at[0], far.at[1])):
        place = f ^ k
        low = jnp.where(place == 0, pieces[0], pieces[1])
        high = jnp.where(place == 2, pieces[2], pieces[3])
        out[...] = jnp.where(place < 2, low, high).astype(BF)


def sum_heads(ids, *pieces):
    return pl.pallas_call(
        sum_heads_kernel,
        in_specs=[SMEM] + [VM] * 4,
        out_specs=[VM] * 2,
        out_shape=[shaped((2, 24, 640), BF)] * 2,
        compiler_params=pltpu.CompilerParams(vmem_limit_bytes=VMEM_LIMIT),
        cost_estimate=pl.CostEstimate(flops=10**6, bytes_accessed=10**6, transcendentals=0),
        name="sum_heads",
    )(ids, *pieces)


def sum_rows_kernel(ids, a0, a1, a2, a3, b0, b1, b2, b3, mine, other):
    core = ids[2]
    one = a0[...].astype(F32) + a1[...].astype(F32) + a2[...].astype(F32) + a3[...].astype(F32)
    two = b0[...].astype(F32) + b1[...].astype(F32) + b2[...].astype(F32) + b3[...].astype(F32)
    rows = jnp.concatenate([one, two], axis=1)
    mine[...] = jnp.where(core == 0, rows[:24], rows[24:]).astype(BF)
    other[...] = jnp.where(core == 0, rows[24:], rows[:24]).astype(BF)


def sum_rows(ids, *pieces):
    return pl.pallas_call(
        sum_rows_kernel,
        in_specs=[SMEM] + [VM] * 8,
        out_specs=[VM] * 2,
        out_shape=[shaped((24, 2176), BF)] * 2,
        compiler_params=pltpu.CompilerParams(vmem_limit_bytes=VMEM_LIMIT),
        cost_estimate=pl.CostEstimate(flops=10**6, bytes_accessed=10**6, transcendentals=0),
        name="sum_rows",
    )(ids, *pieces)


def store_update(gradient, state, outs, rate):
    master, first, second, average = [ref[...] for ref in state]
    for out, value in zip(outs, adam_update(master, first, second, average, gradient, rate)):
        out[...] = value


def update_rows_kernel(ids, mine, came, *refs):
    core = ids[2]
    one, two = mine[...].astype(F32), came[...].astype(F32)
    left, right = jnp.where(core == 0, one, two), jnp.where(core == 0, two, one)
    grads = (
        jnp.concatenate([left[:, :1152], right[:, :1152]], axis=1),
        jnp.concatenate([left[:, 1152:1536], right[:, 1152:1536]], axis=1),
        jnp.concatenate([left[:, 1536:2176], right[:, 1536:2048]], axis=1),
    )
    for i, gradient in enumerate(grads):
        store_update(gradient, refs[4 * i : 4 * i + 4], refs[12 + 5 * i : 17 + 5 * i], MATRIX_RATE)


def update_rows(ids, mine, came, states):
    return pl.pallas_call(
        update_rows_kernel,
        in_specs=[SMEM] + [VM] * 14,
        out_specs=[VM] * 15,
        out_shape=[shaped((24, width), dtype) for width in (2304, 768, 1152) for dtype in (F32,) * 4 + (BF,)],
        compiler_params=pltpu.CompilerParams(vmem_limit_bytes=VMEM_LIMIT),
        cost_estimate=pl.CostEstimate(flops=10**7, bytes_accessed=4 * 10**6, transcendentals=10**5),
        name="update_rows",
    )(ids, mine, came, *[array for state in states for array in state])


def update_heads_kernel(ids, c0, c1, c2, c3, *refs):
    f = ids[0]
    pieces = [c[i].astype(F32) for c, i in ((c0, 0), (c1, 1), (c2, 0), (c3, 1))]
    ordered = []
    for place in range(4):
        k = f ^ place
        low = jnp.where(k == 0, pieces[0], pieces[1])
        high = jnp.where(k == 2, pieces[2], pieces[3])
        ordered.append(jnp.where(k < 2, low, high))
    parts = []
    for part in range(2):
        for piece in ordered:
            for h in range(3):
                parts += [piece[:, 192 * part + 96 * half + 32 * h : 192 * part + 96 * half + 32 * h + 32] for half in range(2)]
    gradient = jnp.concatenate(parts + [piece[:, 384:576] for piece in ordered], axis=1)
    store_update(gradient, refs[:4], refs[8:13], MATRIX_RATE)
    columns = sum(piece[:, 512:640] for piece in pieces)
    row = lax.broadcasted_iota(jnp.int32, (24, 24), 0)
    col = lax.broadcasted_iota(jnp.int32, (24, 24), 1)
    lines = [
        jnp.sum(jnp.where(row == col, columns[:, 64 + i : 65 + i], 0.0), axis=0, keepdims=True) for i in range(2)
    ]
    store_update(jnp.concatenate(lines, axis=0), refs[4:8], refs[13:18], GAIN_RATE)


def update_heads(ids, came, state, gain_state):
    return pl.pallas_call(
        update_heads_kernel,
        in_specs=[SMEM] + [VM] * 12,
        out_specs=[VM] * 10,
        out_shape=[shaped((24, 2304), dtype) for dtype in (F32,) * 4 + (BF,)]
        + [shaped((2, 24), dtype) for dtype in (F32,) * 4 + (BF,)],
        compiler_params=pltpu.CompilerParams(vmem_limit_bytes=VMEM_LIMIT),
        cost_estimate=pl.CostEstimate(flops=10**7, bytes_accessed=3 * 10**6, transcendentals=10**5),
        name="update_heads",
    )(ids, *came, *state, *gain_state)


def pack_layout(count_row, length_row, slots, own_place):
    devices_here = count_row.shape[0]
    places = jnp.arange(devices_here * slots, dtype=jnp.int32)
    holder = (places // slots) ^ own_place
    within = places % slots
    before = jnp.cumsum(count_row) - count_row
    choose = (holder[:, None] == jnp.arange(devices_here, dtype=jnp.int32)[None, :]).astype(jnp.int32)
    offset = jnp.sum(choose * before[None, :], axis=1) + within
    limits = jnp.sum(choose * count_row[None, :], axis=1)
    living = within < limits
    doc_ends = jnp.cumsum(length_row)
    passed = offset[:, None] >= doc_ends[None, :]
    document = jnp.sum(passed.astype(jnp.int32), axis=1)
    begins = jnp.max(jnp.where(passed, doc_ends[None, :], 0), axis=1)
    document = jnp.where(living, document, length_row.shape[0])
    position = jnp.where(living, offset - begins, 0)
    return document, position, living


def after(values, *signals):
    held = lax.optimization_barrier((tuple(values), signals))
    return list(held[0])


def fast_body(
    tokens, cotangent, counts, lengths,
    weight_qkv, weight_out, weight_in, weight_down, norm_gains,
    first_qkv, first_out, first_in, first_down, first_gains,
    second_qkv, second_out, second_in, second_down, second_gains,
    average_qkv, average_out, average_in, average_down, average_gains,
):
    slots = tokens.shape[0]
    group_row = lax.axis_index("dp")
    own_place = lax.axis_index("fsdp")
    core, side = own_place & 1, own_place >> 1
    chip = group_row * 2 + side
    ids = jnp.stack([own_place, group_row, core, chip]).astype(jnp.int32)

    def flag(name):
        return FL.get(name, 0)

    def exchange(near, far, direct=False):
        if direct:
            return [near, xperm(near, 1), xperm(far, 2), xperm(far, 3)]
        came = xperm(far, 2)
        return [near, xperm(near, 1), came, xperm(came, 1)]

    def pick(name, values, *signals):
        k = flag(name)
        if k == 0:
            return list(values)
        chosen = signals[k - 1]
        return after(values, *chosen)

    near, far, mine, other = prologue(ids, weight_qkv, weight_out, weight_in, weight_down, norm_gains)
    tok_c = xperm(tokens, 1)
    rows_here, own_rows = assemble(ids, *exchange(near, far, flag("QX")), mine, xperm(other, 1))
    rows_z = [xperm(rows_here, 8), xperm(rows_here, 16), xperm(rows_here, 24)]
    rows_y = xperm(rows_here, 4)
    rows_z = jnp.stack(rows_z)
    rows_zy = xperm(rows_z, 4)
    w_pieces = [rows_here, rows_y, rows_z, rows_zy]
    (tokens_later,) = pick("H5", [tokens], (rows_here, tok_c), (rows_z,), (rows_y,))
    tok_x = xperm(tokens_later, 2)
    token_pieces = [tokens, tok_c, tok_x, xperm(tok_x, 1)]

    column0 = own_rows
    (own_rows,) = pick("H1", [own_rows], (rows_z, rows_y), (rows_z,), (rows_y,), (rows_zy,))
    column = [own_rows, xperm(own_rows, 8), xperm(own_rows, 16), xperm(own_rows, 24)]
    held = jnp.stack(column)

    count_row = lax.dynamic_index_in_dim(counts, group_row, 0, keepdims=False)
    length_row = lax.dynamic_index_in_dim(lengths, group_row, 0, keepdims=False)
    count_row, length_row = pick("H2", [count_row, length_row], (rows_here,), (rows_z,), (rows_zy,))
    docs, position, living = pack_layout(count_row, length_row, slots, own_place)
    speeds = ROTARY_BASE ** (-(jnp.arange(HD // 2, dtype=F32) * (2.0 / HD)))
    angles = position.astype(F32)[:, None] * jnp.tile(speeds, 4)[None, :]
    cos, sin = jnp.cos(angles), jnp.sin(angles)
    live = living[:slots, None].astype(F32)

    if flag("FS"):
        held_x, held_y = xperm(held, 2), xperm(held, 4)
        (cos_ready,) = pick("H3", [cos], (held,), (column[-1],))
        q8, key, val, gain, wide = project(ids, token_pieces, cos_ready, sin, w_pieces)
        (q8_ready,) = pick("H8", [q8], (held,), (column[0],), (column[0], column[1]))
        att, near, far, prob = attend(q8_ready, key, val, docs)
    else:
        held_x, held_y = xperm(held, 2), xperm(held, 4)
        (cos_ready,) = pick("H3", [cos], (held,), (column[-1],))
        q8, key, val, att, near, far, prob, gain, wide = forward_attention(
            ids, token_pieces, cos_ready, sin, docs, w_pieces
        )
    ready_x, ready_y = pick("H4", [held_x, held_y], (q8,), (near,))
    by_x = jnp.concatenate([ready_y[:, :, :768].reshape(192, 768), far.reshape(128, 768)], axis=0)
    (from_x,) = pick("H6", [ready_x], (near,), (by_x,))
    by_x, by_y = xperm(by_x, 2), xperm(from_x[:, :, 768:], 4)
    held = [held, held_x, held_y]
    held = pick("H7", held, (q8,), (near,), (by_x,))
    (near,) = pick("H9", [near], (by_x,), (by_y,))
    if flag("HC") == 1:
        pair = xperm(jnp.concatenate(held[1:], axis=0), 1)
        held_c = [xperm(held[0], 1), pair[:4], pair[4:]]
    elif flag("HC") == 2:
        trio = xperm(jnp.concatenate(held, axis=0), 1)
        held_c = [trio[:4], trio[4:8], trio[8:]]
    else:
        held_c = [xperm(piece, 1) for piece in held]
    by_x_c, by_y_c = xperm(by_x, 1), xperm(by_y, 1)
    att_pieces = [near, xperm(near, 1), by_x, by_x_c]
    held = held + [by_x, by_y] + held_c + [by_x_c, by_y_c]
    block_out, dmiddle, d_near, d_far, act16, n2low, dgate, dbr, ggain = feed_forward(
        ids, tokens, cotangent, live, gain, att_pieces, held
    )
    d_pieces = exchange(d_near, d_far, flag("DX"))

    def add(*parts):
        total = parts[0].astype(F32)
        for part in parts[1:]:
            total = total + part.astype(F32)
        return total.astype(BF)

    def reduce_column(kept, rest, one, two):
        pieces = [add(kept[12 + kz], rest[12 + kz], one[kz], two[kz]) for kz in range(4)]
        if flag("ZM"):
            return pieces
        return [pieces[0]] + [xperm(pieces[kz], 8 * kz) for kz in (1, 2, 3)]

    if flag("GO") == 2:
        sent_in, kept_in, sent_rest, kept_rest = feed_gradients(
            ids, cotangent, live, act16, dbr, *att_pieces, n2low, dgate
        )
    elif flag("GO"):
        sent_rest, kept_rest = chunk_call(
            grad_rest_kernel, "grad_rest", 1024, ids, cotangent, live, act16, dbr, *att_pieces
        )
        (n2_later,) = pick("T1", [n2low], (sent_rest,), (sent_rest, d_pieces[2]), (d_pieces[2],))
        sent_in, kept_in = chunk_call(grad_in_kernel, "grad_in", 1152, ids, n2_later, dgate)
    else:
        sent_in, kept_in = chunk_call(grad_in_kernel, "grad_in", 1152, ids, n2low, dgate)
        (cot_later,) = pick("T1", [cotangent], (sent_in,), (sent_in, d_pieces[2]), (d_pieces[2],))
        sent_rest, kept_rest = chunk_call(
            grad_rest_kernel, "grad_rest", 1024, ids, cot_later, live, act16, dbr, *att_pieces
        )
    if flag("C1") and flag("GO") == 1:
        (sent_rest,) = after([sent_rest], sent_in)
    elif flag("C1") and flag("GO") == 0:
        (sent_in,) = after([sent_in], sent_rest)
    (sent_in,) = pick("C2", [sent_in], (d_pieces[2],), (d_pieces[3],))
    (sent_rest,) = pick("C3", [sent_rest], (d_pieces[2],), (d_pieces[3],))
    came_in, came_rest = xperm(sent_in, 1), xperm(sent_rest, 1)

    def begin(name, kept, came):
        kept, came = pick(name, [kept, came], tuple(signals)) if signals else (kept, came)
        return xperm(add(kept[:2], came[:2]), 2), xperm(add(kept[2:4], came[2:4]), 4)

    def middle(name, to_y, to_x, kx, rx, ky, ry, *marks):
        kx, ky = pick(name, [kx, ky], *[(mark,) for mark in marks])
        one = jnp.concatenate([add(kx[:2], rx[:2]), add(kx[2:], rx[2:], to_x)], axis=0)
        two = jnp.concatenate([add(ky[:2], ry[:2], to_y), add(ky[2:], ry[2:])], axis=0)
        return xperm(one, 2), xperm(two, 4)

    signals = []
    if flag("RV"):
        to_in = begin("V1", kept_in[:4], came_in[:4])
        early_rest = flag("V2") == 0
        if early_rest:
            to_rest = begin("V0", kept_rest[:4], came_rest[:4])
        marks = [to_in[0], to_in[1]]
        (key_later,) = pick("V3", [key], (to_in[0],), (kept_in, came_in), (kept_rest, came_rest))
        if flag("V4") == 0:
            one_in, two_in = middle("V5", *to_in, kept_in[4:8], came_in[4:8], kept_in[8:12], came_in[8:12], to_in[0])
        if flag("BS"):
            sums = backward_attention(
                ids, token_pieces, cos, sin, q8, key_later, val, att, prob, d_pieces[:2], gain, wide, ggain, 0, 2
            )
            signals = [sums[0]]
            if flag("V4") == 1:
                one_in, two_in = middle(
                    "V5", *to_in, kept_in[4:8], came_in[4:8], kept_in[8:12], came_in[8:12], sums[0]
                )
            if not early_rest:
                to_rest = begin("V6", kept_rest[:4], came_rest[:4])
            if flag("V7"):
                one_rest, two_rest = middle(
                    "V8", *to_rest, kept_rest[8:12], came_rest[8:12], kept_rest[4:8], came_rest[4:8], sums[0]
                )
            (key_last,) = pick("V9", [key], (to_in[0], to_in[1]), (one_in, two_in), (to_rest[0], to_rest[1]))
            dn0, dn1, dn2, dn3, far, near = backward_attention(
                ids, token_pieces, cos, sin, q8, key_last, val, att, prob, d_pieces[2:], gain, wide, ggain, 2, 2, sums
            )
        else:
            dn0, dn1, dn2, dn3, far, near = backward_attention(
                ids, token_pieces, cos, sin, q8, key_later, val, att, prob, d_pieces, gain, wide, ggain
            )
            if flag("V4") == 1:
                one_in, two_in = middle(
                    "V5", *to_in, kept_in[4:8], came_in[4:8], kept_in[8:12], came_in[8:12], near
                )
            signals = [near]
            if not early_rest:
                to_rest = begin("V6", kept_rest[:4], came_rest[:4])
        if not (flag("BS") and flag("V7")):
            one_rest, two_rest = middle(
                "V8", *to_rest, kept_rest[8:12], came_rest[8:12], kept_rest[4:8], came_rest[4:8], near
            )
        (far,) = pick("VA", [far], (one_in, two_in), (one_rest, two_rest), (to_rest[0],))
        far_y = xperm(far, 4)
        along_x, along_y, then_y, then_x = one_in, two_rest, two_in, one_rest
        column_in = reduce_column(kept_in, came_in, one_in, two_in)
        column_rest = reduce_column(kept_rest, came_rest, one_rest, two_rest)
    else:
        lead_in = add(kept_in[:8], came_in[:8])
        lead_rest = add(kept_rest[:8], came_rest[:8])
        along_x, along_y = xperm(lead_in, 2), xperm(lead_rest, 4)
        (key_later,) = pick("T3", [key], (lead_in, lead_rest), (lead_in,), (lead_rest,), (d_pieces[2], d_pieces[3]))
        if flag("BS"):
            sums = backward_attention(
                ids, token_pieces, cos, sin, q8, key_later, val, att, prob, d_pieces[:2], gain, wide, ggain, 0, 2
            )
            (key_last,) = pick("T0", [key], (lead_in, lead_rest), (along_x,), (along_y,), (along_x, along_y))
            signal = sums[0]
            if flag("T5") >= 3:
                along_x, along_y = after([along_x, along_y], signal)
            if flag("T5") == 4:
                next_in = add(kept_in[8:12], came_in[8:12], along_x[:4])
                next_rest = add(kept_rest[8:12], came_rest[8:12], along_y[:4])
                (key_last,) = after([key_last], next_in, next_rest)
            dn0, dn1, dn2, dn3, far, near = backward_attention(
                ids, token_pieces, cos, sin, q8, key_last, val, att, prob, d_pieces[2:], gain, wide, ggain, 2, 2, sums
            )
        else:
            dn0, dn1, dn2, dn3, far, near = backward_attention(
                ids, token_pieces, cos, sin, q8, key_later, val, att, prob, d_pieces, gain, wide, ggain
            )
        if flag("T5") in (1, 2):
            along_x, along_y = after([along_x, along_y], *((near,) if flag("T5") == 1 else (near, far)))
        (far,) = pick("T4", [far], (along_x, along_y), (along_x,), (along_y,))
        far_y = xperm(far, 4)
        next_in = add(kept_in[8:12], came_in[8:12], along_x[:4])
        next_rest = add(kept_rest[8:12], came_rest[8:12], along_y[:4])
        next_in, next_rest = pick("T8", [next_in, next_rest], (far_y,))
        then_y, then_x = xperm(next_in, 4), xperm(next_rest, 2)
        (far_y,) = pick("TA", [far_y], (then_y, then_x), (then_x,), (then_y,))
        column_in = reduce_column(kept_in, came_in, along_x[4:], then_y)
        column_rest = reduce_column(kept_rest, came_rest, along_y[4:], then_x)
    if flag("ZM"):
        wide_z = [jnp.concatenate([column_in[kz], column_rest[kz]], axis=1) for kz in range(4)]
        wide_z = [wide_z[0]] + [xperm(wide_z[kz], 8 * kz) for kz in (1, 2, 3)]
        column_in = [piece[:, :1152] for piece in wide_z]
        column_rest = [piece[:, 1152:] for piece in wide_z]
    (far_y,) = pick("TB", [far_y], (*column_in, *column_rest), tuple(column_rest), tuple(column_in))
    e = [add(near[kz], far_y[kz]) for kz in range(4)]
    heads = [e[0], xperm(e[1], 8), xperm(e[2], 16), xperm(e[3], 24)]
    dn1, dn3 = pick("T6", [dn1, dn3], (far_y,), (then_x, then_y), (along_x, along_y), (e[1],))
    if flag("DM"):
        both = xperm(jnp.stack([dn1, dn3]), 1)
        dn1_came, dn3_came = both[0], both[1]
    else:
        dn1_came, dn3_came = xperm(dn1, 1), xperm(dn3, 1)
    x_sum = add(dn2, dn3_came)
    x_came = xperm(x_sum, 2)
    own_sum = add(dn0, dn1_came)
    heads = pick("T7", heads, (x_came,))
    mine, other = sum_rows(ids, *column_in, *column_rest)
    states = [
        (weight_in, first_in, second_in, average_in),
        (weight_out, first_out, second_out, average_out),
        (weight_down, first_down, second_down, average_down),
    ]
    new_rows = update_rows(ids, mine, xperm(other, 1), states)

    heads = pick("TC", heads, (new_rows[0],), (other,))
    came = exchange(*sum_heads(ids, *heads), flag("UX"))
    new_heads = update_heads(
        ids,
        came,
        (weight_qkv, first_qkv, second_qkv, average_qkv),
        (norm_gains, first_gains, second_gains, average_gains),
    )

    dnormed = own_sum.astype(F32) + x_came.astype(F32)
    normed, inverse = norm_parts(tokens.astype(F32))
    grad_tokens = dmiddle + norm_back(dnormed * gain[0:1, :], normed, inverse)

    updated = [new_heads[:5], new_rows[5:10], new_rows[:5], new_rows[10:], new_heads[5:]]
    return (block_out, grad_tokens) + tuple(updated[i][j] for j in range(5) for i in range(5))


def solution(mesh):
    sizes = dict(mesh.shape)
    body = fast_body if sizes == {"dp": 8, "fsdp": 4} else general_body
    rows, columns = P(("dp", "fsdp"), None), P(None, ("dp", "fsdp"))
    weights = (rows,) * 4 + (columns,)
    return jax.shard_map(
        body,
        mesh=mesh,
        in_specs=(rows, rows, P(), P()) + weights * 4,
        out_specs=(rows, rows) + weights * 5,
        check_vma=False,
    )
```

```python
import functools

import jax
import jax.numpy as jnp
from jax import lax
from jax.experimental import pallas as pl
from jax.experimental.pallas import tpu as pltpu
from jax.sharding import PartitionSpec as P

HEADS = 12
HD = 64
STEP = 6


NORM_EPS = 1e-05
ROTARY_BASE = 160000.0
BETA_FIRST = 0.5
BETA_SECOND = 0.5
ADAM_EPS = 1e-08
WEIGHT_DECAY = 0.01
MATRIX_RATE = 0.04
GAIN_RATE = 0.5
AVERAGE_KEEP = 0.6
MASKED = -1e30


def group_layout(count_row, length_row, slots):
    devices_here = count_row.shape[0]
    places = jnp.arange(devices_here * slots, dtype=jnp.int32)
    holder = places // slots
    within = places - holder * slots
    before = jnp.cumsum(count_row) - count_row
    choose = (holder[:, None] == jnp.arange(devices_here, dtype=jnp.int32)[None, :]).astype(
        jnp.int32
    )
    offset = jnp.sum(choose * before[None, :], axis=1) + within
    limits = jnp.sum(choose * count_row[None, :], axis=1)
    living = within < limits
    doc_ends = jnp.cumsum(length_row)
    passed = offset[:, None] >= doc_ends[None, :]
    document = jnp.sum(passed.astype(jnp.int32), axis=1)
    begins = jnp.max(jnp.where(passed, doc_ends[None, :], 0), axis=1)
    number_docs = length_row.shape[0]
    document = jnp.where(living, document, number_docs)
    position = jnp.where(living, offset - begins, 0)
    return (document, position, living)


def rotary_tables(position, head_size):
    half_size = head_size // 2
    speeds = ROTARY_BASE ** (-(jnp.arange(half_size, dtype=jnp.float32) * (2.0 / head_size)))
    angles = position.astype(jnp.float32)[:, None] * speeds[None, :]
    return (jnp.cos(angles), jnp.sin(angles))


def rotate(heads_in, cosine_table, sine_table):
    half_size = heads_in.shape[-1] // 2
    leading = heads_in[..., :half_size]
    latter = heads_in[..., half_size:]
    cos_wide = cosine_table[:, None, :]
    sin_wide = sine_table[:, None, :]
    return jnp.concatenate(
        [leading * cos_wide - latter * sin_wide, latter * cos_wide + leading * sin_wide], axis=-1
    )


def rotate_back(grads_in, cosine_table, sine_table):
    half_size = grads_in.shape[-1] // 2
    leading = grads_in[..., :half_size]
    latter = grads_in[..., half_size:]
    cos_wide = cosine_table[:, None, :]
    sin_wide = sine_table[:, None, :]
    return jnp.concatenate(
        [leading * cos_wide + latter * sin_wide, latter * cos_wide - leading * sin_wide], axis=-1
    )


def norm_parts(values_in):
    center = values_in - jnp.mean(values_in, axis=-1, keepdims=True)
    inverse = lax.rsqrt(jnp.mean(center * center, axis=-1, keepdims=True) + NORM_EPS)
    return (center * inverse, inverse)


def norm_back(upstream, normed, inverse):
    return inverse * (
        upstream
        - jnp.mean(upstream, axis=-1, keepdims=True)
        - normed * jnp.mean(upstream * normed, axis=-1, keepdims=True)
    )


def block_scores(queries, key_block, doc_query, doc_key, score_scale):
    scores = (
        jnp.einsum("qhd,khd->hqk", queries, key_block, preferred_element_type=jnp.float32)
        * score_scale
    )
    return jnp.where(doc_query[None, :, None] == doc_key[None, None, :], scores, MASKED)


def contract_rows(left_side, right_side):
    return lax.dot_general(
        left_side, right_side, (((0,), (0,)), ((), ())), preferred_element_type=jnp.float32
    )


def contract_cols(left_side, right_side):
    return lax.dot_general(
        left_side, right_side, (((1,), (1,)), ((), ())), preferred_element_type=jnp.float32
    )


def adam_update(master, first_old, second_old, average_old, gradient, step_rate):
    first_new = BETA_FIRST * first_old + (1.0 - BETA_FIRST) * gradient
    second_new = BETA_SECOND * second_old + (1.0 - BETA_SECOND) * gradient * gradient
    first_fix = first_new / (1.0 - BETA_FIRST**STEP)
    second_fix = second_new / (1.0 - BETA_SECOND**STEP)
    master_new = master - step_rate * (
        first_fix / (jnp.sqrt(second_fix) + ADAM_EPS) + WEIGHT_DECAY * master
    )
    average_new = AVERAGE_KEEP * average_old + (1.0 - AVERAGE_KEEP) * master_new
    return (first_new, second_new, master_new, average_new, master_new.astype(jnp.bfloat16))


def general_body(
    tokens,
    cotangent,
    counts,
    lengths,
    weight_qkv,
    weight_out,
    weight_in,
    weight_down,
    norm_gains,
    first_qkv,
    first_out,
    first_in,
    first_down,
    first_gains,
    second_qkv,
    second_out,
    second_in,
    second_down,
    second_gains,
    average_qkv,
    average_out,
    average_in,
    average_down,
    average_gains,
):
    slots = tokens.shape[0]
    model_width = tokens.shape[1]
    hidden_units = weight_down.shape[1]
    head_count = HEADS
    head_size = HD
    score_scale = 1.0 / head_size**0.5
    heads_shape = (slots, head_count, head_size)
    group_row = lax.axis_index("dp")
    own_place = lax.axis_index("fsdp")
    count_row = lax.dynamic_index_in_dim(counts, group_row, 0, keepdims=False)
    length_row = lax.dynamic_index_in_dim(lengths, group_row, 0, keepdims=False)
    doc_all, position_all, living_all = group_layout(count_row, length_row, slots)
    doc_mine = lax.dynamic_slice_in_dim(doc_all, own_place * slots, slots)
    position_mine = lax.dynamic_slice_in_dim(position_all, own_place * slots, slots)
    living_mine = lax.dynamic_slice_in_dim(living_all, own_place * slots, slots)
    cosine_table, sine_table = rotary_tables(position_mine, head_size)
    living_col = living_mine[:, None]
    copies = (
        weight_qkv.astype(jnp.bfloat16),
        weight_out.astype(jnp.bfloat16),
        weight_in.astype(jnp.bfloat16),
        weight_down.astype(jnp.bfloat16),
        norm_gains.astype(jnp.bfloat16),
    )
    qkv_full, out_full, in_full, down_full, gain_full = (
        lax.all_gather(copies[0], ("dp", "fsdp"), axis=0, tiled=True),
        lax.all_gather(copies[1], ("dp", "fsdp"), axis=0, tiled=True),
        lax.all_gather(copies[2], ("dp", "fsdp"), axis=0, tiled=True),
        lax.all_gather(copies[3], ("dp", "fsdp"), axis=0, tiled=True),
        lax.all_gather(copies[4], ("dp", "fsdp"), axis=1, tiled=True),
    )
    tokens_f = tokens.astype(jnp.float32)
    normed_one, inverse_one = norm_parts(tokens_f)
    gain_one = gain_full[0].astype(jnp.float32)
    gain_two = gain_full[1].astype(jnp.float32)
    normed1_low = (normed_one * gain_one).astype(jnp.bfloat16)
    mixed_qkv = jnp.dot(normed1_low, qkv_full, preferred_element_type=jnp.float32)
    queries16 = rotate(
        mixed_qkv[:, :model_width].reshape(heads_shape), cosine_table, sine_table
    ).astype(jnp.bfloat16)
    keys16 = rotate(
        mixed_qkv[:, model_width : 2 * model_width].reshape(heads_shape), cosine_table, sine_table
    ).astype(jnp.bfloat16)
    key_flat = keys16.reshape(slots, model_width)
    value_flat = mixed_qkv[:, 2 * model_width :].astype(jnp.bfloat16)
    key_rows, value_rows = (
        lax.all_gather(key_flat, "fsdp", axis=0, tiled=True),
        lax.all_gather(value_flat, "fsdp", axis=0, tiled=True),
    )
    group_rows = key_rows.shape[0]
    block_rows = 512
    count_blocks = group_rows // block_rows
    blocks_shape = (count_blocks, block_rows, head_count, head_size)
    doc_blocks = doc_all.reshape(count_blocks, block_rows)
    key_blocks = key_rows.reshape(blocks_shape)
    value_blocks = value_rows.reshape(blocks_shape)

    def max_sum(state_now, pieces):
        run_peak, run_total = state_now
        scores = block_scores(queries16, pieces[0], doc_mine, pieces[1], score_scale)
        new_peak = jnp.maximum(run_peak, jnp.max(scores, axis=-1))
        run_total = run_total * jnp.exp(run_peak - new_peak) + jnp.sum(
            jnp.exp(scores - new_peak[:, :, None]), axis=-1
        )
        return ((new_peak, run_total), None)

    start_state = (
        jnp.full((head_count, slots), MASKED, jnp.float32),
        jnp.zeros((head_count, slots), jnp.float32),
    )
    (run_peak, run_total), unused_max = lax.scan(max_sum, start_state, (key_blocks, doc_blocks))
    log_total = run_peak + jnp.log(run_total)

    def weigh_values(accum, pieces):
        scores = block_scores(queries16, pieces[0], doc_mine, pieces[2], score_scale)
        probs16 = jnp.exp(scores - log_total[:, :, None]).astype(jnp.bfloat16)
        return (
            accum
            + jnp.einsum("hqk,khd->qhd", probs16, pieces[1], preferred_element_type=jnp.float32),
            None,
        )

    attended, unused_out = lax.scan(
        weigh_values, jnp.zeros(heads_shape, jnp.float32), (key_blocks, value_blocks, doc_blocks)
    )
    attended16 = attended.reshape(slots, model_width).astype(jnp.bfloat16)
    middle = tokens_f + jnp.dot(attended16, out_full, preferred_element_type=jnp.float32)
    normed_two, inverse_two = norm_parts(middle)
    normed2_low = (normed_two * gain_two).astype(jnp.bfloat16)
    gate_up = jnp.dot(normed2_low, in_full, preferred_element_type=jnp.float32)
    act_half = gate_up[:, :hidden_units]
    gate_half = gate_up[:, hidden_units:]
    activated16 = (jax.nn.gelu(act_half, approximate=False) * gate_half).astype(jnp.bfloat16)
    branch_two = contract_cols(activated16, down_full)
    block_out = jnp.where(living_col, middle + branch_two, 0.0).astype(jnp.bfloat16)
    qkv_back, out_back, in_back, down_back, gain_back = (
        lax.all_gather(copies[0], ("dp", "fsdp"), axis=0, tiled=True),
        lax.all_gather(copies[1], ("dp", "fsdp"), axis=0, tiled=True),
        lax.all_gather(copies[2], ("dp", "fsdp"), axis=0, tiled=True),
        lax.all_gather(copies[3], ("dp", "fsdp"), axis=0, tiled=True),
        lax.all_gather(copies[4], ("dp", "fsdp"), axis=1, tiled=True),
    )
    key_again, value_again = (
        lax.all_gather(key_flat, "fsdp", axis=0, tiled=True),
        lax.all_gather(value_flat, "fsdp", axis=0, tiled=True),
    )
    gain_one_back = gain_back[0].astype(jnp.float32)
    gain_two_back = gain_back[1].astype(jnp.float32)
    dout = jnp.where(living_col, cotangent.astype(jnp.float32), 0.0)
    dym16 = dout.astype(jnp.bfloat16)
    grad_down = contract_rows(dym16, activated16)
    dact = jnp.dot(dym16, down_back, preferred_element_type=jnp.float32)
    unused_gate, gate_pull = jax.vjp(
        lambda front_part, rear_part: jax.nn.gelu(front_part, approximate=False) * rear_part,
        act_half,
        gate_half,
    )
    dfront, drear = gate_pull(dact)
    dgate16 = jnp.concatenate([dfront, drear], axis=1).astype(jnp.bfloat16)
    grad_in = contract_rows(normed2_low, dgate16)
    dnormed_two = contract_cols(dgate16, in_back)
    grad_gain_two = jnp.sum(dnormed_two * normed_two, axis=0)
    dmiddle = dout + norm_back(dnormed_two * gain_two_back, normed_two, inverse_two)
    dbranch16 = dmiddle.astype(jnp.bfloat16)
    grad_out = contract_rows(attended16, dbranch16)
    dattn16 = contract_cols(dbranch16, out_back).astype(jnp.bfloat16).reshape(heads_shape)
    row_delta = jnp.sum(dattn16.astype(jnp.float32) * attended, axis=-1).T
    back_keys = key_again.reshape(blocks_shape)
    back_values = value_again.reshape(blocks_shape)

    def back_block(dquery_sum, pieces):
        key_block, value_block, doc_block = pieces
        scores = block_scores(queries16, key_block, doc_mine, doc_block, score_scale)
        probs = jnp.exp(scores - log_total[:, :, None])
        probs16 = probs.astype(jnp.bfloat16)
        dvalue_block = jnp.einsum(
            "hqk,qhd->khd", probs16, dattn16, preferred_element_type=jnp.float32
        )
        dprobs = jnp.einsum(
            "qhd,khd->hqk", dattn16, value_block, preferred_element_type=jnp.float32
        )
        dscores16 = (probs * (dprobs - row_delta[:, :, None])).astype(jnp.bfloat16)
        dquery_sum = dquery_sum + jnp.einsum(
            "hqk,khd->qhd", dscores16, key_block, preferred_element_type=jnp.float32
        )
        dkey_block = jnp.einsum(
            "hqk,qhd->khd", dscores16, queries16, preferred_element_type=jnp.float32
        )
        return (dquery_sum, (dkey_block, dvalue_block))

    dquery_sum, (dkey_blocks, dvalue_blocks) = lax.scan(
        back_block, jnp.zeros(heads_shape, jnp.float32), (back_keys, back_values, doc_blocks)
    )
    dkey_mine, dvalue_mine = (
        lax.psum_scatter(
            (dkey_blocks.reshape(group_rows, model_width) * score_scale).astype(jnp.bfloat16),
            "fsdp",
            scatter_dimension=0,
            tiled=True,
        ).astype(jnp.float32),
        lax.psum_scatter(
            dvalue_blocks.reshape(group_rows, model_width).astype(jnp.bfloat16),
            "fsdp",
            scatter_dimension=0,
            tiled=True,
        ).astype(jnp.float32),
    )
    dquery_pre = rotate_back(dquery_sum * score_scale, cosine_table, sine_table).reshape(
        slots, model_width
    )
    dkey_pre = rotate_back(dkey_mine.reshape(heads_shape), cosine_table, sine_table).reshape(
        slots, model_width
    )
    dmixed16 = jnp.concatenate([dquery_pre, dkey_pre, dvalue_mine], axis=1).astype(jnp.bfloat16)
    grad_qkv = contract_rows(normed1_low, dmixed16)
    dnormed_one = contract_cols(dmixed16, qkv_back)
    grad_gain_one = jnp.sum(dnormed_one * normed_one, axis=0)
    grad_tokens = dmiddle + norm_back(dnormed_one * gain_one_back, normed_one, inverse_one)
    grad_gains = jnp.stack([grad_gain_one, grad_gain_two], axis=0)
    reduced = (
        lax.psum_scatter(grad_qkv, ("dp", "fsdp"), scatter_dimension=0, tiled=True),
        lax.psum_scatter(grad_out, ("dp", "fsdp"), scatter_dimension=0, tiled=True),
        lax.psum_scatter(grad_in, ("dp", "fsdp"), scatter_dimension=0, tiled=True),
        lax.psum_scatter(grad_down, ("dp", "fsdp"), scatter_dimension=0, tiled=True),
        lax.psum_scatter(grad_gains, ("dp", "fsdp"), scatter_dimension=1, tiled=True),
    )
    masters = (weight_qkv, weight_out, weight_in, weight_down, norm_gains)
    firsts = (first_qkv, first_out, first_in, first_down, first_gains)
    seconds = (second_qkv, second_out, second_in, second_down, second_gains)
    averages = (average_qkv, average_out, average_in, average_down, average_gains)
    rates = (MATRIX_RATE, MATRIX_RATE, MATRIX_RATE, MATRIX_RATE, GAIN_RATE)
    updated = [
        adam_update(
            masters[which],
            firsts[which],
            seconds[which],
            averages[which],
            reduced[which],
            rates[which],
        )
        for which in range(5)
    ]
    return (
        block_out,
        grad_tokens,
        updated[0][0],
        updated[1][0],
        updated[2][0],
        updated[3][0],
        updated[4][0],
        updated[0][1],
        updated[1][1],
        updated[2][1],
        updated[3][1],
        updated[4][1],
        updated[0][2],
        updated[1][2],
        updated[2][2],
        updated[3][2],
        updated[4][2],
        updated[0][3],
        updated[1][3],
        updated[2][3],
        updated[3][3],
        updated[4][3],
        updated[0][4],
        updated[1][4],
        updated[2][4],
        updated[3][4],
        updated[4][4],
    )


FL = {'DM': 1, 'DX': 1, 'H1': 3, 'H2': 2, 'H3': 2, 'H5': 1, 'H6': 1, 'H7': 2, 'QX': 1, 'T4': 1, 'TC': 1}
BF = jnp.bfloat16
F32 = jnp.float32
AXES = ("dp", "fsdp")
VMEM_LIMIT = 60 * 1024 * 1024


def xperm(value, mask):
    count = lax.axis_size("dp") * lax.axis_size("fsdp")
    return lax.ppermute(value, AXES, [(i, i ^ mask) for i in range(count)])


def dot_nn(a, b):
    return jnp.dot(a, b, preferred_element_type=F32)


def dot_nt(a, b):
    return lax.dot_general(a, b, (((1,), (1,)), ((), ())), preferred_element_type=F32)


def dot_tn(a, b):
    return lax.dot_general(a, b, (((0,), (0,)), ((), ())), preferred_element_type=F32)


def spread_columns(weight):
    rows = weight.shape[0]
    gap, end = jnp.zeros((rows, 32), weight.dtype), jnp.zeros((rows, 64), weight.dtype)
    parts = []
    for i in range(4):
        parts += [weight[:, 96 * i : 96 * i + 96], gap]
    return jnp.concatenate(parts + [weight[:, 384:576], end], axis=1)


def pack_columns(spread, last):
    return jnp.concatenate([spread[:, 128 * i : 128 * i + 96] for i in range(4)] + [spread[:, 512:704], last], axis=1)


def pack_heads(block):
    return jnp.concatenate([block[64 * i : 64 * i + 64] for i in range(4)], axis=1)


def unpack_heads(packed):
    return jnp.concatenate([packed[:, 192 * i : 192 * i + 192] for i in range(4)], axis=0)


def head_lanes(width, head):
    lane = lax.broadcasted_iota(jnp.int32, (1, width), 1) % 128
    return (lane >= 32 * head) & (lane < 32 * head + 32)


def value_lanes(width, head):
    lane = lax.broadcasted_iota(jnp.int32, (1, width), 1)
    return (lane >= 64 * head) & (lane < 64 * head + 64)


def prologue_kernel(ids, wq, w_out, w_in, w_down, gains, near, far, mine, other):
    f, core = ids[0], ids[2]
    row = lax.broadcasted_iota(jnp.int32, (24, 24), 0)
    col = lax.broadcasted_iota(jnp.int32, (24, 24), 1)
    parts = []
    for j in range(2):
        spread = jnp.where(row == col, gains[j : j + 1, :], 0.0)
        parts.append(jnp.sum(spread, axis=-1, keepdims=True))
    lane = lax.broadcasted_iota(jnp.int32, (24, 64), 1)
    columns = jnp.where(lane == 0, parts[0], jnp.where(lane == 1, parts[1], 0.0))
    blocks = []
    for j in range(4):
        pieces = []
        for part in range(2):
            heads = wq[:, 768 * part + 192 * j : 768 * part + 192 * j + 192]
            pieces += [heads[:, 64 * h + 32 * half : 64 * h + 32 * half + 32] for half in range(2) for h in range(3)]
        blocks.append(jnp.concatenate(pieces + [wq[:, 1536 + 192 * j : 1728 + 192 * j], columns], axis=1))
    for k, out in enumerate((near.at[0], near.at[1], far.at[0], far.at[1])):
        place = f ^ k
        low = jnp.where(place == 0, blocks[0], blocks[1])
        high = jnp.where(place == 2, blocks[2], blocks[3])
        out[...] = jnp.where(place < 2, low, high).astype(BF)
    left = jnp.concatenate([w_in[:, :1152], w_out[:, :384], w_down[:, :640]], axis=1)
    right = jnp.concatenate([w_in[:, 1152:], w_out[:, 384:], w_down[:, 640:], jnp.zeros((24, 128), F32)], axis=1)
    mine[...] = jnp.where(core == 0, left, right).astype(BF)
    other[...] = jnp.where(core == 0, right, left).astype(BF)


def assemble_kernel(ids, q0, q1, q2, q3, mine, came, rows, other):
    f, core = ids[0], ids[2]
    pieces = [q[i].astype(F32) for q, i in ((q0, 0), (q1, 1), (q2, 0), (q3, 1))]
    ordered = []
    for place in range(4):
        k = f ^ place
        low = jnp.where(k == 0, pieces[0], pieces[1])
        high = jnp.where(k == 2, pieces[2], pieces[3])
        ordered.append(jnp.where(k < 2, low, high))
    rows[...] = jnp.concatenate(ordered, axis=0).astype(BF)
    one, two = mine[...].astype(F32), came[...].astype(F32)
    other[...] = jnp.concatenate([jnp.where(core == 0, one, two), jnp.where(core == 0, two, one)], axis=0).astype(BF)


def forward_kernel(
    ids, t0, t1, t2, t3, cos, sin, docq, dock, w0, w1, w2, w3,
    q8, key, val, att, near, far, prob, gain, wide, wscr, sems,
):
    step = pl.program_id(0)

    @pl.when(step == 0)
    def _():
        copies = []
        pieces = (w0, w1, w2.at[0], w3.at[0], w2.at[1], w3.at[1], w2.at[2], w3.at[2])
        for k, piece in enumerate(pieces):
            at = pl.multiple_of(96 * (ids[1] ^ k), 96)
            copies.append(pltpu.make_async_copy(piece, wscr.at[pl.ds(at, 96)], sems.at[k]))
            copies[-1].start()
        for copy in copies:
            copy.wait()
        weight = wscr[...]
        wide[...] = spread_columns(weight)
        row = lax.broadcasted_iota(jnp.int32, (8, 640), 0)
        col = lax.broadcasted_iota(jnp.int32, (8, 640), 1)
        pick = ((col == row + 576) & (row < 2)).astype(F32).astype(BF)
        gain[...] = dot_nt(pick, weight)
        gain_row = gain[0:1, :]
        for i, piece in enumerate((t0, t1, t2, t3)):
            rows = slice(256 * i, 256 * i + 256)
            x = piece[...].astype(F32)
            center = x - jnp.mean(x, axis=-1, keepdims=True)
            inverse = lax.rsqrt(jnp.mean(center * center, axis=-1, keepdims=True) + NORM_EPS)
            mixed = dot_nn((center * inverse * gain_row).astype(BF), wide[...])
            c, s = cos[rows, :], sin[rows, :]
            qa, qb = mixed[:, :128], mixed[:, 128:256]
            ka, kb = mixed[:, 256:384], mixed[:, 384:512]
            q8[rows, :128] = ((qa * c - qb * s).astype(BF).astype(F32) * 0.125).astype(BF)
            q8[rows, 128:] = ((qb * c + qa * s).astype(BF).astype(F32) * 0.125).astype(BF)
            key[rows, :128] = (ka * c - kb * s).astype(BF)
            key[rows, 128:] = (kb * c + ka * s).astype(BF)
            val[rows, :] = mixed[:, 512:].astype(BF)

    rows = pl.ds(pl.multiple_of(step * 256, 256), 256)
    queries = q8[rows, :]
    keys = key[...]
    values = val[...]
    same = docq[rows, :] == dock[...]
    total = jnp.zeros((256, 256), F32)
    zero = jnp.zeros((), BF)
    for h in range(3):
        scores = dot_nt(jnp.where(head_lanes(256, h), queries, zero), keys)
        scores = jnp.where(same, scores, MASKED)
        peak = jnp.max(scores, axis=-1, keepdims=True)
        weights = jnp.exp(scores - peak)
        scale = 1.0 / jnp.sum(weights, axis=-1, keepdims=True)
        weights16 = (weights * scale).astype(BF)
        prob[h] = weights16
        total += dot_nn(weights16, jnp.where(value_lanes(256, h), values, zero))
    att[...] = total[:, :192]
    low = total[:, :192].astype(BF)

    @pl.when(step < 2)
    def _():
        near[0] = pack_heads(low)

    @pl.when(step >= 2)
    def _():
        far[0] = pack_heads(low)


def project_kernel(ids, t0, t1, t2, t3, cos, sin, w0, w1, w2, w3, q8, key, val, gain, wide, wscr, sems):
    copies = []
    pieces = (w0, w1, w2.at[0], w3.at[0], w2.at[1], w3.at[1], w2.at[2], w3.at[2])
    for k, piece in enumerate(pieces):
        at = pl.multiple_of(96 * (ids[1] ^ k), 96)
        copies.append(pltpu.make_async_copy(piece, wscr.at[pl.ds(at, 96)], sems.at[k]))
        copies[-1].start()
    for copy in copies:
        copy.wait()
    weight = wscr[...]
    wide[...] = spread_columns(weight)
    row = lax.broadcasted_iota(jnp.int32, (8, 640), 0)
    col = lax.broadcasted_iota(jnp.int32, (8, 640), 1)
    pick = ((col == row + 576) & (row < 2)).astype(F32).astype(BF)
    gain[...] = dot_nt(pick, weight)
    gain_row = gain[0:1, :]
    for i, piece in enumerate((t0, t1, t2, t3)):
        rows = slice(256 * i, 256 * i + 256)
        x = piece[...].astype(F32)
        center = x - jnp.mean(x, axis=-1, keepdims=True)
        inverse = lax.rsqrt(jnp.mean(center * center, axis=-1, keepdims=True) + NORM_EPS)
        mixed = dot_nn((center * inverse * gain_row).astype(BF), wide[...])
        c, s = cos[rows, :], sin[rows, :]
        qa, qb = mixed[:, :128], mixed[:, 128:256]
        ka, kb = mixed[:, 256:384], mixed[:, 384:512]
        q8[rows, :128] = ((qa * c - qb * s).astype(BF).astype(F32) * 0.125).astype(BF)
        q8[rows, 128:] = ((qb * c + qa * s).astype(BF).astype(F32) * 0.125).astype(BF)
        key[rows, :128] = (ka * c - kb * s).astype(BF)
        key[rows, 128:] = (kb * c + ka * s).astype(BF)
        val[rows, :] = mixed[:, 512:].astype(BF)


def attend_kernel(q8, key, val, docq, dock, att, near, far, prob):
    step = pl.program_id(0)
    rows = pl.ds(pl.multiple_of(step * 256, 256), 256)
    queries = q8[rows, :]
    keys = key[...]
    values = val[...]
    same = docq[rows, :] == dock[...]
    total = jnp.zeros((256, 256), F32)
    zero = jnp.zeros((), BF)
    for h in range(3):
        scores = dot_nt(jnp.where(head_lanes(256, h), queries, zero), keys)
        scores = jnp.where(same, scores, MASKED)
        peak = jnp.max(scores, axis=-1, keepdims=True)
        weights = jnp.exp(scores - peak)
        scale = 1.0 / jnp.sum(weights, axis=-1, keepdims=True)
        weights16 = (weights * scale).astype(BF)
        prob[h] = weights16
        total += dot_nn(weights16, jnp.where(value_lanes(256, h), values, zero))
    att[...] = total[:, :192]
    low = total[:, :192].astype(BF)

    @pl.when(step < 2)
    def _():
        near[0] = pack_heads(low)

    @pl.when(step >= 2)
    def _():
        far[0] = pack_heads(low)


def full(shape):
    return pl.BlockSpec(shape, lambda *_: (0,) * len(shape))


VM = pl.BlockSpec(memory_space=pltpu.VMEM)
SMEM = pl.BlockSpec(memory_space=pltpu.SMEM)
ANY = pl.BlockSpec(memory_space=pltpu.HBM)


def shaped(shape, dtype):
    return jax.ShapeDtypeStruct(shape, dtype)


def prologue(ids, weight_qkv, weight_out, weight_in, weight_down, norm_gains):
    return pl.pallas_call(
        prologue_kernel,
        in_specs=[SMEM] + [VM] * 5,
        out_specs=[VM] * 4,
        out_shape=[shaped((2, 24, 640), BF)] * 2 + [shaped((24, 2176), BF)] * 2,
        compiler_params=pltpu.CompilerParams(vmem_limit_bytes=VMEM_LIMIT),
        cost_estimate=pl.CostEstimate(flops=10**6, bytes_accessed=10**6, transcendentals=0),
        name="prologue",
    )(ids, weight_qkv, weight_out, weight_in, weight_down, norm_gains)


def assemble(ids, *pieces):
    return pl.pallas_call(
        assemble_kernel,
        in_specs=[SMEM] + [VM] * 6,
        out_specs=[VM] * 2,
        out_shape=[shaped((96, 640), BF), shaped((48, 2176), BF)],
        compiler_params=pltpu.CompilerParams(vmem_limit_bytes=VMEM_LIMIT),
        cost_estimate=pl.CostEstimate(flops=10**6, bytes_accessed=10**6, transcendentals=0),
        name="assemble",
    )(ids, *pieces)


def forward_attention(ids, token_pieces, cos, sin, docs, w_pieces):
    return pl.pallas_call(
        forward_kernel,
        grid=(4,),
        in_specs=[SMEM]
        + [full((256, 768))] * 4
        + [full((1024, 128))] * 2
        + [full((1024, 1)), full((1, 1024))]
        + [ANY] * 4,
        out_specs=[
            full((1024, 256)),
            full((1024, 256)),
            full((1024, 256)),
            pl.BlockSpec((256, 192), lambda i: (i, 0)),
            pl.BlockSpec((1, 64, 768), lambda i: (jnp.minimum(i, 1), 0, 0)),
            pl.BlockSpec((1, 64, 768), lambda i: (jnp.maximum(i - 2, 0), 0, 0)),
            pl.BlockSpec((3, 256, 1024), lambda i: (0, i, 0)),
            full((8, 768)),
            full((768, 768)),
        ],
        out_shape=[
            shaped((1024, 256), BF),
            shaped((1024, 256), BF),
            shaped((1024, 256), BF),
            shaped((1024, 192), F32),
            shaped((2, 64, 768), BF),
            shaped((2, 64, 768), BF),
            shaped((3, 1024, 1024), BF),
            shaped((8, 768), F32),
            shaped((768, 768), BF),
        ],
        scratch_shapes=[pltpu.VMEM((768, 640), BF), pltpu.SemaphoreType.DMA((8,))],
        compiler_params=pltpu.CompilerParams(vmem_limit_bytes=VMEM_LIMIT),
        cost_estimate=pl.CostEstimate(flops=6 * 10**9, bytes_accessed=16 * 10**6, transcendentals=3 * 10**6),
        name="forward_attention",
    )(ids, *token_pieces, cos, sin, docs[:, None], docs[None, :], *w_pieces)


def project(ids, token_pieces, cos, sin, w_pieces):
    return pl.pallas_call(
        project_kernel,
        in_specs=[SMEM] + [VM] * 6 + [ANY] * 4,
        out_specs=[VM] * 5,
        out_shape=[
            shaped((1024, 256), BF),
            shaped((1024, 256), BF),
            shaped((1024, 256), BF),
            shaped((8, 768), F32),
            shaped((768, 768), BF),
        ],
        scratch_shapes=[pltpu.VMEM((768, 640), BF), pltpu.SemaphoreType.DMA((8,))],
        compiler_params=pltpu.CompilerParams(vmem_limit_bytes=VMEM_LIMIT),
        cost_estimate=pl.CostEstimate(flops=3 * 10**9, bytes_accessed=8 * 10**6, transcendentals=0),
        name="project",
    )(ids, *token_pieces, cos, sin, *w_pieces)


def attend(q8, key, val, docs):
    return pl.pallas_call(
        attend_kernel,
        grid=(4,),
        in_specs=[full((1024, 256))] * 3 + [full((1024, 1)), full((1, 1024))],
        out_specs=[
            pl.BlockSpec((256, 192), lambda i: (i, 0)),
            pl.BlockSpec((1, 64, 768), lambda i: (jnp.minimum(i, 1), 0, 0)),
            pl.BlockSpec((1, 64, 768), lambda i: (jnp.maximum(i - 2, 0), 0, 0)),
            pl.BlockSpec((3, 256, 1024), lambda i: (0, i, 0)),
        ],
        out_shape=[
            shaped((1024, 192), F32),
            shaped((2, 64, 768), BF),
            shaped((2, 64, 768), BF),
            shaped((3, 1024, 1024), BF),
        ],
        compiler_params=pltpu.CompilerParams(vmem_limit_bytes=VMEM_LIMIT),
        cost_estimate=pl.CostEstimate(flops=3 * 10**9, bytes_accessed=8 * 10**6, transcendentals=3 * 10**6),
        name="attend",
    )(q8, key, val, docs[:, None], docs[None, :])


def erf_pair(x):
    cdf = 0.5 * (1.0 + lax.erf(x * (0.5**0.5)))
    density = jnp.exp(-0.5 * x * x) * (1.0 / (2.0 * 3.141592653589793) ** 0.5)
    return cdf, density


def load_halves(held, w_in, w_rest, core, chip, sems):
    groups = [[], []]
    for owner in range(2):
        half = core if owner == 0 else 1 - core
        arrays = held[owner * 5 : owner * 5 + 5]
        for group in range(4):
            for kz in range(4):
                rows = pl.ds(pl.multiple_of(48 * (chip ^ (kz * 4 + group)), 48), 48)
                if group < 3:
                    in_parts = [(arrays[group].at[kz, :, pl.ds(0, 1152)], w_in.at[half, rows])]
                    rest_part = arrays[group].at[kz, :, pl.ds(1152, 1024)]
                else:
                    in_parts = [
                        (arrays[3].at[pl.ds(48 * kz, 48)], w_in.at[half, rows, pl.ds(0, 768)]),
                        (arrays[4].at[kz, :, pl.ds(0, 384)], w_in.at[half, rows, pl.ds(768, 384)]),
                    ]
                    rest_part = arrays[4].at[kz, :, pl.ds(384, 1024)]
                for which, parts in ((0, in_parts), (1, [(rest_part, w_rest.at[half, rows])])):
                    for source, target in parts:
                        sem = sems.at[which, len(groups[which])]
                        groups[which].append(pltpu.make_async_copy(source, target, sem))
    for copy in groups[1] + groups[0]:
        copy.start()
    return groups


def store_half(own_pack, other_pack, at, halves, core):
    width = halves[0].shape[1]
    own_pack[:, at : at + width] = jnp.where(core == 0, halves[0], halves[1])
    other_pack[:, at : at + width] = jnp.where(core == 0, halves[1], halves[0])


def feed_kernel(*refs):
    ids, tok, cot, live, gain, a0, a1, a2, a3 = refs[:9]
    held = refs[9:-10]
    (block, dmid, d_near, d_far, own_pack, other_pack, ggain, w_rest, w_in, sems) = refs[-10:]
    f, core, chip = ids[0], ids[2], ids[3]
    in_copies, rest_copies = load_halves(held, w_in, w_rest, core, chip, sems)
    tok_f = tok[...].astype(F32)
    pieces = [unpack_heads(a) for a in (a0[0], a1[1], a2[192:256, :], a3[256:320, :])]
    heads = [pl.ds(pl.multiple_of(192 * (f ^ k), 192), 192) for k in range(4)]
    for copy in rest_copies:
        copy.wait()
    left = jnp.zeros((256, 384), F32)
    right = jnp.zeros((256, 384), F32)
    for k in range(4):
        left += dot_nn(pieces[k], w_rest[0, heads[k], :384])
        right += dot_nn(pieces[k], w_rest[1, heads[k], :384])
    middle = tok_f + jnp.concatenate([left, right], axis=1)
    center = middle - jnp.mean(middle, axis=-1, keepdims=True)
    inverse = lax.rsqrt(jnp.mean(center * center, axis=-1, keepdims=True) + NORM_EPS)
    normed = center * inverse
    gain_row = gain[1:2, :]
    low = (normed * gain_row).astype(BF)
    own_pack[:, :768] = low
    other_pack[:, :768] = low
    for copy in in_copies:
        copy.wait()
    act = dot_nn(low, w_in[0])
    gate = dot_nn(low, w_in[1])
    cdf, density = erf_pair(act)
    gelu = act * cdf
    active = (gelu * gate).astype(BF)
    halves = [active[:, :640], jnp.concatenate([active[:, 640:], jnp.zeros((256, 128), BF)], axis=1)]
    store_half(own_pack, other_pack, 1920, halves, core)
    alive = live[...]
    dout = jnp.where(alive > 0.5, cot[...].astype(F32), 0.0)
    dym = dout.astype(BF)
    dact = jnp.concatenate([dot_nn(dym, w_rest[0, :, 384:1024]), dot_nn(dym, w_rest[1, :, 384:896])], axis=1)
    dg_front = (dact * gate * (cdf + act * density)).astype(BF)
    dg_rear = (dact * gelu).astype(BF)
    store_half(own_pack, other_pack, 768, [dg_front, dg_rear], core)
    dnormed = dot_nt(dg_front, w_in[0]) + dot_nt(dg_rear, w_in[1])
    ggain[...] = jnp.broadcast_to(jnp.sum(dnormed * normed, axis=0, keepdims=True), (8, 768))
    up = dnormed * gain_row
    dmiddle = dout + inverse * (
        up
        - jnp.mean(up, axis=-1, keepdims=True)
        - normed * jnp.mean(up * normed, axis=-1, keepdims=True)
    )
    dmid[...] = dmiddle
    dbranch = dmiddle.astype(BF)
    store_half(own_pack, other_pack, 2560, [dbranch[:, :384], dbranch[:, 384:]], core)
    for k in range(4):
        (d_near, d_far)[k // 2][k % 2] = pack_heads(
            (
                dot_nt(dbranch[:, :384], w_rest[0, heads[k], :384])
                + dot_nt(dbranch[:, 384:], w_rest[1, heads[k], :384])
            ).astype(BF)
        )
    branch = dot_nt(active[:, :640], w_rest[0, :, 384:1024]) + dot_nt(active[:, 640:], w_rest[1, :, 384:896])
    block[...] = jnp.where(alive > 0.5, middle + branch, 0.0).astype(BF)


def feed_forward(ids, tokens, cotangent, live, gain, att_pieces, held):
    return pl.pallas_call(
        feed_kernel,
        in_specs=[SMEM] + [VM] * 8 + [ANY] * len(held),
        out_specs=[VM] * 7,
        out_shape=[
            shaped((256, 768), BF),
            shaped((256, 768), F32),
            shaped((2, 64, 768), BF),
            shaped((2, 64, 768), BF),
            shaped((256, 2944), BF),
            shaped((256, 2944), BF),
            shaped((8, 768), F32),
        ],
        scratch_shapes=[
            pltpu.VMEM((2, 768, 1024), BF),
            pltpu.VMEM((2, 768, 1152), BF),
            pltpu.SemaphoreType.DMA((2, 40)),
        ],
        compiler_params=pltpu.CompilerParams(vmem_limit_bytes=VMEM_LIMIT),
        cost_estimate=pl.CostEstimate(flops=5 * 10**9, bytes_accessed=12 * 10**6, transcendentals=10**6),
        name="feed_forward",
    )(ids, tokens, cotangent, live, gain, *att_pieces, *held)


def grads_kernel(
    ids, cot, cot_c, live, live_c, own, came, near, near_c, by_x, by_x_c,
    lead_in, keep_in, lead_rest, keep_rest, g_in, g_rest, sems,
):
    f, chip = ids[0], ids[3]
    copies = []

    def store(grads, which, lead, keep, order):
        for slot, group in enumerate(order):
            for kz in range(4):
                at = pl.multiple_of(48 * (chip ^ (kz * 4 + group)), 48)
                target = lead.at[slot * 4 + kz] if slot < 2 else keep.at[slot * 4 + kz - 8]
                copies.append(pltpu.make_async_copy(grads.at[pl.ds(at, 48)], target, sems.at[which, slot * 4 + kz]))
                copies[-1].start()

    def both(first, last):
        return jnp.concatenate([own[:, first:last], came[:, first:last]], axis=0)

    g_in[...] = dot_tn(both(0, 768), both(768, 1920)).astype(BF)
    store(g_in, 0, lead_in, keep_in, (3, 1, 2, 0))
    dym = jnp.concatenate([jnp.where(alive[...] > 0.5, c[...].astype(F32), 0.0) for alive, c in ((live, cot), (live_c, cot_c))])
    g_rest[:, 384:] = dot_tn(dym.astype(BF), both(1920, 2560)).astype(BF)
    branch = both(2560, 2944)
    mine = (near[0], near_c[1], by_x[192:256, :], by_x_c[256:320, :])
    others = (near[1], near_c[0], by_x[256:320, :], by_x_c[192:256, :])
    for k in range(4):
        rows = pl.ds(pl.multiple_of(192 * (f ^ k), 192), 192)
        heads = jnp.concatenate([unpack_heads(mine[k]), unpack_heads(others[k])], axis=0)
        g_rest[rows, :384] = dot_tn(heads, branch).astype(BF)
    store(g_rest, 1, lead_rest, keep_rest, (3, 2, 1, 0))
    for copy in copies:
        copy.wait()


def feed_gradients(ids, *operands):
    return pl.pallas_call(
        grads_kernel,
        in_specs=[SMEM] + [VM] * len(operands),
        out_specs=[ANY] * 4,
        out_shape=[shaped((8, 48, width), BF) for width in (1152, 1152, 1024, 1024)],
        scratch_shapes=[
            pltpu.VMEM((768, 1152), BF),
            pltpu.VMEM((768, 1024), BF),
            pltpu.SemaphoreType.DMA((2, 16)),
        ],
        compiler_params=pltpu.CompilerParams(vmem_limit_bytes=VMEM_LIMIT),
        cost_estimate=pl.CostEstimate(flops=3 * 10**9, bytes_accessed=10**7, transcendentals=0),
        name="grads",
    )(ids, *operands)


def backward_kernel(*refs, base, blocks):
    resumed, last = base > 0, base + blocks == 4
    ids, t0, t1, t2, t3, cos, sin, q8, key, val, att, prob, d0, d1, gain, wide, ggain = refs[:17]
    refs = refs[17:]
    if blocks == 4:
        d2, d3, refs = refs[0], refs[1], refs[2:]
    if resumed:
        dq_in, dkt_in, dvt_in, refs = refs[0], refs[1], refs[2], refs[3:]
    if last:
        dn0, dn1, dn2, dn3, far, near, dq, dkt, dvt, n16, grads, sems = refs
    else:
        dq, dkt, dvt = refs
    step = pl.program_id(0)

    @pl.when(step == 0)
    def _():
        if resumed:
            dkt[...] = dkt_in[...]
            dvt[...] = dvt_in[...]
            dq[:512, :256] = dq_in[...]
        else:
            dkt[...] = jnp.zeros((256, 1024), F32)
            dvt[...] = jnp.zeros((256, 1024), F32)

    rows = pl.ds(pl.multiple_of((base + step) * 256, 256), 256)
    zero = jnp.zeros((), BF)
    keys = key[...]
    values = val[...]
    dattn = unpack_heads(d0[0])
    others = ((1, d1[1]),) if blocks == 2 else ((1, d1[1]), (2, d2[0]), (3, d3[1]))
    for i, piece in others:
        dattn = jnp.where(step == i, unpack_heads(piece), dattn)
    dattn = jnp.concatenate([dattn, jnp.zeros((256, 64), BF)], axis=1)
    product = dattn[:, :192].astype(F32) * att[...]
    queries_t = q8[rows, :].T
    dattn_t = dattn.T
    total = jnp.zeros((256, 256), F32)
    for h in range(3):
        weights = prob[h]
        dprob = dot_nt(jnp.where(value_lanes(256, h), dattn, zero), values)
        delta = jnp.sum(jnp.where(value_lanes(192, h), product, 0.0), axis=-1, keepdims=True)
        dscores = (weights.astype(F32) * (dprob - delta)).astype(BF)
        total += dot_nn(dscores, jnp.where(head_lanes(256, h), keys, zero))
        q_head = jnp.concatenate([queries_t[32 * h : 32 * h + 32], queries_t[128 + 32 * h : 160 + 32 * h]], axis=0)
        dk_head = dot_nn(q_head, dscores)
        dkt[32 * h : 32 * h + 32, :] += dk_head[:32]
        dkt[128 + 32 * h : 160 + 32 * h, :] += dk_head[32:]
        dvt[64 * h : 64 * h + 64, :] += dot_nn(dattn_t[64 * h : 64 * h + 64], weights)
    c, s = cos[rows, :], sin[rows, :]
    dqa, dqb = total[:, :128] * 0.125, total[:, 128:] * 0.125
    dq[rows, :128] = (dqa * c + dqb * s).astype(BF)
    dq[rows, 128:256] = (dqb * c - dqa * s).astype(BF)

    if not last:
        return

    @pl.when(step == blocks - 1)
    def _():
        dk = dkt[...].T
        ca, sa = cos[...], sin[...]
        dq[:, 256:384] = (dk[:, :128] * ca + dk[:, 128:] * sa).astype(BF)
        dq[:, 384:512] = (dk[:, 128:] * ca - dk[:, :128] * sa).astype(BF)
        dq[:, 512:768] = dvt[...].T.astype(BF)
        ggain1 = jnp.zeros((1, 768), F32)
        gain_row = gain[0:1, :]
        for i, (piece, out) in enumerate(((t0, dn0), (t1, dn1), (t2, dn2), (t3, dn3))):
            part = dot_nt(dq[256 * i : 256 * i + 256, :], wide[...])
            x = piece[...].astype(F32)
            center = x - jnp.mean(x, axis=-1, keepdims=True)
            inverse = lax.rsqrt(jnp.mean(center * center, axis=-1, keepdims=True) + NORM_EPS)
            normed = center * inverse
            n16[256 * i : 256 * i + 256, :] = (normed * gain_row).astype(BF)
            ggain1 += jnp.sum(part * normed, axis=0, keepdims=True)
            out[...] = part.astype(BF)
        gains = jnp.concatenate([ggain1, ggain[0:1, :], jnp.zeros((126, 768), F32)], axis=0)
        grads[...] = pack_columns(dot_tn(n16[...], dq[...]), gains.T[:, :64]).astype(BF)
        copies = []
        for ky, target in ((1, far), (0, near)):
            for kz in range(4):
                at = pl.multiple_of(96 * (ids[1] ^ (kz * 2 + ky)), 96)
                copies.append(
                    pltpu.make_async_copy(grads.at[pl.ds(at, 96)], target.at[kz], sems.at[len(copies)])
                )
                copies[-1].start()
        for copy in copies:
            copy.wait()


def backward_attention(
    ids, token_pieces, cos, sin, q8, key, val, att, prob, d_pieces, gain, wide, ggain, base=0, blocks=4, sums=()
):
    last = base + blocks == 4
    if last:
        out_specs = [full((256, 768))] * 4 + [ANY, ANY]
        out_shape = [shaped((256, 768), BF)] * 4 + [shaped((4, 96, 640), BF)] * 2
        scratch = [
            pltpu.VMEM((1024, 768), BF),
            pltpu.VMEM((256, 1024), F32),
            pltpu.VMEM((256, 1024), F32),
            pltpu.VMEM((1024, 768), BF),
            pltpu.VMEM((768, 640), BF),
            pltpu.SemaphoreType.DMA((8,)),
        ]
    else:
        out_specs = [full((512, 256)), full((256, 1024)), full((256, 1024))]
        out_shape = [shaped((512, 256), BF), shaped((256, 1024), F32), shaped((256, 1024), F32)]
        scratch = []
    sum_specs = [full((512, 256)), full((256, 1024)), full((256, 1024))] if sums else []
    return pl.pallas_call(
        functools.partial(backward_kernel, base=base, blocks=blocks),
        grid=(blocks,),
        in_specs=[SMEM]
        + [full((256, 768))] * 4
        + [full((1024, 128))] * 2
        + [full((1024, 256))] * 3
        + [pl.BlockSpec((256, 192), lambda i: (base + i, 0))]
        + [pl.BlockSpec((3, 256, 1024), lambda i: (0, base + i, 0))]
        + [full((2, 64, 768))] * 2
        + [full((8, 768)), full((768, 768)), full((8, 768))]
        + [full((2, 64, 768))] * (len(d_pieces) - 2)
        + sum_specs,
        out_specs=out_specs,
        out_shape=out_shape,
        scratch_shapes=scratch,
        compiler_params=pltpu.CompilerParams(vmem_limit_bytes=VMEM_LIMIT),
        cost_estimate=pl.CostEstimate(flops=2 * blocks * 10**9, bytes_accessed=16 * 10**6, transcendentals=0),
        name="backward_attention",
    )(ids, *token_pieces, cos, sin, q8, key, val, att, prob, *d_pieces[:2], gain, wide, ggain, *d_pieces[2:], *sums)


def sum_heads_kernel(ids, e0, e1, e2, e3, near, far):
    f = ids[0]
    total = e0[...].astype(F32) + e1[...].astype(F32) + e2[...].astype(F32) + e3[...].astype(F32)
    pieces = [total[24 * j : 24 * j + 24, :] for j in range(4)]
    for k, out in enumerate((near.at[0], near.at[1], far.at[0], far.at[1])):
        place = f ^ k
        low = jnp.where(place == 0, pieces[0], pieces[1])
        high = jnp.where(place == 2, pieces[2], pieces[3])
        out[...] = jnp.where(place < 2, low, high).astype(BF)


def sum_heads(ids, *pieces):
    return pl.pallas_call(
        sum_heads_kernel,
        in_specs=[SMEM] + [VM] * 4,
        out_specs=[VM] * 2,
        out_shape=[shaped((2, 24, 640), BF)] * 2,
        compiler_params=pltpu.CompilerParams(vmem_limit_bytes=VMEM_LIMIT),
        cost_estimate=pl.CostEstimate(flops=10**6, bytes_accessed=10**6, transcendentals=0),
        name="sum_heads",
    )(ids, *pieces)


def sum_rows_kernel(ids, a0, a1, a2, a3, b0, b1, b2, b3, mine, other):
    core = ids[2]
    one = a0[...].astype(F32) + a1[...].astype(F32) + a2[...].astype(F32) + a3[...].astype(F32)
    two = b0[...].astype(F32) + b1[...].astype(F32) + b2[...].astype(F32) + b3[...].astype(F32)
    rows = jnp.concatenate([one, two], axis=1)
    mine[...] = jnp.where(core == 0, rows[:24], rows[24:]).astype(BF)
    other[...] = jnp.where(core == 0, rows[24:], rows[:24]).astype(BF)


def sum_rows(ids, *pieces):
    return pl.pallas_call(
        sum_rows_kernel,
        in_specs=[SMEM] + [VM] * 8,
        out_specs=[VM] * 2,
        out_shape=[shaped((24, 2176), BF)] * 2,
        compiler_params=pltpu.CompilerParams(vmem_limit_bytes=VMEM_LIMIT),
        cost_estimate=pl.CostEstimate(flops=10**6, bytes_accessed=10**6, transcendentals=0),
        name="sum_rows",
    )(ids, *pieces)


def store_update(gradient, state, outs, rate):
    master, first, second, average = [ref[...] for ref in state]
    for out, value in zip(outs, adam_update(master, first, second, average, gradient, rate)):
        out[...] = value


def update_rows_kernel(ids, mine, came, *refs):
    core = ids[2]
    one, two = mine[...].astype(F32), came[...].astype(F32)
    left, right = jnp.where(core == 0, one, two), jnp.where(core == 0, two, one)
    grads = (
        jnp.concatenate([left[:, :1152], right[:, :1152]], axis=1),
        jnp.concatenate([left[:, 1152:1536], right[:, 1152:1536]], axis=1),
        jnp.concatenate([left[:, 1536:2176], right[:, 1536:2048]], axis=1),
    )
    for i, gradient in enumerate(grads):
        store_update(gradient, refs[4 * i : 4 * i + 4], refs[12 + 5 * i : 17 + 5 * i], MATRIX_RATE)


def update_rows(ids, mine, came, states):
    return pl.pallas_call(
        update_rows_kernel,
        in_specs=[SMEM] + [VM] * 14,
        out_specs=[VM] * 15,
        out_shape=[shaped((24, width), dtype) for width in (2304, 768, 1152) for dtype in (F32,) * 4 + (BF,)],
        compiler_params=pltpu.CompilerParams(vmem_limit_bytes=VMEM_LIMIT),
        cost_estimate=pl.CostEstimate(flops=10**7, bytes_accessed=4 * 10**6, transcendentals=10**5),
        name="update_rows",
    )(ids, mine, came, *[array for state in states for array in state])


def update_heads_kernel(ids, c0, c1, c2, c3, *refs):
    f = ids[0]
    pieces = [c[i].astype(F32) for c, i in ((c0, 0), (c1, 1), (c2, 0), (c3, 1))]
    ordered = []
    for place in range(4):
        k = f ^ place
        low = jnp.where(k == 0, pieces[0], pieces[1])
        high = jnp.where(k == 2, pieces[2], pieces[3])
        ordered.append(jnp.where(k < 2, low, high))
    parts = []
    for part in range(2):
        for piece in ordered:
            for h in range(3):
                parts += [piece[:, 192 * part + 96 * half + 32 * h : 192 * part + 96 * half + 32 * h + 32] for half in range(2)]
    gradient = jnp.concatenate(parts + [piece[:, 384:576] for piece in ordered], axis=1)
    store_update(gradient, refs[:4], refs[8:13], MATRIX_RATE)
    columns = sum(piece[:, 512:640] for piece in pieces)
    row = lax.broadcasted_iota(jnp.int32, (24, 24), 0)
    col = lax.broadcasted_iota(jnp.int32, (24, 24), 1)
    lines = [
        jnp.sum(jnp.where(row == col, columns[:, 64 + i : 65 + i], 0.0), axis=0, keepdims=True) for i in range(2)
    ]
    store_update(jnp.concatenate(lines, axis=0), refs[4:8], refs[13:18], GAIN_RATE)


def update_heads(ids, came, state, gain_state):
    return pl.pallas_call(
        update_heads_kernel,
        in_specs=[SMEM] + [VM] * 12,
        out_specs=[VM] * 10,
        out_shape=[shaped((24, 2304), dtype) for dtype in (F32,) * 4 + (BF,)]
        + [shaped((2, 24), dtype) for dtype in (F32,) * 4 + (BF,)],
        compiler_params=pltpu.CompilerParams(vmem_limit_bytes=VMEM_LIMIT),
        cost_estimate=pl.CostEstimate(flops=10**7, bytes_accessed=3 * 10**6, transcendentals=10**5),
        name="update_heads",
    )(ids, *came, *state, *gain_state)


def pack_layout(count_row, length_row, slots, own_place):
    devices_here = count_row.shape[0]
    places = jnp.arange(devices_here * slots, dtype=jnp.int32)
    holder = (places // slots) ^ own_place
    within = places % slots
    before = jnp.cumsum(count_row) - count_row
    choose = (holder[:, None] == jnp.arange(devices_here, dtype=jnp.int32)[None, :]).astype(jnp.int32)
    offset = jnp.sum(choose * before[None, :], axis=1) + within
    limits = jnp.sum(choose * count_row[None, :], axis=1)
    living = within < limits
    doc_ends = jnp.cumsum(length_row)
    passed = offset[:, None] >= doc_ends[None, :]
    document = jnp.sum(passed.astype(jnp.int32), axis=1)
    begins = jnp.max(jnp.where(passed, doc_ends[None, :], 0), axis=1)
    document = jnp.where(living, document, length_row.shape[0])
    position = jnp.where(living, offset - begins, 0)
    return document, position, living


def after(values, *signals):
    held = lax.optimization_barrier((tuple(values), signals))
    return list(held[0])


def fast_body(
    tokens, cotangent, counts, lengths,
    weight_qkv, weight_out, weight_in, weight_down, norm_gains,
    first_qkv, first_out, first_in, first_down, first_gains,
    second_qkv, second_out, second_in, second_down, second_gains,
    average_qkv, average_out, average_in, average_down, average_gains,
):
    slots = tokens.shape[0]
    group_row = lax.axis_index("dp")
    own_place = lax.axis_index("fsdp")
    core, side = own_place & 1, own_place >> 1
    chip = group_row * 2 + side
    ids = jnp.stack([own_place, group_row, core, chip]).astype(jnp.int32)

    def flag(name):
        return FL.get(name, 0)

    def exchange(near, far, direct=False):
        if direct:
            return [near, xperm(near, 1), xperm(far, 2), xperm(far, 3)]
        came = xperm(far, 2)
        return [near, xperm(near, 1), came, xperm(came, 1)]

    def pick(name, values, *signals):
        k = flag(name)
        if k == 0:
            return list(values)
        chosen = signals[k - 1]
        return after(values, *chosen)

    near, far, mine, other = prologue(ids, weight_qkv, weight_out, weight_in, weight_down, norm_gains)
    tok_c, cot_c = xperm(tokens, 1), xperm(cotangent, 1)
    rows_here, own_rows = assemble(ids, *exchange(near, far, flag("QX")), mine, xperm(other, 1))
    rows_z = [xperm(rows_here, 8), xperm(rows_here, 16), xperm(rows_here, 24)]
    rows_y = xperm(rows_here, 4)
    rows_z = jnp.stack(rows_z)
    rows_zy = xperm(rows_z, 4)
    w_pieces = [rows_here, rows_y, rows_z, rows_zy]
    (tokens_later,) = pick("H5", [tokens], (rows_here, tok_c), (rows_z,), (rows_y,))
    tok_x = xperm(tokens_later, 2)
    token_pieces = [tokens, tok_c, tok_x, xperm(tok_x, 1)]

    column0 = own_rows
    (own_rows,) = pick("H1", [own_rows], (rows_z, rows_y), (rows_z,), (rows_y,), (rows_zy,))
    column = [own_rows, xperm(own_rows, 8), xperm(own_rows, 16), xperm(own_rows, 24)]
    held = jnp.stack(column)

    count_row = lax.dynamic_index_in_dim(counts, group_row, 0, keepdims=False)
    length_row = lax.dynamic_index_in_dim(lengths, group_row, 0, keepdims=False)
    count_row, length_row = pick("H2", [count_row, length_row], (rows_here,), (rows_z,), (rows_zy,))
    docs, position, living = pack_layout(count_row, length_row, slots, own_place)
    speeds = ROTARY_BASE ** (-(jnp.arange(HD // 2, dtype=F32) * (2.0 / HD)))
    angles = position.astype(F32)[:, None] * jnp.tile(speeds, 4)[None, :]
    cos, sin = jnp.cos(angles), jnp.sin(angles)
    live, live_c = living[:slots, None].astype(F32), living[slots : 2 * slots, None].astype(F32)

    if flag("FS"):
        held_x, held_y = xperm(held, 2), xperm(held, 4)
        (cos_ready,) = pick("H3", [cos], (held,), (column[-1],))
        q8, key, val, gain, wide = project(ids, token_pieces, cos_ready, sin, w_pieces)
        (q8_ready,) = pick("H8", [q8], (held,), (column[0],), (column[0], column[1]))
        att, near, far, prob = attend(q8_ready, key, val, docs)
    else:
        held_x, held_y = xperm(held, 2), xperm(held, 4)
        (cos_ready,) = pick("H3", [cos], (held,), (column[-1],))
        q8, key, val, att, near, far, prob, gain, wide = forward_attention(
            ids, token_pieces, cos_ready, sin, docs, w_pieces
        )
    ready_x, ready_y = pick("H4", [held_x, held_y], (q8,), (near,))
    by_x = jnp.concatenate([ready_y[:, :, :768].reshape(192, 768), far.reshape(128, 768)], axis=0)
    (from_x,) = pick("H6", [ready_x], (near,), (by_x,))
    by_x, by_y = xperm(by_x, 2), xperm(from_x[:, :, 768:], 4)
    held = [held, held_x, held_y]
    held = pick("H7", held, (q8,), (near,), (by_x,))
    (near,) = pick("H9", [near], (by_x,), (by_y,))
    if flag("HC") == 1:
        pair = xperm(jnp.concatenate(held[1:], axis=0), 1)
        held_c = [xperm(held[0], 1), pair[:4], pair[4:]]
    elif flag("HC") == 2:
        trio = xperm(jnp.concatenate(held, axis=0), 1)
        held_c = [trio[:4], trio[4:8], trio[8:]]
    else:
        held_c = [xperm(piece, 1) for piece in held]
    by_x_c, by_y_c = xperm(by_x, 1), xperm(by_y, 1)
    att_pieces = [near, xperm(near, 1), by_x, by_x_c]
    held = held + [by_x, by_y] + held_c + [by_x_c, by_y_c]
    block_out, dmiddle, d_near, d_far, own_pack, other_pack, ggain = feed_forward(
        ids, tokens, cotangent, live, gain, att_pieces, held
    )
    d_pieces = exchange(d_near, d_far, flag("DX"))

    def add(*parts):
        total = parts[0].astype(F32)
        for part in parts[1:]:
            total = total + part.astype(F32)
        return total.astype(BF)

    def reduce_column(keep, one, two):
        pieces = [add(keep[4 + kz], one[kz], two[kz]) for kz in range(4)]
        if flag("ZM"):
            return pieces
        return [pieces[0]] + [xperm(pieces[kz], 8 * kz) for kz in (1, 2, 3)]

    (other_pack,) = pick("C2", [other_pack], (d_pieces[2],), (d_pieces[3],))
    came_pack = xperm(other_pack, 1)
    (pack_later,) = pick("C3", [own_pack], (d_pieces[2],), (d_pieces[3],), (d_pieces[1],))
    lead_in, keep_in, lead_rest, keep_rest = feed_gradients(
        ids, cotangent, cot_c, live, live_c, pack_later, came_pack, *att_pieces
    )
    along_x, along_y = xperm(lead_in, 2), xperm(lead_rest, 4)
    (key_later,) = pick("T3", [key], (lead_in,), (d_pieces[2], d_pieces[3]), (lead_in, d_pieces[2], d_pieces[3]))
    if flag("BS"):
        sums = backward_attention(
            ids, token_pieces, cos, sin, q8, key_later, val, att, prob, d_pieces[:2], gain, wide, ggain, 0, 2
        )
        (key_last,) = pick("T0", [key], (along_x,), (along_y,), (along_x, along_y))
        if flag("T5") >= 3:
            along_x, along_y = after([along_x, along_y], sums[0])
        if flag("T5") == 4:
            next_in = add(keep_in[:4], along_x[:4])
            next_rest = add(keep_rest[:4], along_y[:4])
            (key_last,) = after([key_last], next_in, next_rest)
        dn0, dn1, dn2, dn3, far, near = backward_attention(
            ids, token_pieces, cos, sin, q8, key_last, val, att, prob, d_pieces[2:], gain, wide, ggain, 2, 2, sums
        )
    else:
        dn0, dn1, dn2, dn3, far, near = backward_attention(
            ids, token_pieces, cos, sin, q8, key_later, val, att, prob, d_pieces, gain, wide, ggain
        )
    if flag("T5") in (1, 2):
        along_x, along_y = after([along_x, along_y], *((near,) if flag("T5") == 1 else (near, far)))
    (far,) = pick("T4", [far], (along_x, along_y), (along_x,), (along_y,))
    far_y = xperm(far, 4)
    next_in = add(keep_in[:4], along_x[:4])
    next_rest = add(keep_rest[:4], along_y[:4])
    next_in, next_rest = pick("T8", [next_in, next_rest], (far_y,))
    then_y, then_x = xperm(next_in, 4), xperm(next_rest, 2)
    (far_y,) = pick("TA", [far_y], (then_y, then_x), (then_x,), (then_y,))
    e = [add(near[kz], far_y[kz]) for kz in range(4)]
    heads = [e[0], xperm(e[1], 8), xperm(e[2], 16), xperm(e[3], 24)]
    then_x, = pick("Z1", [then_x], (e[1], e[2], e[3]), (heads[1],), (heads[1], heads[2], heads[3]))
    then_y, = pick("Z2", [then_y], (e[1], e[2], e[3]), (heads[1],), (heads[1], heads[2], heads[3]))
    column_in = reduce_column(keep_in, along_x[4:], then_y)
    column_rest = reduce_column(keep_rest, along_y[4:], then_x)
    if flag("ZM"):
        wide_z = [jnp.concatenate([column_in[kz], column_rest[kz]], axis=1) for kz in range(4)]
        wide_z = [wide_z[0]] + [xperm(wide_z[kz], 8 * kz) for kz in (1, 2, 3)]
        column_in = [piece[:, :1152] for piece in wide_z]
        column_rest = [piece[:, 1152:] for piece in wide_z]
    dn1, dn3 = pick("T6", [dn1, dn3], (far_y,), (then_x, then_y), (along_x, along_y), (e[1],))
    if flag("DM"):
        both = xperm(jnp.stack([dn1, dn3]), 1)
        dn1_came, dn3_came = both[0], both[1]
    else:
        dn1_came, dn3_came = xperm(dn1, 1), xperm(dn3, 1)
    x_sum = add(dn2, dn3_came)
    x_came = xperm(x_sum, 2)
    own_sum = add(dn0, dn1_came)
    heads = pick("T7", heads, (x_came,))
    mine, other = sum_rows(ids, *column_in, *column_rest)
    states = [
        (weight_in, first_in, second_in, average_in),
        (weight_out, first_out, second_out, average_out),
        (weight_down, first_down, second_down, average_down),
    ]
    new_rows = update_rows(ids, mine, xperm(other, 1), states)

    heads = pick("TC", heads, (new_rows[0],), (other,))
    came = exchange(*sum_heads(ids, *heads), flag("UX"))
    new_heads = update_heads(
        ids,
        came,
        (weight_qkv, first_qkv, second_qkv, average_qkv),
        (norm_gains, first_gains, second_gains, average_gains),
    )

    dnormed = own_sum.astype(F32) + x_came.astype(F32)
    normed, inverse = norm_parts(tokens.astype(F32))
    grad_tokens = dmiddle + norm_back(dnormed * gain[0:1, :], normed, inverse)

    updated = [new_heads[:5], new_rows[5:10], new_rows[:5], new_rows[10:], new_heads[5:]]
    return (block_out, grad_tokens) + tuple(updated[i][j] for j in range(5) for i in range(5))


def solution(mesh):
    sizes = dict(mesh.shape)
    body = fast_body if sizes == {"dp": 8, "fsdp": 4} else general_body
    rows, columns = P(("dp", "fsdp"), None), P(None, ("dp", "fsdp"))
    weights = (rows,) * 4 + (columns,)
    return jax.shard_map(
        body,
        mesh=mesh,
        in_specs=(rows, rows, P(), P()) + weights * 4,
        out_specs=(rows, rows) + weights * 5,
        check_vma=False,
    )
```

```python
import functools

import jax
import jax.numpy as jnp
from jax import lax
from jax.experimental import pallas as pl
from jax.experimental.pallas import tpu as pltpu
from jax.sharding import PartitionSpec as P

HEADS = 12
HD = 64
STEP = 6


NORM_EPS = 1e-05
ROTARY_BASE = 160000.0
BETA_FIRST = 0.5
BETA_SECOND = 0.5
ADAM_EPS = 1e-08
WEIGHT_DECAY = 0.01
MATRIX_RATE = 0.04
GAIN_RATE = 0.5
AVERAGE_KEEP = 0.6
MASKED = -1e30


def group_layout(count_row, length_row, slots):
    devices_here = count_row.shape[0]
    places = jnp.arange(devices_here * slots, dtype=jnp.int32)
    holder = places // slots
    within = places - holder * slots
    before = jnp.cumsum(count_row) - count_row
    choose = (holder[:, None] == jnp.arange(devices_here, dtype=jnp.int32)[None, :]).astype(
        jnp.int32
    )
    offset = jnp.sum(choose * before[None, :], axis=1) + within
    limits = jnp.sum(choose * count_row[None, :], axis=1)
    living = within < limits
    doc_ends = jnp.cumsum(length_row)
    passed = offset[:, None] >= doc_ends[None, :]
    document = jnp.sum(passed.astype(jnp.int32), axis=1)
    begins = jnp.max(jnp.where(passed, doc_ends[None, :], 0), axis=1)
    number_docs = length_row.shape[0]
    document = jnp.where(living, document, number_docs)
    position = jnp.where(living, offset - begins, 0)
    return (document, position, living)


def rotary_tables(position, head_size):
    half_size = head_size // 2
    speeds = ROTARY_BASE ** (-(jnp.arange(half_size, dtype=jnp.float32) * (2.0 / head_size)))
    angles = position.astype(jnp.float32)[:, None] * speeds[None, :]
    return (jnp.cos(angles), jnp.sin(angles))


def rotate(heads_in, cosine_table, sine_table):
    half_size = heads_in.shape[-1] // 2
    leading = heads_in[..., :half_size]
    latter = heads_in[..., half_size:]
    cos_wide = cosine_table[:, None, :]
    sin_wide = sine_table[:, None, :]
    return jnp.concatenate(
        [leading * cos_wide - latter * sin_wide, latter * cos_wide + leading * sin_wide], axis=-1
    )


def rotate_back(grads_in, cosine_table, sine_table):
    half_size = grads_in.shape[-1] // 2
    leading = grads_in[..., :half_size]
    latter = grads_in[..., half_size:]
    cos_wide = cosine_table[:, None, :]
    sin_wide = sine_table[:, None, :]
    return jnp.concatenate(
        [leading * cos_wide + latter * sin_wide, latter * cos_wide - leading * sin_wide], axis=-1
    )


def norm_parts(values_in):
    center = values_in - jnp.mean(values_in, axis=-1, keepdims=True)
    inverse = lax.rsqrt(jnp.mean(center * center, axis=-1, keepdims=True) + NORM_EPS)
    return (center * inverse, inverse)


def norm_back(upstream, normed, inverse):
    return inverse * (
        upstream
        - jnp.mean(upstream, axis=-1, keepdims=True)
        - normed * jnp.mean(upstream * normed, axis=-1, keepdims=True)
    )


def block_scores(queries, key_block, doc_query, doc_key, score_scale):
    scores = (
        jnp.einsum("qhd,khd->hqk", queries, key_block, preferred_element_type=jnp.float32)
        * score_scale
    )
    return jnp.where(doc_query[None, :, None] == doc_key[None, None, :], scores, MASKED)


def contract_rows(left_side, right_side):
    return lax.dot_general(
        left_side, right_side, (((0,), (0,)), ((), ())), preferred_element_type=jnp.float32
    )


def contract_cols(left_side, right_side):
    return lax.dot_general(
        left_side, right_side, (((1,), (1,)), ((), ())), preferred_element_type=jnp.float32
    )


def adam_update(master, first_old, second_old, average_old, gradient, step_rate):
    first_new = BETA_FIRST * first_old + (1.0 - BETA_FIRST) * gradient
    second_new = BETA_SECOND * second_old + (1.0 - BETA_SECOND) * gradient * gradient
    first_fix = first_new / (1.0 - BETA_FIRST**STEP)
    second_fix = second_new / (1.0 - BETA_SECOND**STEP)
    master_new = master - step_rate * (
        first_fix / (jnp.sqrt(second_fix) + ADAM_EPS) + WEIGHT_DECAY * master
    )
    average_new = AVERAGE_KEEP * average_old + (1.0 - AVERAGE_KEEP) * master_new
    return (first_new, second_new, master_new, average_new, master_new.astype(jnp.bfloat16))


def general_body(
    tokens,
    cotangent,
    counts,
    lengths,
    weight_qkv,
    weight_out,
    weight_in,
    weight_down,
    norm_gains,
    first_qkv,
    first_out,
    first_in,
    first_down,
    first_gains,
    second_qkv,
    second_out,
    second_in,
    second_down,
    second_gains,
    average_qkv,
    average_out,
    average_in,
    average_down,
    average_gains,
):
    slots = tokens.shape[0]
    model_width = tokens.shape[1]
    hidden_units = weight_down.shape[1]
    head_count = HEADS
    head_size = HD
    score_scale = 1.0 / head_size**0.5
    heads_shape = (slots, head_count, head_size)
    group_row = lax.axis_index("dp")
    own_place = lax.axis_index("fsdp")
    count_row = lax.dynamic_index_in_dim(counts, group_row, 0, keepdims=False)
    length_row = lax.dynamic_index_in_dim(lengths, group_row, 0, keepdims=False)
    doc_all, position_all, living_all = group_layout(count_row, length_row, slots)
    doc_mine = lax.dynamic_slice_in_dim(doc_all, own_place * slots, slots)
    position_mine = lax.dynamic_slice_in_dim(position_all, own_place * slots, slots)
    living_mine = lax.dynamic_slice_in_dim(living_all, own_place * slots, slots)
    cosine_table, sine_table = rotary_tables(position_mine, head_size)
    living_col = living_mine[:, None]
    copies = (
        weight_qkv.astype(jnp.bfloat16),
        weight_out.astype(jnp.bfloat16),
        weight_in.astype(jnp.bfloat16),
        weight_down.astype(jnp.bfloat16),
        norm_gains.astype(jnp.bfloat16),
    )
    qkv_full, out_full, in_full, down_full, gain_full = (
        lax.all_gather(copies[0], ("dp", "fsdp"), axis=0, tiled=True),
        lax.all_gather(copies[1], ("dp", "fsdp"), axis=0, tiled=True),
        lax.all_gather(copies[2], ("dp", "fsdp"), axis=0, tiled=True),
        lax.all_gather(copies[3], ("dp", "fsdp"), axis=0, tiled=True),
        lax.all_gather(copies[4], ("dp", "fsdp"), axis=1, tiled=True),
    )
    tokens_f = tokens.astype(jnp.float32)
    normed_one, inverse_one = norm_parts(tokens_f)
    gain_one = gain_full[0].astype(jnp.float32)
    gain_two = gain_full[1].astype(jnp.float32)
    normed1_low = (normed_one * gain_one).astype(jnp.bfloat16)
    mixed_qkv = jnp.dot(normed1_low, qkv_full, preferred_element_type=jnp.float32)
    queries16 = rotate(
        mixed_qkv[:, :model_width].reshape(heads_shape), cosine_table, sine_table
    ).astype(jnp.bfloat16)
    keys16 = rotate(
        mixed_qkv[:, model_width : 2 * model_width].reshape(heads_shape), cosine_table, sine_table
    ).astype(jnp.bfloat16)
    key_flat = keys16.reshape(slots, model_width)
    value_flat = mixed_qkv[:, 2 * model_width :].astype(jnp.bfloat16)
    key_rows, value_rows = (
        lax.all_gather(key_flat, "fsdp", axis=0, tiled=True),
        lax.all_gather(value_flat, "fsdp", axis=0, tiled=True),
    )
    group_rows = key_rows.shape[0]
    block_rows = 512
    count_blocks = group_rows // block_rows
    blocks_shape = (count_blocks, block_rows, head_count, head_size)
    doc_blocks = doc_all.reshape(count_blocks, block_rows)
    key_blocks = key_rows.reshape(blocks_shape)
    value_blocks = value_rows.reshape(blocks_shape)

    def max_sum(state_now, pieces):
        run_peak, run_total = state_now
        scores = block_scores(queries16, pieces[0], doc_mine, pieces[1], score_scale)
        new_peak = jnp.maximum(run_peak, jnp.max(scores, axis=-1))
        run_total = run_total * jnp.exp(run_peak - new_peak) + jnp.sum(
            jnp.exp(scores - new_peak[:, :, None]), axis=-1
        )
        return ((new_peak, run_total), None)

    start_state = (
        jnp.full((head_count, slots), MASKED, jnp.float32),
        jnp.zeros((head_count, slots), jnp.float32),
    )
    (run_peak, run_total), unused_max = lax.scan(max_sum, start_state, (key_blocks, doc_blocks))
    log_total = run_peak + jnp.log(run_total)

    def weigh_values(accum, pieces):
        scores = block_scores(queries16, pieces[0], doc_mine, pieces[2], score_scale)
        probs16 = jnp.exp(scores - log_total[:, :, None]).astype(jnp.bfloat16)
        return (
            accum
            + jnp.einsum("hqk,khd->qhd", probs16, pieces[1], preferred_element_type=jnp.float32),
            None,
        )

    attended, unused_out = lax.scan(
        weigh_values, jnp.zeros(heads_shape, jnp.float32), (key_blocks, value_blocks, doc_blocks)
    )
    attended16 = attended.reshape(slots, model_width).astype(jnp.bfloat16)
    middle = tokens_f + jnp.dot(attended16, out_full, preferred_element_type=jnp.float32)
    normed_two, inverse_two = norm_parts(middle)
    normed2_low = (normed_two * gain_two).astype(jnp.bfloat16)
    gate_up = jnp.dot(normed2_low, in_full, preferred_element_type=jnp.float32)
    act_half = gate_up[:, :hidden_units]
    gate_half = gate_up[:, hidden_units:]
    activated16 = (jax.nn.gelu(act_half, approximate=False) * gate_half).astype(jnp.bfloat16)
    branch_two = contract_cols(activated16, down_full)
    block_out = jnp.where(living_col, middle + branch_two, 0.0).astype(jnp.bfloat16)
    qkv_back, out_back, in_back, down_back, gain_back = (
        lax.all_gather(copies[0], ("dp", "fsdp"), axis=0, tiled=True),
        lax.all_gather(copies[1], ("dp", "fsdp"), axis=0, tiled=True),
        lax.all_gather(copies[2], ("dp", "fsdp"), axis=0, tiled=True),
        lax.all_gather(copies[3], ("dp", "fsdp"), axis=0, tiled=True),
        lax.all_gather(copies[4], ("dp", "fsdp"), axis=1, tiled=True),
    )
    key_again, value_again = (
        lax.all_gather(key_flat, "fsdp", axis=0, tiled=True),
        lax.all_gather(value_flat, "fsdp", axis=0, tiled=True),
    )
    gain_one_back = gain_back[0].astype(jnp.float32)
    gain_two_back = gain_back[1].astype(jnp.float32)
    dout = jnp.where(living_col, cotangent.astype(jnp.float32), 0.0)
    dym16 = dout.astype(jnp.bfloat16)
    grad_down = contract_rows(dym16, activated16)
    dact = jnp.dot(dym16, down_back, preferred_element_type=jnp.float32)
    unused_gate, gate_pull = jax.vjp(
        lambda front_part, rear_part: jax.nn.gelu(front_part, approximate=False) * rear_part,
        act_half,
        gate_half,
    )
    dfront, drear = gate_pull(dact)
    dgate16 = jnp.concatenate([dfront, drear], axis=1).astype(jnp.bfloat16)
    grad_in = contract_rows(normed2_low, dgate16)
    dnormed_two = contract_cols(dgate16, in_back)
    grad_gain_two = jnp.sum(dnormed_two * normed_two, axis=0)
    dmiddle = dout + norm_back(dnormed_two * gain_two_back, normed_two, inverse_two)
    dbranch16 = dmiddle.astype(jnp.bfloat16)
    grad_out = contract_rows(attended16, dbranch16)
    dattn16 = contract_cols(dbranch16, out_back).astype(jnp.bfloat16).reshape(heads_shape)
    row_delta = jnp.sum(dattn16.astype(jnp.float32) * attended, axis=-1).T
    back_keys = key_again.reshape(blocks_shape)
    back_values = value_again.reshape(blocks_shape)

    def back_block(dquery_sum, pieces):
        key_block, value_block, doc_block = pieces
        scores = block_scores(queries16, key_block, doc_mine, doc_block, score_scale)
        probs = jnp.exp(scores - log_total[:, :, None])
        probs16 = probs.astype(jnp.bfloat16)
        dvalue_block = jnp.einsum(
            "hqk,qhd->khd", probs16, dattn16, preferred_element_type=jnp.float32
        )
        dprobs = jnp.einsum(
            "qhd,khd->hqk", dattn16, value_block, preferred_element_type=jnp.float32
        )
        dscores16 = (probs * (dprobs - row_delta[:, :, None])).astype(jnp.bfloat16)
        dquery_sum = dquery_sum + jnp.einsum(
            "hqk,khd->qhd", dscores16, key_block, preferred_element_type=jnp.float32
        )
        dkey_block = jnp.einsum(
            "hqk,qhd->khd", dscores16, queries16, preferred_element_type=jnp.float32
        )
        return (dquery_sum, (dkey_block, dvalue_block))

    dquery_sum, (dkey_blocks, dvalue_blocks) = lax.scan(
        back_block, jnp.zeros(heads_shape, jnp.float32), (back_keys, back_values, doc_blocks)
    )
    dkey_mine, dvalue_mine = (
        lax.psum_scatter(
            (dkey_blocks.reshape(group_rows, model_width) * score_scale).astype(jnp.bfloat16),
            "fsdp",
            scatter_dimension=0,
            tiled=True,
        ).astype(jnp.float32),
        lax.psum_scatter(
            dvalue_blocks.reshape(group_rows, model_width).astype(jnp.bfloat16),
            "fsdp",
            scatter_dimension=0,
            tiled=True,
        ).astype(jnp.float32),
    )
    dquery_pre = rotate_back(dquery_sum * score_scale, cosine_table, sine_table).reshape(
        slots, model_width
    )
    dkey_pre = rotate_back(dkey_mine.reshape(heads_shape), cosine_table, sine_table).reshape(
        slots, model_width
    )
    dmixed16 = jnp.concatenate([dquery_pre, dkey_pre, dvalue_mine], axis=1).astype(jnp.bfloat16)
    grad_qkv = contract_rows(normed1_low, dmixed16)
    dnormed_one = contract_cols(dmixed16, qkv_back)
    grad_gain_one = jnp.sum(dnormed_one * normed_one, axis=0)
    grad_tokens = dmiddle + norm_back(dnormed_one * gain_one_back, normed_one, inverse_one)
    grad_gains = jnp.stack([grad_gain_one, grad_gain_two], axis=0)
    reduced = (
        lax.psum_scatter(grad_qkv, ("dp", "fsdp"), scatter_dimension=0, tiled=True),
        lax.psum_scatter(grad_out, ("dp", "fsdp"), scatter_dimension=0, tiled=True),
        lax.psum_scatter(grad_in, ("dp", "fsdp"), scatter_dimension=0, tiled=True),
        lax.psum_scatter(grad_down, ("dp", "fsdp"), scatter_dimension=0, tiled=True),
        lax.psum_scatter(grad_gains, ("dp", "fsdp"), scatter_dimension=1, tiled=True),
    )
    masters = (weight_qkv, weight_out, weight_in, weight_down, norm_gains)
    firsts = (first_qkv, first_out, first_in, first_down, first_gains)
    seconds = (second_qkv, second_out, second_in, second_down, second_gains)
    averages = (average_qkv, average_out, average_in, average_down, average_gains)
    rates = (MATRIX_RATE, MATRIX_RATE, MATRIX_RATE, MATRIX_RATE, GAIN_RATE)
    updated = [
        adam_update(
            masters[which],
            firsts[which],
            seconds[which],
            averages[which],
            reduced[which],
            rates[which],
        )
        for which in range(5)
    ]
    return (
        block_out,
        grad_tokens,
        updated[0][0],
        updated[1][0],
        updated[2][0],
        updated[3][0],
        updated[4][0],
        updated[0][1],
        updated[1][1],
        updated[2][1],
        updated[3][1],
        updated[4][1],
        updated[0][2],
        updated[1][2],
        updated[2][2],
        updated[3][2],
        updated[4][2],
        updated[0][3],
        updated[1][3],
        updated[2][3],
        updated[3][3],
        updated[4][3],
        updated[0][4],
        updated[1][4],
        updated[2][4],
        updated[3][4],
        updated[4][4],
    )


FL = {'H1': 3, 'H2': 2, 'H3': 2, 'H5': 1, 'H6': 1, 'H7': 2, 'QX': 1, 'DX': 1, 'T4': 1, 'TC': 1}
BF = jnp.bfloat16
F32 = jnp.float32
AXES = ("dp", "fsdp")
VMEM_LIMIT = 60 * 1024 * 1024


def xperm(value, mask):
    count = lax.axis_size("dp") * lax.axis_size("fsdp")
    return lax.ppermute(value, AXES, [(i, i ^ mask) for i in range(count)])


def dot_nn(a, b):
    return jnp.dot(a, b, preferred_element_type=F32)


def dot_nt(a, b):
    return lax.dot_general(a, b, (((1,), (1,)), ((), ())), preferred_element_type=F32)


def dot_tn(a, b):
    return lax.dot_general(a, b, (((0,), (0,)), ((), ())), preferred_element_type=F32)


def spread_columns(weight):
    rows = weight.shape[0]
    gap, end = jnp.zeros((rows, 32), weight.dtype), jnp.zeros((rows, 64), weight.dtype)
    parts = []
    for i in range(4):
        parts += [weight[:, 96 * i : 96 * i + 96], gap]
    return jnp.concatenate(parts + [weight[:, 384:576], end], axis=1)


def pack_columns(spread, last):
    return jnp.concatenate([spread[:, 128 * i : 128 * i + 96] for i in range(4)] + [spread[:, 512:704], last], axis=1)


def live_rows(count):
    return lax.broadcasted_iota(jnp.int32, (256, 1), 0) < count


def pack_heads(block):
    return jnp.concatenate([block[64 * i : 64 * i + 64] for i in range(4)], axis=1)


def unpack_heads(packed):
    return jnp.concatenate([packed[:, 192 * i : 192 * i + 192] for i in range(4)], axis=0)


def head_lanes(width, head):
    lane = lax.broadcasted_iota(jnp.int32, (1, width), 1) % 128
    return (lane >= 32 * head) & (lane < 32 * head + 32)


def value_lanes(width, head):
    lane = lax.broadcasted_iota(jnp.int32, (1, width), 1)
    return (lane >= 64 * head) & (lane < 64 * head + 64)


def prologue_kernel(ids, wq, w_out, w_in, w_down, gains, near, far, mine, other):
    f, core = ids[0] & 3, ids[0] & 1
    row = lax.broadcasted_iota(jnp.int32, (24, 24), 0)
    col = lax.broadcasted_iota(jnp.int32, (24, 24), 1)
    parts = []
    for j in range(2):
        spread = jnp.where(row == col, gains[j : j + 1, :], 0.0)
        parts.append(jnp.sum(spread, axis=-1, keepdims=True))
    lane = lax.broadcasted_iota(jnp.int32, (24, 64), 1)
    columns = jnp.where(lane == 0, parts[0], jnp.where(lane == 1, parts[1], 0.0))
    blocks = []
    for j in range(4):
        pieces = []
        for part in range(2):
            heads = wq[:, 768 * part + 192 * j : 768 * part + 192 * j + 192]
            pieces += [heads[:, 64 * h + 32 * half : 64 * h + 32 * half + 32] for half in range(2) for h in range(3)]
        blocks.append(jnp.concatenate(pieces + [wq[:, 1536 + 192 * j : 1728 + 192 * j], columns], axis=1))
    for k, out in enumerate((near.at[0], near.at[1], far.at[0], far.at[1])):
        place = f ^ k
        low = jnp.where(place == 0, blocks[0], blocks[1])
        high = jnp.where(place == 2, blocks[2], blocks[3])
        out[...] = jnp.where(place < 2, low, high).astype(BF)
    left = jnp.concatenate([w_out[:, :384], w_in[:, :1152], w_down[:, :640]], axis=1)
    right = jnp.concatenate([w_out[:, 384:], w_in[:, 1152:], w_down[:, 640:], jnp.zeros((24, 128), F32)], axis=1)
    mine[...] = jnp.where(core == 0, left, right).astype(BF)
    other[...] = jnp.where(core == 0, right, left).astype(BF)


def assemble_kernel(ids, q0, q1, q2, q3, mine, came, rows, other):
    f, core = ids[0] & 3, ids[0] & 1
    pieces = [q[i].astype(F32) for q, i in ((q0, 0), (q1, 1), (q2, 0), (q3, 1))]
    ordered = []
    for place in range(4):
        k = f ^ place
        low = jnp.where(k == 0, pieces[0], pieces[1])
        high = jnp.where(k == 2, pieces[2], pieces[3])
        ordered.append(jnp.where(k < 2, low, high))
    rows[...] = jnp.concatenate(ordered, axis=0).astype(BF)
    one, two = mine[...].astype(F32), came[...].astype(F32)
    other[...] = jnp.concatenate([jnp.where(core == 0, one, two), jnp.where(core == 0, two, one)], axis=0).astype(BF)


def forward_kernel(
    ids, t0, t1, t2, t3, cos, sin, docq, dock, w0, w1, w2, w3,
    q8, key, val, att, near, far, prob, gain, wide, wscr, sems,
):
    step = pl.program_id(0)

    @pl.when(step == 0)
    def _():
        copies = []
        pieces = (w0, w1, w2.at[0], w3.at[0], w2.at[1], w3.at[1], w2.at[2], w3.at[2])
        for k, piece in enumerate(pieces):
            at = pl.multiple_of(96 * ((ids[0] >> 2) ^ k), 96)
            copies.append(pltpu.make_async_copy(piece, wscr.at[pl.ds(at, 96)], sems.at[k]))
            copies[-1].start()
        for copy in copies:
            copy.wait()
        weight = wscr[...]
        wide[...] = spread_columns(weight)
        row = lax.broadcasted_iota(jnp.int32, (8, 640), 0)
        col = lax.broadcasted_iota(jnp.int32, (8, 640), 1)
        pick = ((col == row + 576) & (row < 2)).astype(F32).astype(BF)
        gain[...] = dot_nt(pick, weight)
        gain_row = gain[0:1, :]
        for i, piece in enumerate((t0, t1, t2, t3)):
            rows = slice(256 * i, 256 * i + 256)
            x = piece[...].astype(F32)
            center = x - jnp.mean(x, axis=-1, keepdims=True)
            inverse = lax.rsqrt(jnp.mean(center * center, axis=-1, keepdims=True) + NORM_EPS)
            mixed = dot_nn((center * inverse * gain_row).astype(BF), wide[...])
            c, s = cos[rows, :], sin[rows, :]
            qa, qb = mixed[:, :128], mixed[:, 128:256]
            ka, kb = mixed[:, 256:384], mixed[:, 384:512]
            q8[rows, :128] = ((qa * c - qb * s).astype(BF).astype(F32) * 0.125).astype(BF)
            q8[rows, 128:] = ((qb * c + qa * s).astype(BF).astype(F32) * 0.125).astype(BF)
            key[rows, :128] = (ka * c - kb * s).astype(BF)
            key[rows, 128:] = (kb * c + ka * s).astype(BF)
            val[rows, :] = mixed[:, 512:].astype(BF)

    rows = pl.ds(pl.multiple_of(step * 256, 256), 256)
    queries = q8[rows, :]
    keys = key[...]
    values = val[...]
    same = docq[rows, :] == dock[...]
    total = jnp.zeros((256, 256), F32)
    zero = jnp.zeros((), BF)
    for h in range(3):
        scores = dot_nt(jnp.where(head_lanes(256, h), queries, zero), keys)
        scores = jnp.where(same, scores, MASKED)
        peak = jnp.max(scores, axis=-1, keepdims=True)
        weights = jnp.exp(scores - peak)
        scale = 1.0 / jnp.sum(weights, axis=-1, keepdims=True)
        weights16 = (weights * scale).astype(BF)
        prob[h] = weights16
        total += dot_nn(weights16, jnp.where(value_lanes(256, h), values, zero))
    att[...] = total[:, :192]
    low = total[:, :192].astype(BF)

    @pl.when(step < 2)
    def _():
        near[0] = pack_heads(low)

    @pl.when(step >= 2)
    def _():
        far[0] = pack_heads(low)


def project_kernel(ids, t0, t1, t2, t3, cos, sin, w0, w1, w2, w3, q8, key, val, gain, wide, wscr, sems):
    copies = []
    pieces = (w0, w1, w2.at[0], w3.at[0], w2.at[1], w3.at[1], w2.at[2], w3.at[2])
    for k, piece in enumerate(pieces):
        at = pl.multiple_of(96 * ((ids[0] >> 2) ^ k), 96)
        copies.append(pltpu.make_async_copy(piece, wscr.at[pl.ds(at, 96)], sems.at[k]))
        copies[-1].start()
    for copy in copies:
        copy.wait()
    weight = wscr[...]
    wide[...] = spread_columns(weight)
    row = lax.broadcasted_iota(jnp.int32, (8, 640), 0)
    col = lax.broadcasted_iota(jnp.int32, (8, 640), 1)
    pick = ((col == row + 576) & (row < 2)).astype(F32).astype(BF)
    gain[...] = dot_nt(pick, weight)
    gain_row = gain[0:1, :]
    for i, piece in enumerate((t0, t1, t2, t3)):
        rows = slice(256 * i, 256 * i + 256)
        x = piece[...].astype(F32)
        center = x - jnp.mean(x, axis=-1, keepdims=True)
        inverse = lax.rsqrt(jnp.mean(center * center, axis=-1, keepdims=True) + NORM_EPS)
        mixed = dot_nn((center * inverse * gain_row).astype(BF), wide[...])
        c, s = cos[rows, :], sin[rows, :]
        qa, qb = mixed[:, :128], mixed[:, 128:256]
        ka, kb = mixed[:, 256:384], mixed[:, 384:512]
        q8[rows, :128] = ((qa * c - qb * s).astype(BF).astype(F32) * 0.125).astype(BF)
        q8[rows, 128:] = ((qb * c + qa * s).astype(BF).astype(F32) * 0.125).astype(BF)
        key[rows, :128] = (ka * c - kb * s).astype(BF)
        key[rows, 128:] = (kb * c + ka * s).astype(BF)
        val[rows, :] = mixed[:, 512:].astype(BF)


def attend_kernel(q8, key, val, docq, dock, att, near, far, prob):
    step = pl.program_id(0)
    rows = pl.ds(pl.multiple_of(step * 256, 256), 256)
    queries = q8[rows, :]
    keys = key[...]
    values = val[...]
    same = docq[rows, :] == dock[...]
    total = jnp.zeros((256, 256), F32)
    zero = jnp.zeros((), BF)
    for h in range(3):
        scores = dot_nt(jnp.where(head_lanes(256, h), queries, zero), keys)
        scores = jnp.where(same, scores, MASKED)
        peak = jnp.max(scores, axis=-1, keepdims=True)
        weights = jnp.exp(scores - peak)
        scale = 1.0 / jnp.sum(weights, axis=-1, keepdims=True)
        weights16 = (weights * scale).astype(BF)
        prob[h] = weights16
        total += dot_nn(weights16, jnp.where(value_lanes(256, h), values, zero))
    att[...] = total[:, :192]
    low = total[:, :192].astype(BF)

    @pl.when(step < 2)
    def _():
        near[0] = pack_heads(low)

    @pl.when(step >= 2)
    def _():
        far[0] = pack_heads(low)


def full(shape):
    return pl.BlockSpec(shape, lambda *_: (0,) * len(shape))


VM = pl.BlockSpec(memory_space=pltpu.VMEM)
SMEM = pl.BlockSpec(memory_space=pltpu.SMEM)
ANY = pl.BlockSpec(memory_space=pltpu.HBM)


def shaped(shape, dtype):
    return jax.ShapeDtypeStruct(shape, dtype)


def prologue(ids, weight_qkv, weight_out, weight_in, weight_down, norm_gains):
    return pl.pallas_call(
        prologue_kernel,
        in_specs=[SMEM] + [VM] * 5,
        out_specs=[VM] * 4,
        out_shape=[shaped((2, 24, 640), BF)] * 2 + [shaped((24, 2176), BF)] * 2,
        compiler_params=pltpu.CompilerParams(vmem_limit_bytes=VMEM_LIMIT),
        cost_estimate=pl.CostEstimate(flops=10**6, bytes_accessed=10**6, transcendentals=0),
        name="prologue",
    )(ids, weight_qkv, weight_out, weight_in, weight_down, norm_gains)


def assemble(ids, *pieces):
    return pl.pallas_call(
        assemble_kernel,
        in_specs=[SMEM] + [VM] * 6,
        out_specs=[VM] * 2,
        out_shape=[shaped((96, 640), BF), shaped((48, 2176), BF)],
        compiler_params=pltpu.CompilerParams(vmem_limit_bytes=VMEM_LIMIT),
        cost_estimate=pl.CostEstimate(flops=10**6, bytes_accessed=10**6, transcendentals=0),
        name="assemble",
    )(ids, *pieces)


def forward_attention(ids, token_pieces, cos, sin, docs, w_pieces):
    return pl.pallas_call(
        forward_kernel,
        grid=(4,),
        in_specs=[SMEM]
        + [full((256, 768))] * 4
        + [full((1024, 128))] * 2
        + [full((1024, 1)), full((1, 1024))]
        + [ANY] * 4,
        out_specs=[
            full((1024, 256)),
            full((1024, 256)),
            full((1024, 256)),
            pl.BlockSpec((256, 192), lambda i: (i, 0)),
            pl.BlockSpec((1, 64, 768), lambda i: (jnp.minimum(i, 1), 0, 0)),
            pl.BlockSpec((1, 64, 768), lambda i: (jnp.maximum(i - 2, 0), 0, 0)),
            pl.BlockSpec((3, 256, 1024), lambda i: (0, i, 0)),
            full((8, 768)),
            full((768, 768)),
        ],
        out_shape=[
            shaped((1024, 256), BF),
            shaped((1024, 256), BF),
            shaped((1024, 256), BF),
            shaped((1024, 192), F32),
            shaped((2, 64, 768), BF),
            shaped((2, 64, 768), BF),
            shaped((3, 1024, 1024), BF),
            shaped((8, 768), F32),
            shaped((768, 768), BF),
        ],
        scratch_shapes=[pltpu.VMEM((768, 640), BF), pltpu.SemaphoreType.DMA((8,))],
        compiler_params=pltpu.CompilerParams(vmem_limit_bytes=VMEM_LIMIT),
        cost_estimate=pl.CostEstimate(flops=6 * 10**9, bytes_accessed=16 * 10**6, transcendentals=3 * 10**6),
        name="forward_attention",
    )(ids, *token_pieces, cos, sin, docs[:, None], docs[None, :], *w_pieces)


def project(ids, token_pieces, cos, sin, w_pieces):
    return pl.pallas_call(
        project_kernel,
        in_specs=[SMEM] + [VM] * 6 + [ANY] * 4,
        out_specs=[VM] * 5,
        out_shape=[
            shaped((1024, 256), BF),
            shaped((1024, 256), BF),
            shaped((1024, 256), BF),
            shaped((8, 768), F32),
            shaped((768, 768), BF),
        ],
        scratch_shapes=[pltpu.VMEM((768, 640), BF), pltpu.SemaphoreType.DMA((8,))],
        compiler_params=pltpu.CompilerParams(vmem_limit_bytes=VMEM_LIMIT),
        cost_estimate=pl.CostEstimate(flops=3 * 10**9, bytes_accessed=8 * 10**6, transcendentals=0),
        name="project",
    )(ids, *token_pieces, cos, sin, *w_pieces)


def attend(q8, key, val, docs):
    return pl.pallas_call(
        attend_kernel,
        grid=(4,),
        in_specs=[full((1024, 256))] * 3 + [full((1024, 1)), full((1, 1024))],
        out_specs=[
            pl.BlockSpec((256, 192), lambda i: (i, 0)),
            pl.BlockSpec((1, 64, 768), lambda i: (jnp.minimum(i, 1), 0, 0)),
            pl.BlockSpec((1, 64, 768), lambda i: (jnp.maximum(i - 2, 0), 0, 0)),
            pl.BlockSpec((3, 256, 1024), lambda i: (0, i, 0)),
        ],
        out_shape=[
            shaped((1024, 192), F32),
            shaped((2, 64, 768), BF),
            shaped((2, 64, 768), BF),
            shaped((3, 1024, 1024), BF),
        ],
        compiler_params=pltpu.CompilerParams(vmem_limit_bytes=VMEM_LIMIT),
        cost_estimate=pl.CostEstimate(flops=3 * 10**9, bytes_accessed=8 * 10**6, transcendentals=3 * 10**6),
        name="attend",
    )(q8, key, val, docs[:, None], docs[None, :])


def erf_pair(x):
    cdf = 0.5 * (1.0 + lax.erf(x * (0.5**0.5)))
    density = jnp.exp(-0.5 * x * x) * (1.0 / (2.0 * 3.141592653589793) ** 0.5)
    return cdf, density


def load_halves(held, targets, core, chip, sems):
    groups = [[], []]
    early, held = held[: len(held) - 10], held[len(held) - 10 :]
    for which, columns in enumerate((pl.ds(0, 768), pl.ds(768, 1408))):
        for owner in range(2):
            half = core if owner == 0 else 1 - core
            arrays = held[owner * 5 : owner * 5 + 5]
            for group in range(4):
                for kz in range(4):
                    rows = pl.ds(pl.multiple_of(48 * (chip ^ (kz * 4 + group)), 48), 48)
                    if group == 3:
                        piece = arrays[4].at[kz] if which else arrays[3].at[pl.ds(48 * kz, 48)]
                    elif early:
                        piece = early[owner].at[group] if kz == 0 else arrays[group].at[kz - 1]
                        piece = piece.at[:, columns]
                    else:
                        piece = arrays[group].at[kz, :, columns]
                    sem = sems.at[which, len(groups[which])]
                    groups[which].append(pltpu.make_async_copy(piece, targets[which].at[half, rows], sem))
                    groups[which][-1].start()
    return groups


def store_half(own_pack, other_pack, at, halves, core):
    width = halves[0].shape[1]
    own_pack[:, at : at + width] = jnp.where(core == 0, halves[0], halves[1])
    other_pack[:, at : at + width] = jnp.where(core == 0, halves[1], halves[0])


def feed_kernel(*refs):
    ids, lives, tok, cot, gain, a0, a1, a2, a3 = refs[:9]
    held = refs[9:-10]
    (block, dmid, d_near, d_far, own_pack, other_pack, ggain, w_lead, w_rest, sems) = refs[-10:]
    f, core, chip = ids[0] & 3, ids[0] & 1, ids[0] >> 1
    lead_copies, rest_copies = load_halves(held, (w_lead, w_rest), core, chip, sems)
    tok_f = tok[...].astype(F32)
    pieces = [unpack_heads(a) for a in (a0[0], a1[1], a2[192:256, :], a3[256:320, :])]
    heads = [pl.ds(pl.multiple_of(192 * (f ^ k), 192), 192) for k in range(4)]
    for copy in lead_copies:
        copy.wait()
    left = jnp.zeros((256, 384), F32)
    right = jnp.zeros((256, 384), F32)
    for k in range(4):
        left += dot_nn(pieces[k], w_lead[0, heads[k], :384])
        right += dot_nn(pieces[k], w_lead[1, heads[k], :384])
    middle = tok_f + jnp.concatenate([left, right], axis=1)
    center = middle - jnp.mean(middle, axis=-1, keepdims=True)
    inverse = lax.rsqrt(jnp.mean(center * center, axis=-1, keepdims=True) + NORM_EPS)
    normed = center * inverse
    gain_row = gain[1:2, :]
    low = (normed * gain_row).astype(BF)
    own_pack[:, :768] = low
    other_pack[:, :768] = low
    for copy in rest_copies:
        copy.wait()
    act, gate = [
        jnp.concatenate([dot_nn(low, w_lead[h, :, 384:]), dot_nn(low, w_rest[h, :, :768])], axis=1) for h in range(2)
    ]
    cdf, density = erf_pair(act)
    gelu = act * cdf
    active = (gelu * gate).astype(BF)
    halves = [active[:, :640], jnp.concatenate([active[:, 640:], jnp.zeros((256, 128), BF)], axis=1)]
    store_half(own_pack, other_pack, 1920, halves, core)
    alive = live_rows(lives[0])
    dout = jnp.where(alive, cot[...].astype(F32), 0.0)
    dym = dout.astype(BF)
    dact = jnp.concatenate([dot_nn(dym, w_rest[0, :, 768:]), dot_nn(dym, w_rest[1, :, 768:1280])], axis=1)
    dg_front = (dact * gate * (cdf + act * density)).astype(BF)
    dg_rear = (dact * gelu).astype(BF)
    store_half(own_pack, other_pack, 768, [dg_front, dg_rear], core)
    dnormed = jnp.zeros((256, 768), F32)
    for h, part in enumerate((dg_front, dg_rear)):
        dnormed += dot_nt(part[:, :384], w_lead[h, :, 384:]) + dot_nt(part[:, 384:], w_rest[h, :, :768])
    ggain[...] = jnp.broadcast_to(jnp.sum(dnormed * normed, axis=0, keepdims=True), (8, 768))
    up = dnormed * gain_row
    dmiddle = dout + inverse * (
        up
        - jnp.mean(up, axis=-1, keepdims=True)
        - normed * jnp.mean(up * normed, axis=-1, keepdims=True)
    )
    dmid[...] = dmiddle
    dbranch = dmiddle.astype(BF)
    store_half(own_pack, other_pack, 2560, [dbranch[:, :384], dbranch[:, 384:]], core)
    for k in range(4):
        (d_near, d_far)[k // 2][k % 2] = pack_heads(
            (
                dot_nt(dbranch[:, :384], w_lead[0, heads[k], :384])
                + dot_nt(dbranch[:, 384:], w_lead[1, heads[k], :384])
            ).astype(BF)
        )
    branch = dot_nt(active[:, :640], w_rest[0, :, 768:]) + dot_nt(active[:, 640:], w_rest[1, :, 768:1280])
    block[...] = jnp.where(alive, middle + branch, 0.0).astype(BF)


def feed_forward(ids, lives, tokens, cotangent, gain, att_pieces, held):
    return pl.pallas_call(
        feed_kernel,
        in_specs=[SMEM] * 2 + [VM] * 7 + [ANY] * len(held),
        out_specs=[VM] * 7,
        out_shape=[
            shaped((256, 768), BF),
            shaped((256, 768), F32),
            shaped((2, 64, 768), BF),
            shaped((2, 64, 768), BF),
            shaped((256, 2944), BF),
            shaped((256, 2944), BF),
            shaped((8, 768), F32),
        ],
        scratch_shapes=[
            pltpu.VMEM((2, 768, 768), BF),
            pltpu.VMEM((2, 768, 1408), BF),
            pltpu.SemaphoreType.DMA((2, 32)),
        ],
        compiler_params=pltpu.CompilerParams(vmem_limit_bytes=VMEM_LIMIT),
        cost_estimate=pl.CostEstimate(flops=5 * 10**9, bytes_accessed=12 * 10**6, transcendentals=10**6),
        name="feed_forward",
    )(ids, lives, tokens, cotangent, gain, *att_pieces, *held)


def grads_kernel(
    ids, lives, cot, cot_c, own, came, near, near_c, by_x, by_x_c,
    lead_in, keep_in, lead_rest, keep_rest, g_in, g_rest, sems,
):
    f, chip = ids[0] & 3, ids[0] >> 1
    copies = []

    def store(grads, which, lead, keep, order):
        for slot, group in enumerate(order):
            for kz in range(4):
                at = pl.multiple_of(48 * (chip ^ (kz * 4 + group)), 48)
                target = lead.at[slot * 4 + kz] if slot < 2 else keep.at[slot * 4 + kz - 8]
                copies.append(pltpu.make_async_copy(grads.at[pl.ds(at, 48)], target, sems.at[which, slot * 4 + kz]))
                copies[-1].start()

    def both(first, last):
        return jnp.concatenate([own[:, first:last], came[:, first:last]], axis=0)

    g_in[...] = dot_tn(both(0, 768), both(768, 1920)).astype(BF)
    store(g_in, 0, lead_in, keep_in, (3, 2, 1, 0))
    dym = jnp.concatenate([jnp.where(live_rows(lives[i]), c[...].astype(F32), 0.0) for i, c in enumerate((cot, cot_c))])
    g_rest[:, 384:] = dot_tn(dym.astype(BF), both(1920, 2560)).astype(BF)
    branch = both(2560, 2944)
    mine = (near[0], near_c[1], by_x[192:256, :], by_x_c[256:320, :])
    others = (near[1], near_c[0], by_x[256:320, :], by_x_c[192:256, :])
    for k in range(4):
        rows = pl.ds(pl.multiple_of(192 * (f ^ k), 192), 192)
        heads = jnp.concatenate([unpack_heads(mine[k]), unpack_heads(others[k])], axis=0)
        g_rest[rows, :384] = dot_tn(heads, branch).astype(BF)
    store(g_rest, 1, lead_rest, keep_rest, (3, 1, 2, 0))
    for copy in copies:
        copy.wait()


def feed_gradients(ids, lives, *operands):
    return pl.pallas_call(
        grads_kernel,
        in_specs=[SMEM] * 2 + [VM] * len(operands),
        out_specs=[ANY] * 4,
        out_shape=[shaped((8, 48, width), BF) for width in (1152, 1152, 1024, 1024)],
        scratch_shapes=[
            pltpu.VMEM((768, 1152), BF),
            pltpu.VMEM((768, 1024), BF),
            pltpu.SemaphoreType.DMA((2, 16)),
        ],
        compiler_params=pltpu.CompilerParams(vmem_limit_bytes=VMEM_LIMIT),
        cost_estimate=pl.CostEstimate(flops=3 * 10**9, bytes_accessed=10**7, transcendentals=0),
        name="grads",
    )(ids, lives, *operands)


def backward_kernel(
    ids, q8, key, val, att, prob, d0, d1, d2, d3, gain, ggain, t0_far, t1_far, t2_far, t3_far, cos_far, sin_far, wide_far,
    dn_keep, dn_sent, far, near,
    dqf, dq, dkt, dvt, n16, grads, t0, t1, t2, t3, cos, sin, wide, sems, late_sems,
):
    step = pl.program_id(0)
    late = ((t0_far, t0), (t1_far, t1), (t2_far, t2), (t3_far, t3), (cos_far, cos), (sin_far, sin), (wide_far, wide))
    loads = [pltpu.make_async_copy(a, b, late_sems.at[i]) for i, (a, b) in enumerate(late)]

    @pl.when(step == 0)
    def _():
        for load in loads:
            load.start()
        dkt[...] = jnp.zeros((256, 1024), F32)
        dvt[...] = jnp.zeros((256, 1024), F32)

    rows = pl.ds(pl.multiple_of(step * 256, 256), 256)
    zero = jnp.zeros((), BF)
    keys = key[...]
    values = val[...]
    dattn = unpack_heads(d0[0])
    for i, piece in ((1, d1[1]), (2, d2[0]), (3, d3[1])):
        dattn = jnp.where(step == i, unpack_heads(piece), dattn)
    dattn = jnp.concatenate([dattn, jnp.zeros((256, 64), BF)], axis=1)
    product = dattn[:, :192].astype(F32) * att[...]
    queries_t = q8[rows, :].T
    dattn_t = dattn.T
    total = jnp.zeros((256, 256), F32)
    for h in range(3):
        weights = prob[h]
        dprob = dot_nt(jnp.where(value_lanes(256, h), dattn, zero), values)
        delta = jnp.sum(jnp.where(value_lanes(192, h), product, 0.0), axis=-1, keepdims=True)
        dscores = (weights.astype(F32) * (dprob - delta)).astype(BF)
        total += dot_nn(dscores, jnp.where(head_lanes(256, h), keys, zero))
        q_head = jnp.concatenate([queries_t[32 * h : 32 * h + 32], queries_t[128 + 32 * h : 160 + 32 * h]], axis=0)
        dk_head = dot_nn(q_head, dscores)
        dkt[32 * h : 32 * h + 32, :] += dk_head[:32]
        dkt[128 + 32 * h : 160 + 32 * h, :] += dk_head[32:]
        dvt[64 * h : 64 * h + 64, :] += dot_nn(dattn_t[64 * h : 64 * h + 64], weights)
    dqf[rows, :] = total * 0.125

    @pl.when(step == 3)
    def _():
        for load in loads:
            load.wait()
        dk = dkt[...].T
        c, s = cos[...], sin[...]
        dq[:, :128] = (dqf[:, :128] * c + dqf[:, 128:] * s).astype(BF)
        dq[:, 128:256] = (dqf[:, 128:] * c - dqf[:, :128] * s).astype(BF)
        dq[:, 256:384] = (dk[:, :128] * c + dk[:, 128:] * s).astype(BF)
        dq[:, 384:512] = (dk[:, 128:] * c - dk[:, :128] * s).astype(BF)
        dq[:, 512:768] = dvt[...].T.astype(BF)
        ggain1 = jnp.zeros((1, 768), F32)
        gain_row = gain[0:1, :]
        for i, (piece, out) in enumerate(((t0, dn_keep.at[0]), (t1, dn_sent.at[0]), (t2, dn_keep.at[1]), (t3, dn_sent.at[1]))):
            part = dot_nt(dq[256 * i : 256 * i + 256, :], wide[...])
            x = piece[...].astype(F32)
            center = x - jnp.mean(x, axis=-1, keepdims=True)
            inverse = lax.rsqrt(jnp.mean(center * center, axis=-1, keepdims=True) + NORM_EPS)
            normed = center * inverse
            n16[256 * i : 256 * i + 256, :] = (normed * gain_row).astype(BF)
            ggain1 += jnp.sum(part * normed, axis=0, keepdims=True)
            out[...] = part.astype(BF)
        gains = jnp.concatenate([ggain1, ggain[0:1, :], jnp.zeros((126, 768), F32)], axis=0)
        grads[...] = pack_columns(dot_tn(n16[...], dq[...]), gains.T[:, :64]).astype(BF)
        copies = []
        for ky, target in ((1, far), (0, near)):
            for kz in range(4):
                at = pl.multiple_of(96 * ((ids[0] >> 2) ^ (kz * 2 + ky)), 96)
                copies.append(
                    pltpu.make_async_copy(grads.at[pl.ds(at, 96)], target.at[kz], sems.at[len(copies)])
                )
                copies[-1].start()
        for copy in copies:
            copy.wait()


def backward_attention(ids, token_pieces, cos, sin, q8, key, val, att, prob, d_pieces, gain, wide, ggain):
    return pl.pallas_call(
        backward_kernel,
        grid=(4,),
        in_specs=[SMEM]
        + [full((1024, 256))] * 3
        + [pl.BlockSpec((256, 192), lambda i: (i, 0))]
        + [pl.BlockSpec((3, 256, 1024), lambda i: (0, i, 0))]
        + [full((2, 64, 768))] * 4
        + [full((8, 768))] * 2
        + [ANY] * 7,
        out_specs=[full((2, 256, 768))] * 2 + [ANY, ANY],
        out_shape=[shaped((2, 256, 768), BF)] * 2 + [shaped((4, 96, 640), BF)] * 2,
        scratch_shapes=[
            pltpu.VMEM((1024, 256), F32),
            pltpu.VMEM((1024, 768), BF),
            pltpu.VMEM((256, 1024), F32),
            pltpu.VMEM((256, 1024), F32),
            pltpu.VMEM((1024, 768), BF),
            pltpu.VMEM((768, 640), BF),
        ]
        + [pltpu.VMEM((256, 768), BF)] * 4
        + [pltpu.VMEM((1024, 128), F32)] * 2
        + [pltpu.VMEM((768, 768), BF), pltpu.SemaphoreType.DMA((8,)), pltpu.SemaphoreType.DMA((7,))],
        compiler_params=pltpu.CompilerParams(vmem_limit_bytes=VMEM_LIMIT),
        cost_estimate=pl.CostEstimate(flops=8 * 10**9, bytes_accessed=16 * 10**6, transcendentals=0),
        name="backward_attention",
    )(ids, q8, key, val, att, prob, *d_pieces, gain, ggain, *token_pieces, cos, sin, wide)


def sum_heads_kernel(ids, e0, e1, e2, e3, near, far):
    f = ids[0] & 3
    total = e0[...].astype(F32) + e1[...].astype(F32) + e2[...].astype(F32) + e3[...].astype(F32)
    pieces = [total[24 * j : 24 * j + 24, :] for j in range(4)]
    for k, out in enumerate((near.at[0], near.at[1], far.at[0], far.at[1])):
        place = f ^ k
        low = jnp.where(place == 0, pieces[0], pieces[1])
        high = jnp.where(place == 2, pieces[2], pieces[3])
        out[...] = jnp.where(place < 2, low, high).astype(BF)


def sum_heads(ids, *pieces):
    return pl.pallas_call(
        sum_heads_kernel,
        in_specs=[SMEM] + [VM] * 4,
        out_specs=[VM] * 2,
        out_shape=[shaped((2, 24, 640), BF)] * 2,
        compiler_params=pltpu.CompilerParams(vmem_limit_bytes=VMEM_LIMIT),
        cost_estimate=pl.CostEstimate(flops=10**6, bytes_accessed=10**6, transcendentals=0),
        name="sum_heads",
    )(ids, *pieces)


def sum_rows_kernel(ids, a0, a1, a2, a3, b0, b1, b2, b3, mine, other):
    core = ids[0] & 1
    one = a0[...].astype(F32) + a1[...].astype(F32) + a2[...].astype(F32) + a3[...].astype(F32)
    two = b0[...].astype(F32) + b1[...].astype(F32) + b2[...].astype(F32) + b3[...].astype(F32)
    rows = jnp.concatenate([one, two], axis=1)
    mine[...] = jnp.where(core == 0, rows[:24], rows[24:]).astype(BF)
    other[...] = jnp.where(core == 0, rows[24:], rows[:24]).astype(BF)


def sum_rows(ids, *pieces):
    return pl.pallas_call(
        sum_rows_kernel,
        in_specs=[SMEM] + [VM] * 8,
        out_specs=[VM] * 2,
        out_shape=[shaped((24, 2176), BF)] * 2,
        compiler_params=pltpu.CompilerParams(vmem_limit_bytes=VMEM_LIMIT),
        cost_estimate=pl.CostEstimate(flops=10**6, bytes_accessed=10**6, transcendentals=0),
        name="sum_rows",
    )(ids, *pieces)


def store_update(gradient, state, outs, rate):
    master, first, second, average = [ref[...] for ref in state]
    for out, value in zip(outs, adam_update(master, first, second, average, gradient, rate)):
        out[...] = value


def update_rows_kernel(ids, mine, came, *refs):
    core = ids[0] & 1
    one, two = mine[...].astype(F32), came[...].astype(F32)
    left, right = jnp.where(core == 0, one, two), jnp.where(core == 0, two, one)
    grads = (
        jnp.concatenate([left[:, :1152], right[:, :1152]], axis=1),
        jnp.concatenate([left[:, 1152:1536], right[:, 1152:1536]], axis=1),
        jnp.concatenate([left[:, 1536:2176], right[:, 1536:2048]], axis=1),
    )
    for i, gradient in enumerate(grads):
        store_update(gradient, refs[4 * i : 4 * i + 4], refs[12 + 5 * i : 17 + 5 * i], MATRIX_RATE)


def update_rows(ids, mine, came, states):
    return pl.pallas_call(
        update_rows_kernel,
        in_specs=[SMEM] + [VM] * 14,
        out_specs=[VM] * 15,
        out_shape=[shaped((24, width), dtype) for width in (2304, 768, 1152) for dtype in (F32,) * 4 + (BF,)],
        compiler_params=pltpu.CompilerParams(vmem_limit_bytes=VMEM_LIMIT),
        cost_estimate=pl.CostEstimate(flops=10**7, bytes_accessed=4 * 10**6, transcendentals=10**5),
        name="update_rows",
    )(ids, mine, came, *[array for state in states for array in state])


def update_heads_kernel(ids, c0, c1, c2, c3, *refs):
    f = ids[0] & 3
    pieces = [c[i].astype(F32) for c, i in ((c0, 0), (c1, 1), (c2, 0), (c3, 1))]
    ordered = []
    for place in range(4):
        k = f ^ place
        low = jnp.where(k == 0, pieces[0], pieces[1])
        high = jnp.where(k == 2, pieces[2], pieces[3])
        ordered.append(jnp.where(k < 2, low, high))
    parts = []
    for part in range(2):
        for piece in ordered:
            for h in range(3):
                parts += [piece[:, 192 * part + 96 * half + 32 * h : 192 * part + 96 * half + 32 * h + 32] for half in range(2)]
    gradient = jnp.concatenate(parts + [piece[:, 384:576] for piece in ordered], axis=1)
    store_update(gradient, refs[:4], refs[8:13], MATRIX_RATE)
    columns = sum(piece[:, 512:640] for piece in pieces)
    row = lax.broadcasted_iota(jnp.int32, (24, 24), 0)
    col = lax.broadcasted_iota(jnp.int32, (24, 24), 1)
    lines = [
        jnp.sum(jnp.where(row == col, columns[:, 64 + i : 65 + i], 0.0), axis=0, keepdims=True) for i in range(2)
    ]
    store_update(jnp.concatenate(lines, axis=0), refs[4:8], refs[13:18], GAIN_RATE)


def update_heads(ids, came, state, gain_state):
    return pl.pallas_call(
        update_heads_kernel,
        in_specs=[SMEM] + [VM] * 12,
        out_specs=[VM] * 10,
        out_shape=[shaped((24, 2304), dtype) for dtype in (F32,) * 4 + (BF,)]
        + [shaped((2, 24), dtype) for dtype in (F32,) * 4 + (BF,)],
        compiler_params=pltpu.CompilerParams(vmem_limit_bytes=VMEM_LIMIT),
        cost_estimate=pl.CostEstimate(flops=10**7, bytes_accessed=3 * 10**6, transcendentals=10**5),
        name="update_heads",
    )(ids, *came, *state, *gain_state)


def pack_layout(count_row, length_row, slots, own_place):
    devices_here = count_row.shape[0]
    places = jnp.arange(devices_here * slots, dtype=jnp.int32)
    holder = (places // slots) ^ own_place
    within = places % slots
    before = jnp.cumsum(count_row) - count_row
    choose = (holder[:, None] == jnp.arange(devices_here, dtype=jnp.int32)[None, :]).astype(jnp.int32)
    offset = jnp.sum(choose * before[None, :], axis=1) + within
    limits = jnp.sum(choose * count_row[None, :], axis=1)
    living = within < limits
    doc_ends = jnp.cumsum(length_row)
    passed = offset[:, None] >= doc_ends[None, :]
    document = jnp.sum(passed.astype(jnp.int32), axis=1)
    begins = jnp.max(jnp.where(passed, doc_ends[None, :], 0), axis=1)
    document = jnp.where(living, document, length_row.shape[0])
    position = jnp.where(living, offset - begins, 0)
    return document, position, living


def after(values, *signals):
    held = lax.optimization_barrier((tuple(values), signals))
    return list(held[0])


def fast_body(
    tokens, cotangent, counts, lengths,
    weight_qkv, weight_out, weight_in, weight_down, norm_gains,
    first_qkv, first_out, first_in, first_down, first_gains,
    second_qkv, second_out, second_in, second_down, second_gains,
    average_qkv, average_out, average_in, average_down, average_gains,
):
    slots = tokens.shape[0]
    group_row = lax.axis_index("dp")
    own_place = lax.axis_index("fsdp")
    core, side = own_place & 1, own_place >> 1
    chip = group_row * 2 + side
    count_row = lax.dynamic_index_in_dim(counts, group_row, 0, keepdims=False)
    length_row = lax.dynamic_index_in_dim(lengths, group_row, 0, keepdims=False)
    own_count = lax.dynamic_index_in_dim(count_row, own_place, 0, keepdims=False)
    core_count = lax.dynamic_index_in_dim(count_row, own_place ^ 1, 0, keepdims=False)
    ids = lax.axis_index(AXES).astype(jnp.int32).reshape(1)
    lives = jnp.stack([own_count, core_count])

    def flag(name):
        return FL.get(name, 0)

    def exchange(near, far, direct=False):
        if direct:
            return [near, xperm(near, 1), xperm(far, 2), xperm(far, 3)]
        came = xperm(far, 2)
        return [near, xperm(near, 1), came, xperm(came, 1)]

    def pick(name, values, *signals):
        k = flag(name)
        if k == 0:
            return list(values)
        chosen = signals[k - 1]
        return after(values, *chosen)

    near, far, mine, other = prologue(ids, weight_qkv, weight_out, weight_in, weight_down, norm_gains)
    tok_c, cot_c = xperm(tokens, 1), xperm(cotangent, 1)
    rows_here, own_rows = assemble(ids, *exchange(near, far, flag("QX")), mine, xperm(other, 1))
    rows_z = [xperm(rows_here, 8), xperm(rows_here, 16), xperm(rows_here, 24)]
    rows_y = xperm(rows_here, 4)
    rows_z = jnp.stack(rows_z)
    rows_zy = xperm(rows_z, 4)
    w_pieces = [rows_here, rows_y, rows_z, rows_zy]
    (tokens_later,) = pick("H5", [tokens], (rows_here, tok_c), (rows_z,), (rows_y,))
    tok_x = xperm(tokens_later, 2)
    token_pieces = [tokens, tok_c, tok_x, xperm(tok_x, 1)]

    column0 = own_rows
    rows_unmarked = own_rows
    (own_rows,) = pick("H1", [own_rows], (rows_z, rows_y), (rows_z,), (rows_y,), (rows_zy,))
    column = [own_rows, xperm(own_rows, 8), xperm(own_rows, 16), xperm(own_rows, 24)]
    if flag("EP"):
        (rows_first,) = pick("E1", [rows_unmarked], (rows_y,), (rows_z[:1],), (tok_c,))
        early_x = xperm(rows_first, 2)
        (rows_first,) = pick("E2", [rows_first], (rows_y,), (early_x,), (rows_z[:1],))
        early_y = xperm(rows_first, 4)
        trio = jnp.stack([rows_unmarked, early_x, early_y])
        (trio,) = pick("E3", [trio], (column[3],), (rows_zy,))
        column = column[1:]
    held = jnp.stack(column)

    count_row, length_row = pick("H2", [count_row, length_row], (rows_here,), (rows_z,), (rows_zy,))
    docs, position, _ = pack_layout(count_row, length_row, slots, own_place)
    speeds = ROTARY_BASE ** (-(jnp.arange(HD // 2, dtype=F32) * (2.0 / HD)))
    angles = position.astype(F32)[:, None] * jnp.tile(speeds, 4)[None, :]
    cos, sin = jnp.cos(angles), jnp.sin(angles)

    if flag("FS"):
        held_x, held_y = xperm(held, 2), xperm(held, 4)
        (cos_ready,) = pick("H3", [cos], (held,), (column[-1],))
        q8, key, val, gain, wide = project(ids, token_pieces, cos_ready, sin, w_pieces)
        (q8_ready,) = pick("H8", [q8], (held,), (column[0],), (column[0], column[1]))
        att, near, far, prob = attend(q8_ready, key, val, docs)
    else:
        held_x, held_y = xperm(held, 2), xperm(held, 4)
        (cos_ready,) = pick("H3", [cos], (held,), (column[-1],))
        q8, key, val, att, near, far, prob, gain, wide = forward_attention(
            ids, token_pieces, cos_ready, sin, docs, w_pieces
        )
    ready_x, ready_y = pick("H4", [held_x, held_y], (q8,), (near,))
    if flag("EP"):
        front = [early_y[:, :768], ready_y[:, :, :768].reshape(144, 768)]
        by_x = jnp.concatenate(front + [far.reshape(128, 768)], axis=0)
        (from_x,) = pick("H6", [ready_x], (near,), (by_x,))
        by_y = jnp.concatenate([early_x[None, :, 768:], from_x[:, :, 768:]], axis=0)
        by_x, by_y = xperm(by_x, 2), xperm(by_y, 4)
    else:
        by_x = jnp.concatenate([ready_y[:, :, :768].reshape(192, 768), far.reshape(128, 768)], axis=0)
        (from_x,) = pick("H6", [ready_x], (near,), (by_x,))
        by_x, by_y = xperm(by_x, 2), xperm(from_x[:, :, 768:], 4)
    held = [held, held_x, held_y]
    held = pick("H7", held, (q8,), (near,), (by_x,))
    (near,) = pick("H9", [near], (by_x,), (by_y,))
    if flag("HC") == 1:
        count = held[1].shape[0]
        pair = xperm(jnp.concatenate(held[1:], axis=0), 1)
        held_c = [xperm(held[0], 1), pair[:count], pair[count:]]
    elif flag("HC") == 2:
        count = held[1].shape[0]
        three = xperm(jnp.concatenate(held, axis=0), 1)
        held_c = [three[:count], three[count : 2 * count], three[2 * count :]]
    else:
        held_c = [xperm(piece, 1) for piece in held]
    by_x_c, by_y_c = xperm(by_x, 1), xperm(by_y, 1)
    att_pieces = [near, xperm(near, 1), by_x, by_x_c]
    held = held + [by_x, by_y] + held_c + [by_x_c, by_y_c]
    if flag("EP"):
        held = [trio, xperm(trio, 1)] + held
    block_out, dmiddle, d_near, d_far, own_pack, other_pack, ggain = feed_forward(
        ids, lives, tokens, cotangent, gain, att_pieces, held
    )
    d_pieces = exchange(d_near, d_far, flag("DX"))

    def add(*parts):
        total = parts[0].astype(F32)
        for part in parts[1:]:
            total = total + part.astype(F32)
        return total.astype(BF)

    def reduce_column(keep, one, two):
        pieces = [add(keep[4 + kz], one[kz], two[kz]) for kz in range(4)]
        if flag("ZM"):
            return pieces
        return [pieces[0]] + [xperm(pieces[kz], 8 * kz) for kz in (1, 2, 3)]

    (other_pack,) = pick("C2", [other_pack], (d_pieces[2],), (d_pieces[3],))
    came_pack = xperm(other_pack, 1)
    (pack_later,) = pick("C3", [own_pack], (d_pieces[2],), (d_pieces[3],), (d_pieces[1],))
    lead_in, keep_in, lead_rest, keep_rest = feed_gradients(
        ids, lives, cotangent, cot_c, pack_later, came_pack, *att_pieces
    )
    along_x, along_y = xperm(lead_rest, 2), xperm(lead_in, 4)
    (key_later,) = pick("T3", [key], (lead_in,), (d_pieces[2], d_pieces[3]), (lead_in, d_pieces[2], d_pieces[3]))
    dn_keep, dn_sent, far, near = backward_attention(
        ids, token_pieces, cos, sin, q8, key_later, val, att, prob, d_pieces, gain, wide, ggain
    )
    if flag("T5") in (1, 2):
        along_x, along_y = after([along_x, along_y], *((near,) if flag("T5") == 1 else (near, far)))
    (far,) = pick("T4", [far], (along_x, along_y), (along_x,), (along_y,))
    far_y = xperm(far, 4)
    next_in = add(keep_in[:4], along_y[:4])
    next_rest = add(keep_rest[:4], along_x[:4])
    next_in, next_rest = pick("T8", [next_in, next_rest], (far_y,))
    (next_in,) = pick("T9", [next_in], (far_y,), (dn_sent,), (far,))
    (next_rest,) = pick("TD", [next_rest], (far_y,), (dn_sent,), (far,))
    then_y, then_x = xperm(next_rest, 4), xperm(next_in, 2)
    (far_y,) = pick("TA", [far_y], (then_y, then_x), (then_x,), (then_y,))
    (near,) = pick("T2", [near], (along_x, along_y), (then_x,), (then_y,))
    e = [add(near[kz], far_y[kz]) for kz in range(4)]
    heads = [e[0], xperm(e[1], 8), xperm(e[2], 16), xperm(e[3], 24)]
    then_x, = pick("Z1", [then_x], (e[1], e[2], e[3]), (heads[1],), (heads[1], heads[2], heads[3]))
    then_y, = pick("Z2", [then_y], (e[1], e[2], e[3]), (heads[1],), (heads[1], heads[2], heads[3]))
    column_in = reduce_column(keep_in, along_y[4:], then_x)
    column_rest = reduce_column(keep_rest, along_x[4:], then_y)
    if flag("ZM"):
        wide_z = [jnp.concatenate([column_in[kz], column_rest[kz]], axis=1) for kz in range(4)]
        wide_z = [wide_z[0]] + [xperm(wide_z[kz], 8 * kz) for kz in (1, 2, 3)]
        column_in = [piece[:, :1152] for piece in wide_z]
        column_rest = [piece[:, 1152:] for piece in wide_z]
    (dn_sent,) = pick("T6", [dn_sent], (far_y,), (then_x, then_y), (along_x, along_y), (e[1],))
    dn_came = xperm(dn_sent, 1)
    x_came = xperm(add(dn_keep[1], dn_came[1]), 2)
    heads = pick("T7", heads, (x_came,))
    column_in = pick("Z3", column_in, (heads[1],), (heads[1], heads[2], heads[3]))
    mine, other = sum_rows(ids, *column_in, *column_rest)
    states = [
        (weight_in, first_in, second_in, average_in),
        (weight_out, first_out, second_out, average_out),
        (weight_down, first_down, second_down, average_down),
    ]
    (other,) = pick("Z5", [other], (heads[1],), (heads[1], heads[2], heads[3]))
    other_came = xperm(other, 1)
    if flag("TC"):
        heads = pick("TC", heads, (other_came,), (other,))
    head_sums = sum_heads(ids, *heads)
    came = exchange(*head_sums, flag("UX"))
    (mine,) = pick("Z4", [mine], (heads[1],), (heads[1], heads[2], heads[3]), (head_sums[0],), (came[2],))
    new_rows = update_rows(ids, mine, other_came, states)
    new_heads = update_heads(
        ids,
        came,
        (weight_qkv, first_qkv, second_qkv, average_qkv),
        (norm_gains, first_gains, second_gains, average_gains),
    )

    dnormed = dn_keep[0].astype(F32) + dn_came[0].astype(F32) + x_came.astype(F32)
    normed, inverse = norm_parts(tokens.astype(F32))
    grad_tokens = dmiddle + norm_back(dnormed * gain[0:1, :], normed, inverse)

    updated = [new_heads[:5], new_rows[5:10], new_rows[:5], new_rows[10:], new_heads[5:]]
    return (block_out, grad_tokens) + tuple(updated[i][j] for j in range(5) for i in range(5))


def solution(mesh):
    sizes = dict(mesh.shape)
    body = fast_body if sizes == {"dp": 8, "fsdp": 4} else general_body
    rows, columns = P(("dp", "fsdp"), None), P(None, ("dp", "fsdp"))
    weights = (rows,) * 4 + (columns,)
    return jax.shard_map(
        body,
        mesh=mesh,
        in_specs=(rows, rows, P(), P()) + weights * 4,
        out_specs=(rows, rows) + weights * 5,
        check_vma=False,
    )
```

```python
import functools

import jax
import jax.numpy as jnp
from jax import lax
from jax.experimental import pallas as pl
from jax.experimental.pallas import tpu as pltpu
from jax.sharding import PartitionSpec as P

HEADS = 12
HD = 64
STEP = 6


NORM_EPS = 1e-05
ROTARY_BASE = 160000.0
BETA_FIRST = 0.5
BETA_SECOND = 0.5
ADAM_EPS = 1e-08
WEIGHT_DECAY = 0.01
MATRIX_RATE = 0.04
GAIN_RATE = 0.5
AVERAGE_KEEP = 0.6
MASKED = -1e30


def group_layout(count_row, length_row, slots):
    devices_here = count_row.shape[0]
    places = jnp.arange(devices_here * slots, dtype=jnp.int32)
    holder = places // slots
    within = places - holder * slots
    before = jnp.cumsum(count_row) - count_row
    choose = (holder[:, None] == jnp.arange(devices_here, dtype=jnp.int32)[None, :]).astype(
        jnp.int32
    )
    offset = jnp.sum(choose * before[None, :], axis=1) + within
    limits = jnp.sum(choose * count_row[None, :], axis=1)
    living = within < limits
    doc_ends = jnp.cumsum(length_row)
    passed = offset[:, None] >= doc_ends[None, :]
    document = jnp.sum(passed.astype(jnp.int32), axis=1)
    begins = jnp.max(jnp.where(passed, doc_ends[None, :], 0), axis=1)
    number_docs = length_row.shape[0]
    document = jnp.where(living, document, number_docs)
    position = jnp.where(living, offset - begins, 0)
    return (document, position, living)


def rotary_tables(position, head_size):
    half_size = head_size // 2
    speeds = ROTARY_BASE ** (-(jnp.arange(half_size, dtype=jnp.float32) * (2.0 / head_size)))
    angles = position.astype(jnp.float32)[:, None] * speeds[None, :]
    return (jnp.cos(angles), jnp.sin(angles))


def rotate(heads_in, cosine_table, sine_table):
    half_size = heads_in.shape[-1] // 2
    leading = heads_in[..., :half_size]
    latter = heads_in[..., half_size:]
    cos_wide = cosine_table[:, None, :]
    sin_wide = sine_table[:, None, :]
    return jnp.concatenate(
        [leading * cos_wide - latter * sin_wide, latter * cos_wide + leading * sin_wide], axis=-1
    )


def rotate_back(grads_in, cosine_table, sine_table):
    half_size = grads_in.shape[-1] // 2
    leading = grads_in[..., :half_size]
    latter = grads_in[..., half_size:]
    cos_wide = cosine_table[:, None, :]
    sin_wide = sine_table[:, None, :]
    return jnp.concatenate(
        [leading * cos_wide + latter * sin_wide, latter * cos_wide - leading * sin_wide], axis=-1
    )


def norm_parts(values_in):
    center = values_in - jnp.mean(values_in, axis=-1, keepdims=True)
    inverse = lax.rsqrt(jnp.mean(center * center, axis=-1, keepdims=True) + NORM_EPS)
    return (center * inverse, inverse)


def norm_back(upstream, normed, inverse):
    return inverse * (
        upstream
        - jnp.mean(upstream, axis=-1, keepdims=True)
        - normed * jnp.mean(upstream * normed, axis=-1, keepdims=True)
    )


def block_scores(queries, key_block, doc_query, doc_key, score_scale):
    scores = (
        jnp.einsum("qhd,khd->hqk", queries, key_block, preferred_element_type=jnp.float32)
        * score_scale
    )
    return jnp.where(doc_query[None, :, None] == doc_key[None, None, :], scores, MASKED)


def contract_rows(left_side, right_side):
    return lax.dot_general(
        left_side, right_side, (((0,), (0,)), ((), ())), preferred_element_type=jnp.float32
    )


def contract_cols(left_side, right_side):
    return lax.dot_general(
        left_side, right_side, (((1,), (1,)), ((), ())), preferred_element_type=jnp.float32
    )


def adam_update(master, first_old, second_old, average_old, gradient, step_rate):
    first_new = BETA_FIRST * first_old + (1.0 - BETA_FIRST) * gradient
    second_new = BETA_SECOND * second_old + (1.0 - BETA_SECOND) * gradient * gradient
    first_fix = first_new / (1.0 - BETA_FIRST**STEP)
    second_fix = second_new / (1.0 - BETA_SECOND**STEP)
    master_new = master - step_rate * (
        first_fix / (jnp.sqrt(second_fix) + ADAM_EPS) + WEIGHT_DECAY * master
    )
    average_new = AVERAGE_KEEP * average_old + (1.0 - AVERAGE_KEEP) * master_new
    return (first_new, second_new, master_new, average_new, master_new.astype(jnp.bfloat16))


def general_body(
    tokens,
    cotangent,
    counts,
    lengths,
    weight_qkv,
    weight_out,
    weight_in,
    weight_down,
    norm_gains,
    first_qkv,
    first_out,
    first_in,
    first_down,
    first_gains,
    second_qkv,
    second_out,
    second_in,
    second_down,
    second_gains,
    average_qkv,
    average_out,
    average_in,
    average_down,
    average_gains,
):
    slots = tokens.shape[0]
    model_width = tokens.shape[1]
    hidden_units = weight_down.shape[1]
    head_count = HEADS
    head_size = HD
    score_scale = 1.0 / head_size**0.5
    heads_shape = (slots, head_count, head_size)
    group_row = lax.axis_index("dp")
    own_place = lax.axis_index("fsdp")
    count_row = lax.dynamic_index_in_dim(counts, group_row, 0, keepdims=False)
    length_row = lax.dynamic_index_in_dim(lengths, group_row, 0, keepdims=False)
    doc_all, position_all, living_all = group_layout(count_row, length_row, slots)
    doc_mine = lax.dynamic_slice_in_dim(doc_all, own_place * slots, slots)
    position_mine = lax.dynamic_slice_in_dim(position_all, own_place * slots, slots)
    living_mine = lax.dynamic_slice_in_dim(living_all, own_place * slots, slots)
    cosine_table, sine_table = rotary_tables(position_mine, head_size)
    living_col = living_mine[:, None]
    copies = (
        weight_qkv.astype(jnp.bfloat16),
        weight_out.astype(jnp.bfloat16),
        weight_in.astype(jnp.bfloat16),
        weight_down.astype(jnp.bfloat16),
        norm_gains.astype(jnp.bfloat16),
    )
    qkv_full, out_full, in_full, down_full, gain_full = (
        lax.all_gather(copies[0], ("dp", "fsdp"), axis=0, tiled=True),
        lax.all_gather(copies[1], ("dp", "fsdp"), axis=0, tiled=True),
        lax.all_gather(copies[2], ("dp", "fsdp"), axis=0, tiled=True),
        lax.all_gather(copies[3], ("dp", "fsdp"), axis=0, tiled=True),
        lax.all_gather(copies[4], ("dp", "fsdp"), axis=1, tiled=True),
    )
    tokens_f = tokens.astype(jnp.float32)
    normed_one, inverse_one = norm_parts(tokens_f)
    gain_one = gain_full[0].astype(jnp.float32)
    gain_two = gain_full[1].astype(jnp.float32)
    normed1_low = (normed_one * gain_one).astype(jnp.bfloat16)
    mixed_qkv = jnp.dot(normed1_low, qkv_full, preferred_element_type=jnp.float32)
    queries16 = rotate(
        mixed_qkv[:, :model_width].reshape(heads_shape), cosine_table, sine_table
    ).astype(jnp.bfloat16)
    keys16 = rotate(
        mixed_qkv[:, model_width : 2 * model_width].reshape(heads_shape), cosine_table, sine_table
    ).astype(jnp.bfloat16)
    key_flat = keys16.reshape(slots, model_width)
    value_flat = mixed_qkv[:, 2 * model_width :].astype(jnp.bfloat16)
    key_rows, value_rows = (
        lax.all_gather(key_flat, "fsdp", axis=0, tiled=True),
        lax.all_gather(value_flat, "fsdp", axis=0, tiled=True),
    )
    group_rows = key_rows.shape[0]
    block_rows = 512
    count_blocks = group_rows // block_rows
    blocks_shape = (count_blocks, block_rows, head_count, head_size)
    doc_blocks = doc_all.reshape(count_blocks, block_rows)
    key_blocks = key_rows.reshape(blocks_shape)
    value_blocks = value_rows.reshape(blocks_shape)

    def max_sum(state_now, pieces):
        run_peak, run_total = state_now
        scores = block_scores(queries16, pieces[0], doc_mine, pieces[1], score_scale)
        new_peak = jnp.maximum(run_peak, jnp.max(scores, axis=-1))
        run_total = run_total * jnp.exp(run_peak - new_peak) + jnp.sum(
            jnp.exp(scores - new_peak[:, :, None]), axis=-1
        )
        return ((new_peak, run_total), None)

    start_state = (
        jnp.full((head_count, slots), MASKED, jnp.float32),
        jnp.zeros((head_count, slots), jnp.float32),
    )
    (run_peak, run_total), unused_max = lax.scan(max_sum, start_state, (key_blocks, doc_blocks))
    log_total = run_peak + jnp.log(run_total)

    def weigh_values(accum, pieces):
        scores = block_scores(queries16, pieces[0], doc_mine, pieces[2], score_scale)
        probs16 = jnp.exp(scores - log_total[:, :, None]).astype(jnp.bfloat16)
        return (
            accum
            + jnp.einsum("hqk,khd->qhd", probs16, pieces[1], preferred_element_type=jnp.float32),
            None,
        )

    attended, unused_out = lax.scan(
        weigh_values, jnp.zeros(heads_shape, jnp.float32), (key_blocks, value_blocks, doc_blocks)
    )
    attended16 = attended.reshape(slots, model_width).astype(jnp.bfloat16)
    middle = tokens_f + jnp.dot(attended16, out_full, preferred_element_type=jnp.float32)
    normed_two, inverse_two = norm_parts(middle)
    normed2_low = (normed_two * gain_two).astype(jnp.bfloat16)
    gate_up = jnp.dot(normed2_low, in_full, preferred_element_type=jnp.float32)
    act_half = gate_up[:, :hidden_units]
    gate_half = gate_up[:, hidden_units:]
    activated16 = (jax.nn.gelu(act_half, approximate=False) * gate_half).astype(jnp.bfloat16)
    branch_two = contract_cols(activated16, down_full)
    block_out = jnp.where(living_col, middle + branch_two, 0.0).astype(jnp.bfloat16)
    qkv_back, out_back, in_back, down_back, gain_back = (
        lax.all_gather(copies[0], ("dp", "fsdp"), axis=0, tiled=True),
        lax.all_gather(copies[1], ("dp", "fsdp"), axis=0, tiled=True),
        lax.all_gather(copies[2], ("dp", "fsdp"), axis=0, tiled=True),
        lax.all_gather(copies[3], ("dp", "fsdp"), axis=0, tiled=True),
        lax.all_gather(copies[4], ("dp", "fsdp"), axis=1, tiled=True),
    )
    key_again, value_again = (
        lax.all_gather(key_flat, "fsdp", axis=0, tiled=True),
        lax.all_gather(value_flat, "fsdp", axis=0, tiled=True),
    )
    gain_one_back = gain_back[0].astype(jnp.float32)
    gain_two_back = gain_back[1].astype(jnp.float32)
    dout = jnp.where(living_col, cotangent.astype(jnp.float32), 0.0)
    dym16 = dout.astype(jnp.bfloat16)
    grad_down = contract_rows(dym16, activated16)
    dact = jnp.dot(dym16, down_back, preferred_element_type=jnp.float32)
    unused_gate, gate_pull = jax.vjp(
        lambda front_part, rear_part: jax.nn.gelu(front_part, approximate=False) * rear_part,
        act_half,
        gate_half,
    )
    dfront, drear = gate_pull(dact)
    dgate16 = jnp.concatenate([dfront, drear], axis=1).astype(jnp.bfloat16)
    grad_in = contract_rows(normed2_low, dgate16)
    dnormed_two = contract_cols(dgate16, in_back)
    grad_gain_two = jnp.sum(dnormed_two * normed_two, axis=0)
    dmiddle = dout + norm_back(dnormed_two * gain_two_back, normed_two, inverse_two)
    dbranch16 = dmiddle.astype(jnp.bfloat16)
    grad_out = contract_rows(attended16, dbranch16)
    dattn16 = contract_cols(dbranch16, out_back).astype(jnp.bfloat16).reshape(heads_shape)
    row_delta = jnp.sum(dattn16.astype(jnp.float32) * attended, axis=-1).T
    back_keys = key_again.reshape(blocks_shape)
    back_values = value_again.reshape(blocks_shape)

    def back_block(dquery_sum, pieces):
        key_block, value_block, doc_block = pieces
        scores = block_scores(queries16, key_block, doc_mine, doc_block, score_scale)
        probs = jnp.exp(scores - log_total[:, :, None])
        probs16 = probs.astype(jnp.bfloat16)
        dvalue_block = jnp.einsum(
            "hqk,qhd->khd", probs16, dattn16, preferred_element_type=jnp.float32
        )
        dprobs = jnp.einsum(
            "qhd,khd->hqk", dattn16, value_block, preferred_element_type=jnp.float32
        )
        dscores16 = (probs * (dprobs - row_delta[:, :, None])).astype(jnp.bfloat16)
        dquery_sum = dquery_sum + jnp.einsum(
            "hqk,khd->qhd", dscores16, key_block, preferred_element_type=jnp.float32
        )
        dkey_block = jnp.einsum(
            "hqk,qhd->khd", dscores16, queries16, preferred_element_type=jnp.float32
        )
        return (dquery_sum, (dkey_block, dvalue_block))

    dquery_sum, (dkey_blocks, dvalue_blocks) = lax.scan(
        back_block, jnp.zeros(heads_shape, jnp.float32), (back_keys, back_values, doc_blocks)
    )
    dkey_mine, dvalue_mine = (
        lax.psum_scatter(
            (dkey_blocks.reshape(group_rows, model_width) * score_scale).astype(jnp.bfloat16),
            "fsdp",
            scatter_dimension=0,
            tiled=True,
        ).astype(jnp.float32),
        lax.psum_scatter(
            dvalue_blocks.reshape(group_rows, model_width).astype(jnp.bfloat16),
            "fsdp",
            scatter_dimension=0,
            tiled=True,
        ).astype(jnp.float32),
    )
    dquery_pre = rotate_back(dquery_sum * score_scale, cosine_table, sine_table).reshape(
        slots, model_width
    )
    dkey_pre = rotate_back(dkey_mine.reshape(heads_shape), cosine_table, sine_table).reshape(
        slots, model_width
    )
    dmixed16 = jnp.concatenate([dquery_pre, dkey_pre, dvalue_mine], axis=1).astype(jnp.bfloat16)
    grad_qkv = contract_rows(normed1_low, dmixed16)
    dnormed_one = contract_cols(dmixed16, qkv_back)
    grad_gain_one = jnp.sum(dnormed_one * normed_one, axis=0)
    grad_tokens = dmiddle + norm_back(dnormed_one * gain_one_back, normed_one, inverse_one)
    grad_gains = jnp.stack([grad_gain_one, grad_gain_two], axis=0)
    reduced = (
        lax.psum_scatter(grad_qkv, ("dp", "fsdp"), scatter_dimension=0, tiled=True),
        lax.psum_scatter(grad_out, ("dp", "fsdp"), scatter_dimension=0, tiled=True),
        lax.psum_scatter(grad_in, ("dp", "fsdp"), scatter_dimension=0, tiled=True),
        lax.psum_scatter(grad_down, ("dp", "fsdp"), scatter_dimension=0, tiled=True),
        lax.psum_scatter(grad_gains, ("dp", "fsdp"), scatter_dimension=1, tiled=True),
    )
    masters = (weight_qkv, weight_out, weight_in, weight_down, norm_gains)
    firsts = (first_qkv, first_out, first_in, first_down, first_gains)
    seconds = (second_qkv, second_out, second_in, second_down, second_gains)
    averages = (average_qkv, average_out, average_in, average_down, average_gains)
    rates = (MATRIX_RATE, MATRIX_RATE, MATRIX_RATE, MATRIX_RATE, GAIN_RATE)
    updated = [
        adam_update(
            masters[which],
            firsts[which],
            seconds[which],
            averages[which],
            reduced[which],
            rates[which],
        )
        for which in range(5)
    ]
    return (
        block_out,
        grad_tokens,
        updated[0][0],
        updated[1][0],
        updated[2][0],
        updated[3][0],
        updated[4][0],
        updated[0][1],
        updated[1][1],
        updated[2][1],
        updated[3][1],
        updated[4][1],
        updated[0][2],
        updated[1][2],
        updated[2][2],
        updated[3][2],
        updated[4][2],
        updated[0][3],
        updated[1][3],
        updated[2][3],
        updated[3][3],
        updated[4][3],
        updated[0][4],
        updated[1][4],
        updated[2][4],
        updated[3][4],
        updated[4][4],
    )


FL = {'DX': 1, 'H1': 3, 'H3': 2, 'H6': 1, 'H7': 2, 'T2': 1, 'T3': 1, 'T4': 2, 'T6': 3, 'TD': 1, 'UX': 1, 'Z1': 1, 'Z3': 2, 'Z4': 2, 'T7': 1, 'H5': 1, 'QX': 1}
BF = jnp.bfloat16
F32 = jnp.float32
AXES = ("dp", "fsdp")
VMEM_LIMIT = 60 * 1024 * 1024


def xperm(value, mask):
    count = lax.axis_size("dp") * lax.axis_size("fsdp")
    return lax.ppermute(value, AXES, [(i, i ^ mask) for i in range(count)])


def dot_nn(a, b):
    return jnp.dot(a, b, preferred_element_type=F32)


def dot_nt(a, b):
    return lax.dot_general(a, b, (((1,), (1,)), ((), ())), preferred_element_type=F32)


def dot_tn(a, b):
    return lax.dot_general(a, b, (((0,), (0,)), ((), ())), preferred_element_type=F32)


def spread_columns(weight):
    rows = weight.shape[0]
    gap, end = jnp.zeros((rows, 32), weight.dtype), jnp.zeros((rows, 64), weight.dtype)
    parts = []
    for i in range(4):
        parts += [weight[:, 96 * i : 96 * i + 96], gap]
    return jnp.concatenate(parts + [weight[:, 384:576], end], axis=1)


def pack_columns(spread, last):
    return jnp.concatenate([spread[:, 128 * i : 128 * i + 96] for i in range(4)] + [spread[:, 512:704], last], axis=1)


def live_rows(count):
    return lax.broadcasted_iota(jnp.int32, (256, 1), 0) < count


def pack_heads(block):
    return jnp.concatenate([block[64 * i : 64 * i + 64] for i in range(4)], axis=1)


def unpack_heads(packed):
    return jnp.concatenate([packed[:, 192 * i : 192 * i + 192] for i in range(4)], axis=0)


def head_lanes(width, head):
    lane = lax.broadcasted_iota(jnp.int32, (1, width), 1) % 128
    return (lane >= 32 * head) & (lane < 32 * head + 32)


def value_lanes(width, head):
    lane = lax.broadcasted_iota(jnp.int32, (1, width), 1)
    return (lane >= 64 * head) & (lane < 64 * head + 64)


def prologue_kernel(ids, wq, w_out, w_in, w_down, gains, near, far, mine, other):
    f, core = ids[0] & 3, ids[0] & 1
    row = lax.broadcasted_iota(jnp.int32, (24, 24), 0)
    col = lax.broadcasted_iota(jnp.int32, (24, 24), 1)
    parts = []
    for j in range(2):
        spread = jnp.where(row == col, gains[j : j + 1, :], 0.0)
        parts.append(jnp.sum(spread, axis=-1, keepdims=True))
    lane = lax.broadcasted_iota(jnp.int32, (24, 64), 1)
    columns = jnp.where(lane == 0, parts[0], jnp.where(lane == 1, parts[1], 0.0))
    blocks = []
    for j in range(4):
        pieces = []
        for part in range(2):
            heads = wq[:, 768 * part + 192 * j : 768 * part + 192 * j + 192]
            pieces += [heads[:, 64 * h + 32 * half : 64 * h + 32 * half + 32] for half in range(2) for h in range(3)]
        blocks.append(jnp.concatenate(pieces + [wq[:, 1536 + 192 * j : 1728 + 192 * j], columns], axis=1))
    for k, out in enumerate((near.at[0], near.at[1], far.at[0], far.at[1])):
        place = f ^ k
        low = jnp.where(place == 0, blocks[0], blocks[1])
        high = jnp.where(place == 2, blocks[2], blocks[3])
        out[...] = jnp.where(place < 2, low, high).astype(BF)
    left = jnp.concatenate([w_out[:, :384], w_in[:, :1152], w_down[:, :640]], axis=1)
    right = jnp.concatenate([w_out[:, 384:], w_in[:, 1152:], w_down[:, 640:], jnp.zeros((24, 128), F32)], axis=1)
    mine[...] = jnp.where(core == 0, left, right).astype(BF)
    other[...] = jnp.where(core == 0, right, left).astype(BF)


def assemble_kernel(ids, q0, q1, q2, q3, mine, came, rows, other):
    f, core = ids[0] & 3, ids[0] & 1
    pieces = [q[i].astype(F32) for q, i in ((q0, 0), (q1, 1), (q2, 0), (q3, 1))]
    ordered = []
    for place in range(4):
        k = f ^ place
        low = jnp.where(k == 0, pieces[0], pieces[1])
        high = jnp.where(k == 2, pieces[2], pieces[3])
        ordered.append(jnp.where(k < 2, low, high))
    rows[...] = jnp.concatenate(ordered, axis=0).astype(BF)
    one, two = mine[...].astype(F32), came[...].astype(F32)
    other[...] = jnp.concatenate([jnp.where(core == 0, one, two), jnp.where(core == 0, two, one)], axis=0).astype(BF)


def forward_kernel(
    ids, t0, t1, t2, t3, cos, sin, docq, dock, w0, w1, w2, w3,
    q8, key, val, att, near, far, prob, gain, wide, wscr, sems,
):
    step = pl.program_id(0)

    @pl.when(step == 0)
    def _():
        copies = []
        pieces = (w0, w1, w2.at[0], w3.at[0], w2.at[1], w3.at[1], w2.at[2], w3.at[2])
        for k, piece in enumerate(pieces):
            at = pl.multiple_of(96 * ((ids[0] >> 2) ^ k), 96)
            copies.append(pltpu.make_async_copy(piece, wscr.at[pl.ds(at, 96)], sems.at[k]))
            copies[-1].start()
        for copy in copies:
            copy.wait()
        weight = wscr[...]
        wide[...] = spread_columns(weight)
        row = lax.broadcasted_iota(jnp.int32, (8, 640), 0)
        col = lax.broadcasted_iota(jnp.int32, (8, 640), 1)
        pick = ((col == row + 576) & (row < 2)).astype(F32).astype(BF)
        gain[...] = dot_nt(pick, weight)
        gain_row = gain[0:1, :]
        for i, piece in enumerate((t0, t1, t2, t3)):
            rows = slice(256 * i, 256 * i + 256)
            x = piece[...].astype(F32)
            center = x - jnp.mean(x, axis=-1, keepdims=True)
            inverse = lax.rsqrt(jnp.mean(center * center, axis=-1, keepdims=True) + NORM_EPS)
            mixed = dot_nn((center * inverse * gain_row).astype(BF), wide[...])
            c, s = cos[rows, :], sin[rows, :]
            qa, qb = mixed[:, :128], mixed[:, 128:256]
            ka, kb = mixed[:, 256:384], mixed[:, 384:512]
            q8[rows, :128] = ((qa * c - qb * s).astype(BF).astype(F32) * 0.125).astype(BF)
            q8[rows, 128:] = ((qb * c + qa * s).astype(BF).astype(F32) * 0.125).astype(BF)
            key[rows, :128] = (ka * c - kb * s).astype(BF)
            key[rows, 128:] = (kb * c + ka * s).astype(BF)
            val[rows, :] = mixed[:, 512:].astype(BF)

    rows = pl.ds(pl.multiple_of(step * 256, 256), 256)
    queries = q8[rows, :]
    keys = key[...]
    values = val[...]
    same = docq[rows, :] == dock[...]
    total = jnp.zeros((256, 256), F32)
    zero = jnp.zeros((), BF)
    for h in range(3):
        scores = dot_nt(jnp.where(head_lanes(256, h), queries, zero), keys)
        scores = jnp.where(same, scores, MASKED)
        peak = jnp.max(scores, axis=-1, keepdims=True)
        weights = jnp.exp(scores - peak)
        scale = 1.0 / jnp.sum(weights, axis=-1, keepdims=True)
        weights16 = (weights * scale).astype(BF)
        prob[h] = weights16
        total += dot_nn(weights16, jnp.where(value_lanes(256, h), values, zero))
    att[...] = total[:, :192]
    low = total[:, :192].astype(BF)

    @pl.when(step < 2)
    def _():
        near[0] = pack_heads(low)

    @pl.when(step >= 2)
    def _():
        far[0] = pack_heads(low)


def project_kernel(ids, t0, t1, t2, t3, cos, sin, w0, w1, w2, w3, q8, key, val, gain, wide, wscr, sems):
    copies = []
    pieces = (w0, w1, w2.at[0], w3.at[0], w2.at[1], w3.at[1], w2.at[2], w3.at[2])
    for k, piece in enumerate(pieces):
        at = pl.multiple_of(96 * ((ids[0] >> 2) ^ k), 96)
        copies.append(pltpu.make_async_copy(piece, wscr.at[pl.ds(at, 96)], sems.at[k]))
        copies[-1].start()
    for copy in copies:
        copy.wait()
    weight = wscr[...]
    wide[...] = spread_columns(weight)
    row = lax.broadcasted_iota(jnp.int32, (8, 640), 0)
    col = lax.broadcasted_iota(jnp.int32, (8, 640), 1)
    pick = ((col == row + 576) & (row < 2)).astype(F32).astype(BF)
    gain[...] = dot_nt(pick, weight)
    gain_row = gain[0:1, :]
    for i, piece in enumerate((t0, t1, t2, t3)):
        rows = slice(256 * i, 256 * i + 256)
        x = piece[...].astype(F32)
        center = x - jnp.mean(x, axis=-1, keepdims=True)
        inverse = lax.rsqrt(jnp.mean(center * center, axis=-1, keepdims=True) + NORM_EPS)
        mixed = dot_nn((center * inverse * gain_row).astype(BF), wide[...])
        c, s = cos[rows, :], sin[rows, :]
        qa, qb = mixed[:, :128], mixed[:, 128:256]
        ka, kb = mixed[:, 256:384], mixed[:, 384:512]
        q8[rows, :128] = ((qa * c - qb * s).astype(BF).astype(F32) * 0.125).astype(BF)
        q8[rows, 128:] = ((qb * c + qa * s).astype(BF).astype(F32) * 0.125).astype(BF)
        key[rows, :128] = (ka * c - kb * s).astype(BF)
        key[rows, 128:] = (kb * c + ka * s).astype(BF)
        val[rows, :] = mixed[:, 512:].astype(BF)


def attend_kernel(q8, key, val, docq, dock, att, near, far, prob):
    step = pl.program_id(0)
    rows = pl.ds(pl.multiple_of(step * 256, 256), 256)
    queries = q8[rows, :]
    keys = key[...]
    values = val[...]
    same = docq[rows, :] == dock[...]
    total = jnp.zeros((256, 256), F32)
    zero = jnp.zeros((), BF)
    for h in range(3):
        scores = dot_nt(jnp.where(head_lanes(256, h), queries, zero), keys)
        scores = jnp.where(same, scores, MASKED)
        peak = jnp.max(scores, axis=-1, keepdims=True)
        weights = jnp.exp(scores - peak)
        scale = 1.0 / jnp.sum(weights, axis=-1, keepdims=True)
        weights16 = (weights * scale).astype(BF)
        prob[h] = weights16
        total += dot_nn(weights16, jnp.where(value_lanes(256, h), values, zero))
    att[...] = total[:, :192]
    low = total[:, :192].astype(BF)

    @pl.when(step < 2)
    def _():
        near[0] = pack_heads(low)

    @pl.when(step >= 2)
    def _():
        far[0] = pack_heads(low)


def full(shape):
    return pl.BlockSpec(shape, lambda *_: (0,) * len(shape))


VM = pl.BlockSpec(memory_space=pltpu.VMEM)
SMEM = pl.BlockSpec(memory_space=pltpu.SMEM)
ANY = pl.BlockSpec(memory_space=pltpu.HBM)


def shaped(shape, dtype):
    return jax.ShapeDtypeStruct(shape, dtype)


def prologue(ids, weight_qkv, weight_out, weight_in, weight_down, norm_gains):
    return pl.pallas_call(
        prologue_kernel,
        in_specs=[SMEM] + [VM] * 5,
        out_specs=[VM] * 4,
        out_shape=[shaped((2, 24, 640), BF)] * 2 + [shaped((24, 2176), BF)] * 2,
        compiler_params=pltpu.CompilerParams(vmem_limit_bytes=VMEM_LIMIT),
        cost_estimate=pl.CostEstimate(flops=10**6, bytes_accessed=10**6, transcendentals=0),
        name="prologue",
    )(ids, weight_qkv, weight_out, weight_in, weight_down, norm_gains)


def assemble(ids, *pieces):
    return pl.pallas_call(
        assemble_kernel,
        in_specs=[SMEM] + [VM] * 6,
        out_specs=[VM] * 2,
        out_shape=[shaped((96, 640), BF), shaped((48, 2176), BF)],
        compiler_params=pltpu.CompilerParams(vmem_limit_bytes=VMEM_LIMIT),
        cost_estimate=pl.CostEstimate(flops=10**6, bytes_accessed=10**6, transcendentals=0),
        name="assemble",
    )(ids, *pieces)


def forward_attention(ids, token_pieces, cos, sin, docs, w_pieces):
    return pl.pallas_call(
        forward_kernel,
        grid=(4,),
        in_specs=[SMEM]
        + [full((256, 768))] * 4
        + [full((1024, 128))] * 2
        + [full((1024, 1)), full((1, 1024))]
        + [ANY] * 4,
        out_specs=[
            full((1024, 256)),
            full((1024, 256)),
            full((1024, 256)),
            pl.BlockSpec((256, 192), lambda i: (i, 0)),
            pl.BlockSpec((1, 64, 768), lambda i: (jnp.minimum(i, 1), 0, 0)),
            pl.BlockSpec((1, 64, 768), lambda i: (jnp.maximum(i - 2, 0), 0, 0)),
            pl.BlockSpec((3, 256, 1024), lambda i: (0, i, 0)),
            full((8, 768)),
            full((768, 768)),
        ],
        out_shape=[
            shaped((1024, 256), BF),
            shaped((1024, 256), BF),
            shaped((1024, 256), BF),
            shaped((1024, 192), F32),
            shaped((2, 64, 768), BF),
            shaped((2, 64, 768), BF),
            shaped((3, 1024, 1024), BF),
            shaped((8, 768), F32),
            shaped((768, 768), BF),
        ],
        scratch_shapes=[pltpu.VMEM((768, 640), BF), pltpu.SemaphoreType.DMA((8,))],
        compiler_params=pltpu.CompilerParams(vmem_limit_bytes=VMEM_LIMIT),
        cost_estimate=pl.CostEstimate(flops=6 * 10**9, bytes_accessed=16 * 10**6, transcendentals=3 * 10**6),
        name="forward_attention",
    )(ids, *token_pieces, cos, sin, docs[:, None], docs[None, :], *w_pieces)


def project(ids, token_pieces, cos, sin, w_pieces):
    return pl.pallas_call(
        project_kernel,
        in_specs=[SMEM] + [VM] * 6 + [ANY] * 4,
        out_specs=[VM] * 5,
        out_shape=[
            shaped((1024, 256), BF),
            shaped((1024, 256), BF),
            shaped((1024, 256), BF),
            shaped((8, 768), F32),
            shaped((768, 768), BF),
        ],
        scratch_shapes=[pltpu.VMEM((768, 640), BF), pltpu.SemaphoreType.DMA((8,))],
        compiler_params=pltpu.CompilerParams(vmem_limit_bytes=VMEM_LIMIT),
        cost_estimate=pl.CostEstimate(flops=3 * 10**9, bytes_accessed=8 * 10**6, transcendentals=0),
        name="project",
    )(ids, *token_pieces, cos, sin, *w_pieces)


def attend(q8, key, val, docs):
    return pl.pallas_call(
        attend_kernel,
        grid=(4,),
        in_specs=[full((1024, 256))] * 3 + [full((1024, 1)), full((1, 1024))],
        out_specs=[
            pl.BlockSpec((256, 192), lambda i: (i, 0)),
            pl.BlockSpec((1, 64, 768), lambda i: (jnp.minimum(i, 1), 0, 0)),
            pl.BlockSpec((1, 64, 768), lambda i: (jnp.maximum(i - 2, 0), 0, 0)),
            pl.BlockSpec((3, 256, 1024), lambda i: (0, i, 0)),
        ],
        out_shape=[
            shaped((1024, 192), F32),
            shaped((2, 64, 768), BF),
            shaped((2, 64, 768), BF),
            shaped((3, 1024, 1024), BF),
        ],
        compiler_params=pltpu.CompilerParams(vmem_limit_bytes=VMEM_LIMIT),
        cost_estimate=pl.CostEstimate(flops=3 * 10**9, bytes_accessed=8 * 10**6, transcendentals=3 * 10**6),
        name="attend",
    )(q8, key, val, docs[:, None], docs[None, :])


def erf_pair(x):
    cdf = 0.5 * (1.0 + lax.erf(x * (0.5**0.5)))
    density = jnp.exp(-0.5 * x * x) * (1.0 / (2.0 * 3.141592653589793) ** 0.5)
    return cdf, density


def load_halves(held, targets, core, chip, sems):
    groups = [[], []]
    early, held = held[: len(held) - 10], held[len(held) - 10 :]
    for which, columns in enumerate((pl.ds(0, 768), pl.ds(768, 1408))):
        for owner in range(2):
            half = core if owner == 0 else 1 - core
            arrays = held[owner * 5 : owner * 5 + 5]
            for group in range(4):
                for kz in range(4):
                    rows = pl.ds(pl.multiple_of(48 * (chip ^ (kz * 4 + group)), 48), 48)
                    if group == 3:
                        piece = arrays[4].at[kz] if which else arrays[3].at[pl.ds(48 * kz, 48)]
                    elif early:
                        piece = early[owner].at[group] if kz == 0 else arrays[group].at[kz - 1]
                        piece = piece.at[:, columns]
                    else:
                        piece = arrays[group].at[kz, :, columns]
                    sem = sems.at[which, len(groups[which])]
                    groups[which].append(pltpu.make_async_copy(piece, targets[which].at[half, rows], sem))
                    groups[which][-1].start()
    return groups


def store_half(own_pack, other_pack, at, halves, core):
    width = halves[0].shape[1]
    own_pack[:, at : at + width] = jnp.where(core == 0, halves[0], halves[1])
    other_pack[:, at : at + width] = jnp.where(core == 0, halves[1], halves[0])


def feed_kernel(*refs):
    ids, lives, tok, cot, gain, a0, a1, a2, a3 = refs[:9]
    held = refs[9:-10]
    (block, dmid, d_near, d_far, own_pack, other_pack, ggain, w_lead, w_rest, sems) = refs[-10:]
    f, core, chip = ids[0] & 3, ids[0] & 1, ids[0] >> 1
    lead_copies, rest_copies = load_halves(held, (w_lead, w_rest), core, chip, sems)
    tok_f = tok[...].astype(F32)
    pieces = [unpack_heads(a) for a in (a0[0], a1[1], a2[192:256, :], a3[256:320, :])]
    heads = [pl.ds(pl.multiple_of(192 * (f ^ k), 192), 192) for k in range(4)]
    for copy in lead_copies:
        copy.wait()
    left = jnp.zeros((256, 384), F32)
    right = jnp.zeros((256, 384), F32)
    for k in range(4):
        left += dot_nn(pieces[k], w_lead[0, heads[k], :384])
        right += dot_nn(pieces[k], w_lead[1, heads[k], :384])
    middle = tok_f + jnp.concatenate([left, right], axis=1)
    center = middle - jnp.mean(middle, axis=-1, keepdims=True)
    inverse = lax.rsqrt(jnp.mean(center * center, axis=-1, keepdims=True) + NORM_EPS)
    normed = center * inverse
    gain_row = gain[1:2, :]
    low = (normed * gain_row).astype(BF)
    own_pack[:, :768] = low
    other_pack[:, :768] = low
    for copy in rest_copies:
        copy.wait()
    act, gate = [
        jnp.concatenate([dot_nn(low, w_lead[h, :, 384:]), dot_nn(low, w_rest[h, :, :768])], axis=1) for h in range(2)
    ]
    cdf, density = erf_pair(act)
    gelu = act * cdf
    active = (gelu * gate).astype(BF)
    halves = [active[:, :640], jnp.concatenate([active[:, 640:], jnp.zeros((256, 128), BF)], axis=1)]
    store_half(own_pack, other_pack, 1920, halves, core)
    alive = live_rows(lives[0])
    dout = jnp.where(alive, cot[...].astype(F32), 0.0)
    dym = dout.astype(BF)
    dact = jnp.concatenate([dot_nn(dym, w_rest[0, :, 768:]), dot_nn(dym, w_rest[1, :, 768:1280])], axis=1)
    dg_front = (dact * gate * (cdf + act * density)).astype(BF)
    dg_rear = (dact * gelu).astype(BF)
    store_half(own_pack, other_pack, 768, [dg_front, dg_rear], core)
    dnormed = jnp.zeros((256, 768), F32)
    for h, part in enumerate((dg_front, dg_rear)):
        dnormed += dot_nt(part[:, :384], w_lead[h, :, 384:]) + dot_nt(part[:, 384:], w_rest[h, :, :768])
    ggain[...] = jnp.broadcast_to(jnp.sum(dnormed * normed, axis=0, keepdims=True), (8, 768))
    up = dnormed * gain_row
    dmiddle = dout + inverse * (
        up
        - jnp.mean(up, axis=-1, keepdims=True)
        - normed * jnp.mean(up * normed, axis=-1, keepdims=True)
    )
    dmid[...] = dmiddle
    dbranch = dmiddle.astype(BF)
    store_half(own_pack, other_pack, 2560, [dbranch[:, :384], dbranch[:, 384:]], core)
    for k in range(4):
        (d_near, d_far)[k // 2][k % 2] = pack_heads(
            (
                dot_nt(dbranch[:, :384], w_lead[0, heads[k], :384])
                + dot_nt(dbranch[:, 384:], w_lead[1, heads[k], :384])
            ).astype(BF)
        )
    branch = dot_nt(active[:, :640], w_rest[0, :, 768:]) + dot_nt(active[:, 640:], w_rest[1, :, 768:1280])
    block[...] = jnp.where(alive, middle + branch, 0.0).astype(BF)


def feed_forward(ids, lives, tokens, cotangent, gain, att_pieces, held):
    return pl.pallas_call(
        feed_kernel,
        in_specs=[SMEM] * 2 + [VM] * 7 + [ANY] * len(held),
        out_specs=[VM] * 7,
        out_shape=[
            shaped((256, 768), BF),
            shaped((256, 768), F32),
            shaped((2, 64, 768), BF),
            shaped((2, 64, 768), BF),
            shaped((256, 2944), BF),
            shaped((256, 2944), BF),
            shaped((8, 768), F32),
        ],
        scratch_shapes=[
            pltpu.VMEM((2, 768, 768), BF),
            pltpu.VMEM((2, 768, 1408), BF),
            pltpu.SemaphoreType.DMA((2, 32)),
        ],
        compiler_params=pltpu.CompilerParams(vmem_limit_bytes=VMEM_LIMIT),
        cost_estimate=pl.CostEstimate(flops=5 * 10**9, bytes_accessed=12 * 10**6, transcendentals=10**6),
        name="feed_forward",
    )(ids, lives, tokens, cotangent, gain, *att_pieces, *held)


def grads_kernel(
    ids, lives, cot, cot_c, own, came, near, near_c, by_x, by_x_c,
    lead_in, keep_in, lead_rest, keep_rest, g_in, g_rest, sems,
):
    f, chip = ids[0] & 3, ids[0] >> 1
    copies = []

    def store(grads, which, lead, keep, order):
        for slot, group in enumerate(order):
            for kz in range(4):
                at = pl.multiple_of(48 * (chip ^ (kz * 4 + group)), 48)
                target = lead.at[slot * 4 + kz] if slot < 2 else keep.at[slot * 4 + kz - 8]
                copies.append(pltpu.make_async_copy(grads.at[pl.ds(at, 48)], target, sems.at[which, slot * 4 + kz]))
                copies[-1].start()

    def both(first, last):
        return jnp.concatenate([own[:, first:last], came[:, first:last]], axis=0)

    g_in[...] = dot_tn(both(0, 768), both(768, 1920)).astype(BF)
    store(g_in, 0, lead_in, keep_in, (3, 2, 1, 0))
    dym = jnp.concatenate([jnp.where(live_rows(lives[i]), c[...].astype(F32), 0.0) for i, c in enumerate((cot, cot_c))])
    g_rest[:, 384:] = dot_tn(dym.astype(BF), both(1920, 2560)).astype(BF)
    branch = both(2560, 2944)
    mine = (near[0], near_c[1], by_x[192:256, :], by_x_c[256:320, :])
    others = (near[1], near_c[0], by_x[256:320, :], by_x_c[192:256, :])
    for k in range(4):
        rows = pl.ds(pl.multiple_of(192 * (f ^ k), 192), 192)
        heads = jnp.concatenate([unpack_heads(mine[k]), unpack_heads(others[k])], axis=0)
        g_rest[rows, :384] = dot_tn(heads, branch).astype(BF)
    store(g_rest, 1, lead_rest, keep_rest, (3, 1, 2, 0))
    for copy in copies:
        copy.wait()


def feed_gradients(ids, lives, *operands):
    return pl.pallas_call(
        grads_kernel,
        in_specs=[SMEM] * 2 + [VM] * len(operands),
        out_specs=[ANY] * 4,
        out_shape=[shaped((8, 48, width), BF) for width in (1152, 1152, 1024, 1024)],
        scratch_shapes=[
            pltpu.VMEM((768, 1152), BF),
            pltpu.VMEM((768, 1024), BF),
            pltpu.SemaphoreType.DMA((2, 16)),
        ],
        compiler_params=pltpu.CompilerParams(vmem_limit_bytes=VMEM_LIMIT),
        cost_estimate=pl.CostEstimate(flops=3 * 10**9, bytes_accessed=10**7, transcendentals=0),
        name="grads",
    )(ids, lives, *operands)


def backward_kernel(
    ids, q8, key, val, att, prob, d0, d1, d2, d3, gain, ggain, t0_far, t1_far, t2_far, t3_far, cos_far, sin_far, wide_far,
    dn_keep, dn_sent, far, near,
    dqf, dq, dkt, dvt, n16, grads, t0, t1, t2, t3, cos, sin, wide, sems, late_sems,
):
    step = pl.program_id(0)
    late = ((t0_far, t0), (t1_far, t1), (t2_far, t2), (t3_far, t3), (cos_far, cos), (sin_far, sin), (wide_far, wide))
    loads = [pltpu.make_async_copy(a, b, late_sems.at[i]) for i, (a, b) in enumerate(late)]

    @pl.when(step == 0)
    def _():
        for load in loads:
            load.start()
        dkt[...] = jnp.zeros((256, 1024), F32)
        dvt[...] = jnp.zeros((256, 1024), F32)

    rows = pl.ds(pl.multiple_of(step * 256, 256), 256)
    zero = jnp.zeros((), BF)
    keys = key[...]
    values = val[...]
    dattn = unpack_heads(d0[0])
    for i, piece in ((1, d1[1]), (2, d2[0]), (3, d3[1])):
        dattn = jnp.where(step == i, unpack_heads(piece), dattn)
    dattn = jnp.concatenate([dattn, jnp.zeros((256, 64), BF)], axis=1)
    product = dattn[:, :192].astype(F32) * att[...]
    queries_t = q8[rows, :].T
    dattn_t = dattn.T
    total = jnp.zeros((256, 256), F32)
    for h in range(3):
        weights = prob[h]
        dprob = dot_nt(jnp.where(value_lanes(256, h), dattn, zero), values)
        delta = jnp.sum(jnp.where(value_lanes(192, h), product, 0.0), axis=-1, keepdims=True)
        dscores = (weights.astype(F32) * (dprob - delta)).astype(BF)
        total += dot_nn(dscores, jnp.where(head_lanes(256, h), keys, zero))
        q_head = jnp.concatenate([queries_t[32 * h : 32 * h + 32], queries_t[128 + 32 * h : 160 + 32 * h]], axis=0)
        dk_head = dot_nn(q_head, dscores)
        dkt[32 * h : 32 * h + 32, :] += dk_head[:32]
        dkt[128 + 32 * h : 160 + 32 * h, :] += dk_head[32:]
        dvt[64 * h : 64 * h + 64, :] += dot_nn(dattn_t[64 * h : 64 * h + 64], weights)
    dqf[rows, :] = total * 0.125

    @pl.when(step == 3)
    def _():
        for load in loads:
            load.wait()
        dk = dkt[...].T
        c, s = cos[...], sin[...]
        dq[:, :128] = (dqf[:, :128] * c + dqf[:, 128:] * s).astype(BF)
        dq[:, 128:256] = (dqf[:, 128:] * c - dqf[:, :128] * s).astype(BF)
        dq[:, 256:384] = (dk[:, :128] * c + dk[:, 128:] * s).astype(BF)
        dq[:, 384:512] = (dk[:, 128:] * c - dk[:, :128] * s).astype(BF)
        dq[:, 512:768] = dvt[...].T.astype(BF)
        ggain1 = jnp.zeros((1, 768), F32)
        gain_row = gain[0:1, :]
        for i, (piece, out) in enumerate(((t0, dn_keep.at[0]), (t1, dn_sent.at[0]), (t2, dn_keep.at[1]), (t3, dn_sent.at[1]))):
            part = dot_nt(dq[256 * i : 256 * i + 256, :], wide[...])
            x = piece[...].astype(F32)
            center = x - jnp.mean(x, axis=-1, keepdims=True)
            inverse = lax.rsqrt(jnp.mean(center * center, axis=-1, keepdims=True) + NORM_EPS)
            normed = center * inverse
            n16[256 * i : 256 * i + 256, :] = (normed * gain_row).astype(BF)
            ggain1 += jnp.sum(part * normed, axis=0, keepdims=True)
            out[...] = part.astype(BF)
        gains = jnp.concatenate([ggain1, ggain[0:1, :], jnp.zeros((126, 768), F32)], axis=0)
        grads[...] = pack_columns(dot_tn(n16[...], dq[...]), gains.T[:, :64]).astype(BF)
        copies = []
        for ky, target in ((1, far), (0, near)):
            for kz in range(4):
                at = pl.multiple_of(96 * ((ids[0] >> 2) ^ (kz * 2 + ky)), 96)
                copies.append(
                    pltpu.make_async_copy(grads.at[pl.ds(at, 96)], target.at[kz], sems.at[len(copies)])
                )
                copies[-1].start()
        for copy in copies:
            copy.wait()


def backward_attention(ids, token_pieces, cos, sin, q8, key, val, att, prob, d_pieces, gain, wide, ggain):
    return pl.pallas_call(
        backward_kernel,
        grid=(4,),
        in_specs=[SMEM]
        + [full((1024, 256))] * 3
        + [pl.BlockSpec((256, 192), lambda i: (i, 0))]
        + [pl.BlockSpec((3, 256, 1024), lambda i: (0, i, 0))]
        + [full((2, 64, 768))] * 4
        + [full((8, 768))] * 2
        + [ANY] * 7,
        out_specs=[full((2, 256, 768))] * 2 + [ANY, ANY],
        out_shape=[shaped((2, 256, 768), BF)] * 2 + [shaped((4, 96, 640), BF)] * 2,
        scratch_shapes=[
            pltpu.VMEM((1024, 256), F32),
            pltpu.VMEM((1024, 768), BF),
            pltpu.VMEM((256, 1024), F32),
            pltpu.VMEM((256, 1024), F32),
            pltpu.VMEM((1024, 768), BF),
            pltpu.VMEM((768, 640), BF),
        ]
        + [pltpu.VMEM((256, 768), BF)] * 4
        + [pltpu.VMEM((1024, 128), F32)] * 2
        + [pltpu.VMEM((768, 768), BF), pltpu.SemaphoreType.DMA((8,)), pltpu.SemaphoreType.DMA((7,))],
        compiler_params=pltpu.CompilerParams(vmem_limit_bytes=VMEM_LIMIT),
        cost_estimate=pl.CostEstimate(flops=8 * 10**9, bytes_accessed=16 * 10**6, transcendentals=0),
        name="backward_attention",
    )(ids, q8, key, val, att, prob, *d_pieces, gain, ggain, *token_pieces, cos, sin, wide)


def sum_heads_kernel(ids, own, pair, last, near, far):
    f = ids[0] & 3
    total = own[...].astype(F32) + pair[0].astype(F32) + last[...].astype(F32)
    pieces = [total[24 * j : 24 * j + 24, :] for j in range(4)]
    for k, out in enumerate((near.at[0], near.at[1], far.at[0], far.at[1])):
        place = f ^ k
        low = jnp.where(place == 0, pieces[0], pieces[1])
        high = jnp.where(place == 2, pieces[2], pieces[3])
        out[...] = jnp.where(place < 2, low, high).astype(BF)


def sum_heads(ids, *pieces):
    return pl.pallas_call(
        sum_heads_kernel,
        in_specs=[SMEM] + [VM] * 3,
        out_specs=[VM] * 2,
        out_shape=[shaped((2, 24, 640), BF)] * 2,
        compiler_params=pltpu.CompilerParams(vmem_limit_bytes=VMEM_LIMIT),
        cost_estimate=pl.CostEstimate(flops=10**6, bytes_accessed=10**6, transcendentals=0),
        name="sum_heads",
    )(ids, *pieces)


def sum_rows_kernel(ids, a0, a1, a2, b0, b1, b2, mine, other):
    core = ids[0] & 1
    one = a0[...].astype(F32) + a1[0].astype(F32) + a2[...].astype(F32)
    two = b0[...].astype(F32) + b1[0].astype(F32) + b2[...].astype(F32)
    rows = jnp.concatenate([two[:, :384], one, two[:, 384:]], axis=1)
    mine[...] = jnp.where(core == 0, rows[:24], rows[24:]).astype(BF)
    other[...] = jnp.where(core == 0, rows[24:], rows[:24]).astype(BF)


def sum_rows(ids, *pieces):
    return pl.pallas_call(
        sum_rows_kernel,
        in_specs=[SMEM] + [VM] * 6,
        out_specs=[VM] * 2,
        out_shape=[shaped((24, 2176), BF)] * 2,
        compiler_params=pltpu.CompilerParams(vmem_limit_bytes=VMEM_LIMIT),
        cost_estimate=pl.CostEstimate(flops=10**6, bytes_accessed=10**6, transcendentals=0),
        name="sum_rows",
    )(ids, *pieces)


def store_update(gradient, state, outs, rate):
    master, first, second, average = [ref[...] for ref in state]
    for out, value in zip(outs, adam_update(master, first, second, average, gradient, rate)):
        out[...] = value


def update_rows_kernel(ids, mine, came, *refs):
    core = ids[0] & 1
    one, two = mine[...].astype(F32), came[...].astype(F32)
    left, right = jnp.where(core == 0, one, two), jnp.where(core == 0, two, one)
    grads = (
        jnp.concatenate([left[:, 384:1536], right[:, 384:1536]], axis=1),
        jnp.concatenate([left[:, :384], right[:, :384]], axis=1),
        jnp.concatenate([left[:, 1536:2176], right[:, 1536:2048]], axis=1),
    )
    for i, gradient in enumerate(grads):
        store_update(gradient, refs[4 * i : 4 * i + 4], refs[12 + 5 * i : 17 + 5 * i], MATRIX_RATE)


def update_rows(ids, mine, came, states):
    return pl.pallas_call(
        update_rows_kernel,
        in_specs=[SMEM] + [VM] * 14,
        out_specs=[VM] * 15,
        out_shape=[shaped((24, width), dtype) for width in (2304, 768, 1152) for dtype in (F32,) * 4 + (BF,)],
        compiler_params=pltpu.CompilerParams(vmem_limit_bytes=VMEM_LIMIT),
        cost_estimate=pl.CostEstimate(flops=10**7, bytes_accessed=4 * 10**6, transcendentals=10**5),
        name="update_rows",
    )(ids, mine, came, *[array for state in states for array in state])


def update_heads_kernel(ids, c0, c1, c2, c3, *refs):
    f = ids[0] & 3
    pieces = [c[i].astype(F32) for c, i in ((c0, 0), (c1, 1), (c2, 0), (c3, 1))]
    ordered = []
    for place in range(4):
        k = f ^ place
        low = jnp.where(k == 0, pieces[0], pieces[1])
        high = jnp.where(k == 2, pieces[2], pieces[3])
        ordered.append(jnp.where(k < 2, low, high))
    parts = []
    for part in range(2):
        for piece in ordered:
            for h in range(3):
                parts += [piece[:, 192 * part + 96 * half + 32 * h : 192 * part + 96 * half + 32 * h + 32] for half in range(2)]
    gradient = jnp.concatenate(parts + [piece[:, 384:576] for piece in ordered], axis=1)
    store_update(gradient, refs[:4], refs[8:13], MATRIX_RATE)
    columns = sum(piece[:, 512:640] for piece in pieces)
    row = lax.broadcasted_iota(jnp.int32, (24, 24), 0)
    col = lax.broadcasted_iota(jnp.int32, (24, 24), 1)
    lines = [
        jnp.sum(jnp.where(row == col, columns[:, 64 + i : 65 + i], 0.0), axis=0, keepdims=True) for i in range(2)
    ]
    store_update(jnp.concatenate(lines, axis=0), refs[4:8], refs[13:18], GAIN_RATE)


def update_heads(ids, came, state, gain_state):
    return pl.pallas_call(
        update_heads_kernel,
        in_specs=[SMEM] + [VM] * 12,
        out_specs=[VM] * 10,
        out_shape=[shaped((24, 2304), dtype) for dtype in (F32,) * 4 + (BF,)]
        + [shaped((2, 24), dtype) for dtype in (F32,) * 4 + (BF,)],
        compiler_params=pltpu.CompilerParams(vmem_limit_bytes=VMEM_LIMIT),
        cost_estimate=pl.CostEstimate(flops=10**7, bytes_accessed=3 * 10**6, transcendentals=10**5),
        name="update_heads",
    )(ids, *came, *state, *gain_state)


def pack_layout(count_row, length_row, slots, own_place):
    devices_here = count_row.shape[0]
    places = jnp.arange(devices_here * slots, dtype=jnp.int32)
    holder = (places // slots) ^ own_place
    within = places % slots
    before = jnp.cumsum(count_row) - count_row
    choose = (holder[:, None] == jnp.arange(devices_here, dtype=jnp.int32)[None, :]).astype(jnp.int32)
    offset = jnp.sum(choose * before[None, :], axis=1) + within
    limits = jnp.sum(choose * count_row[None, :], axis=1)
    living = within < limits
    doc_ends = jnp.cumsum(length_row)
    passed = offset[:, None] >= doc_ends[None, :]
    document = jnp.sum(passed.astype(jnp.int32), axis=1)
    begins = jnp.max(jnp.where(passed, doc_ends[None, :], 0), axis=1)
    document = jnp.where(living, document, length_row.shape[0])
    position = jnp.where(living, offset - begins, 0)
    return document, position, living


def after(values, *signals):
    held = lax.optimization_barrier((tuple(values), signals))
    return list(held[0])


def fast_body(
    tokens, cotangent, counts, lengths,
    weight_qkv, weight_out, weight_in, weight_down, norm_gains,
    first_qkv, first_out, first_in, first_down, first_gains,
    second_qkv, second_out, second_in, second_down, second_gains,
    average_qkv, average_out, average_in, average_down, average_gains,
):
    slots = tokens.shape[0]
    group_row = lax.axis_index("dp")
    own_place = lax.axis_index("fsdp")
    core, side = own_place & 1, own_place >> 1
    chip = group_row * 2 + side
    count_row = lax.dynamic_index_in_dim(counts, group_row, 0, keepdims=False)
    length_row = lax.dynamic_index_in_dim(lengths, group_row, 0, keepdims=False)
    own_count = lax.dynamic_index_in_dim(count_row, own_place, 0, keepdims=False)
    core_count = lax.dynamic_index_in_dim(count_row, own_place ^ 1, 0, keepdims=False)
    ids = lax.axis_index(AXES).astype(jnp.int32).reshape(1)
    lives = jnp.stack([own_count, core_count])

    def flag(name):
        return FL.get(name, 0)

    def exchange(near, far, direct=False):
        if direct:
            return [near, xperm(near, 1), xperm(far, 2), xperm(far, 3)]
        came = xperm(far, 2)
        return [near, xperm(near, 1), came, xperm(came, 1)]

    def pick(name, values, *signals):
        k = flag(name)
        if k == 0:
            return list(values)
        chosen = signals[k - 1]
        return after(values, *chosen)

    near, far, mine, other = prologue(ids, weight_qkv, weight_out, weight_in, weight_down, norm_gains)
    tok_c, cot_c = xperm(tokens, 1), xperm(cotangent, 1)
    rows_here, own_rows = assemble(ids, *exchange(near, far, flag("QX")), mine, xperm(other, 1))
    rows_z = [xperm(rows_here, 8), xperm(rows_here, 16), xperm(rows_here, 24)]
    rows_y = xperm(rows_here, 4)
    rows_z = jnp.stack(rows_z)
    rows_zy = xperm(rows_z, 4)
    w_pieces = [rows_here, rows_y, rows_z, rows_zy]
    (tokens_later,) = pick("H5", [tokens], (rows_here, tok_c), (rows_z,), (rows_y,))
    tok_x = xperm(tokens_later, 2)
    token_pieces = [tokens, tok_c, tok_x, xperm(tok_x, 1)]

    column0 = own_rows
    rows_unmarked = own_rows
    (own_rows,) = pick("H1", [own_rows], (rows_z, rows_y), (rows_z,), (rows_y,), (rows_zy,))
    column = [own_rows, xperm(own_rows, 8), xperm(own_rows, 16), xperm(own_rows, 24)]
    if flag("EP"):
        (rows_first,) = pick("E1", [rows_unmarked], (rows_y,), (rows_z[:1],), (tok_c,))
        early_x = xperm(rows_first, 2)
        (rows_first,) = pick("E2", [rows_first], (rows_y,), (early_x,), (rows_z[:1],))
        early_y = xperm(rows_first, 4)
        trio = jnp.stack([rows_unmarked, early_x, early_y])
        (trio,) = pick("E3", [trio], (column[3],), (rows_zy,))
        column = column[1:]
    held = jnp.stack(column)

    count_row, length_row = pick("H2", [count_row, length_row], (rows_here,), (rows_z,), (rows_zy,))
    docs, position, _ = pack_layout(count_row, length_row, slots, own_place)
    speeds = ROTARY_BASE ** (-(jnp.arange(HD // 2, dtype=F32) * (2.0 / HD)))
    angles = position.astype(F32)[:, None] * jnp.tile(speeds, 4)[None, :]
    cos, sin = jnp.cos(angles), jnp.sin(angles)

    if flag("FS"):
        held_x, held_y = xperm(held, 2), xperm(held, 4)
        (cos_ready,) = pick("H3", [cos], (held,), (column[-1],))
        q8, key, val, gain, wide = project(ids, token_pieces, cos_ready, sin, w_pieces)
        (q8_ready,) = pick("H8", [q8], (held,), (column[0],), (column[0], column[1]))
        att, near, far, prob = attend(q8_ready, key, val, docs)
    else:
        held_x, held_y = xperm(held, 2), xperm(held, 4)
        (cos_ready,) = pick("H3", [cos], (held,), (column[-1],))
        q8, key, val, att, near, far, prob, gain, wide = forward_attention(
            ids, token_pieces, cos_ready, sin, docs, w_pieces
        )
    ready_x, ready_y = pick("H4", [held_x, held_y], (q8,), (near,))
    if flag("EP"):
        front = [early_y[:, :768], ready_y[:, :, :768].reshape(144, 768)]
        by_x = jnp.concatenate(front + [far.reshape(128, 768)], axis=0)
        (from_x,) = pick("H6", [ready_x], (near,), (by_x,))
        by_y = jnp.concatenate([early_x[None, :, 768:], from_x[:, :, 768:]], axis=0)
        by_x, by_y = xperm(by_x, 2), xperm(by_y, 4)
    else:
        by_x = jnp.concatenate([ready_y[:, :, :768].reshape(192, 768), far.reshape(128, 768)], axis=0)
        (from_x,) = pick("H6", [ready_x], (near,), (by_x,))
        by_x, by_y = xperm(by_x, 2), xperm(from_x[:, :, 768:], 4)
    held = [held, held_x, held_y]
    held = pick("H7", held, (q8,), (near,), (by_x,))
    (near,) = pick("H9", [near], (by_x,), (by_y,))
    if flag("HC") == 1:
        count = held[1].shape[0]
        pair = xperm(jnp.concatenate(held[1:], axis=0), 1)
        held_c = [xperm(held[0], 1), pair[:count], pair[count:]]
    elif flag("HC") == 2:
        count = held[1].shape[0]
        three = xperm(jnp.concatenate(held, axis=0), 1)
        held_c = [three[:count], three[count : 2 * count], three[2 * count :]]
    else:
        held_c = [xperm(piece, 1) for piece in held]
    by_x_c, by_y_c = xperm(by_x, 1), xperm(by_y, 1)
    att_pieces = [near, xperm(near, 1), by_x, by_x_c]
    held = held + [by_x, by_y] + held_c + [by_x_c, by_y_c]
    if flag("EP"):
        held = [trio, xperm(trio, 1)] + held
    block_out, dmiddle, d_near, d_far, own_pack, other_pack, ggain = feed_forward(
        ids, lives, tokens, cotangent, gain, att_pieces, held
    )
    d_pieces = exchange(d_near, d_far, flag("DX"))

    def add(*parts):
        total = parts[0].astype(F32)
        for part in parts[1:]:
            total = total + part.astype(F32)
        return total.astype(BF)

    def reduce_column(name, pieces):
        came = xperm(jnp.stack([pieces[1], pieces[3]]), 8)
        (came,) = pick(name, [came], (then_y,), (then_x,), (far_y,))
        return [pieces[0], came, xperm(add(pieces[2], came[1]), 16)]

    (other_pack,) = pick("C2", [other_pack], (d_pieces[2],), (d_pieces[3],))
    came_pack = xperm(other_pack, 1)
    (pack_later,) = pick("C3", [own_pack], (d_pieces[2],), (d_pieces[3],), (d_pieces[1],))
    lead_in, keep_in, lead_rest, keep_rest = feed_gradients(
        ids, lives, cotangent, cot_c, pack_later, came_pack, *att_pieces
    )
    along_x, along_y = xperm(lead_rest, 2), xperm(lead_in, 4)
    (key_later,) = pick("T3", [key], (lead_in,), (d_pieces[2], d_pieces[3]), (lead_in, d_pieces[2], d_pieces[3]))
    dn_keep, dn_sent, far, near = backward_attention(
        ids, token_pieces, cos, sin, q8, key_later, val, att, prob, d_pieces, gain, wide, ggain
    )
    if flag("T5") in (1, 2):
        along_x, along_y = after([along_x, along_y], *((near,) if flag("T5") == 1 else (near, far)))
    (far,) = pick("T4", [far], (along_x, along_y), (along_x,), (along_y,))
    far_y = xperm(far, 4)
    next_in = add(keep_in[:4], along_y[:4])
    next_rest = add(keep_rest[:4], along_x[:4])
    next_in, next_rest = pick("T8", [next_in, next_rest], (far_y,))
    (next_in,) = pick("T9", [next_in], (far_y,), (dn_sent,), (far,))
    (next_rest,) = pick("TD", [next_rest], (far_y,), (dn_sent,), (far,))
    then_y, then_x = xperm(next_rest, 4), xperm(next_in, 2)
    (far_y,) = pick("TA", [far_y], (then_y, then_x), (then_x,), (then_y,))
    (near,) = pick("T2", [near], (along_x, along_y), (then_x,), (then_y,))
    e = [add(near[kz], far_y[kz]) for kz in range(4)]
    heads = reduce_column("Z0", e)
    (then_x,) = pick("Z1", [then_x], (e[1], e[2], e[3]), (heads[1],), (heads[2],))
    (then_y,) = pick("Z2", [then_y], (e[1], e[2], e[3]), (heads[1],), (heads[2],))
    column_in = reduce_column("Z6", [add(keep_in[4 + kz], along_y[4 + kz], then_x[kz]) for kz in range(4)])
    column_rest = reduce_column("Z7", [add(keep_rest[4 + kz], along_x[4 + kz], then_y[kz]) for kz in range(4)])
    (dn_sent,) = pick("T6", [dn_sent], (far_y,), (then_x, then_y), (along_x, along_y), (e[1],))
    dn_came = xperm(dn_sent, 1)
    x_came = xperm(add(dn_keep[1], dn_came[1]), 2)
    heads = pick("T7", heads, (x_came,))
    column_in = pick("Z3", column_in, (heads[1],), (heads[2],))
    mine, other = sum_rows(ids, *column_in, *column_rest)
    states = [
        (weight_in, first_in, second_in, average_in),
        (weight_out, first_out, second_out, average_out),
        (weight_down, first_down, second_down, average_down),
    ]
    (other,) = pick("Z5", [other], (heads[1],), (heads[2],))
    other_came = xperm(other, 1)
    if flag("TC"):
        heads = pick("TC", heads, (other_came,), (other,))
    head_sums = sum_heads(ids, *heads)
    came = exchange(*head_sums, flag("UX"))
    (mine,) = pick("Z4", [mine], (heads[1],), (heads[2],), (head_sums[0],), (came[2],))
    new_rows = update_rows(ids, mine, other_came, states)
    new_heads = update_heads(
        ids,
        came,
        (weight_qkv, first_qkv, second_qkv, average_qkv),
        (norm_gains, first_gains, second_gains, average_gains),
    )

    dnormed = dn_keep[0].astype(F32) + dn_came[0].astype(F32) + x_came.astype(F32)
    normed, inverse = norm_parts(tokens.astype(F32))
    grad_tokens = dmiddle + norm_back(dnormed * gain[0:1, :], normed, inverse)

    updated = [new_heads[:5], new_rows[5:10], new_rows[:5], new_rows[10:], new_heads[5:]]
    return (block_out, grad_tokens) + tuple(updated[i][j] for j in range(5) for i in range(5))


def solution(mesh):
    sizes = dict(mesh.shape)
    body = fast_body if sizes == {"dp": 8, "fsdp": 4} else general_body
    rows, columns = P(("dp", "fsdp"), None), P(None, ("dp", "fsdp"))
    weights = (rows,) * 4 + (columns,)
    return jax.shard_map(
        body,
        mesh=mesh,
        in_specs=(rows, rows, P(), P()) + weights * 4,
        out_specs=(rows, rows) + weights * 5,
        check_vma=False,
    )
```
